32 devices in a mesh: dp: 4 (over y, core), mp: 8 (over z, x).
Axes of the slice: x: 2, y: 2, z: 4, core: 2. Of those that a mesh axis runs over, the one named last changes fastest.
Arguments:
- tokens: bfloat16 [8192, 1152], P(('dp', 'mp')), may hold values from -6 to 6
- conditioning: bfloat16 [32, 1152], P('dp'), may hold values from -6 to 6, as said below
- lengths: int32 [32], P('dp'), may hold values from 128 to 256, as said below
- w_ada: bfloat16 [1152, 6, 1152], P('dp', None, 'mp'), may hold values from -1 to 1, as said below
- b_ada: bfloat16 [6, 1152], P(None, 'mp'), may hold values from -3 to 3, as said below
- w_qkv: bfloat16 [3, 1152, 1152], P(None, 'dp', 'mp'), may hold values from -1 to 1, as said below
- b_qv: bfloat16 [2, 1152], P(None, 'mp'), may hold values from -3 to 3, as said below
- w_out: bfloat16 [1152, 1152], P('mp', 'dp'), may hold values from -0.75 to 0.75
- b_out: bfloat16 [1152], replicated, may hold values from -3 to 3
- w_up: bfloat16 [1152, 4608], P('dp', 'mp'), may hold values from -0.1875 to 0.1875
- b_up: bfloat16 [4608], P('mp'), may hold values from -3 to 3
- w_down: bfloat16 [4608, 1152], P('mp', 'dp'), may hold values from -0.09375 to 0.09375
- b_down: bfloat16 [1152], replicated, may hold values from -3 to 3
- cotangent: bfloat16 [8192, 1152], P(('dp', 'mp')), may hold values from -6 to 6
Outputs:
- output: bfloat16 [8192, 1152], P(('dp', 'mp'))
- grad_tokens: float32 [8192, 1152], P(('dp', 'mp'))
- grad_w_ada: float32 [1152, 6, 1152], P('dp', None, 'mp')
- grad_b_ada: float32 [6, 1152], P(None, 'mp')
- grad_w_qkv: float32 [3, 1152, 1152], P(None, 'dp', 'mp')
- grad_b_qv: float32 [2, 1152], P(None, 'mp')
- grad_w_out: float32 [1152, 1152], P('mp', 'dp')
- grad_b_out: float32 [1152], replicated
- grad_w_up: float32 [1152, 4608], P('dp', 'mp')
- grad_b_up: float32 [4608], P('mp')
- grad_w_down: float32 [4608, 1152], P('mp', 'dp')
- grad_b_down: float32 [1152], replicated
The draws below stay inside these ranges and needn't reach their ends.
Inputs may be any that keep to these rules, and one draw needn't show every extreme that they name: `lengths`: each entry is 128 or 256; in every draw the images of some group all have 256 kept tokens, so that group's rows are all used; other groups end with unused rows. `conditioning`: independent entries of mean zero. `b_ada`: independent entries of mean zero. `b_qv`: independent entries of mean zero. `w_ada`: independent entries of mean zero, spread as one over the root of 1152. `w_qkv`: independent entries of mean zero, spread as one over the root of 1152.
All inputs are finite; a program needn't handle non-finite values.
Results may differ from the reference program's by a relative error of at most 0.02.
Values may be sent and summed in bfloat16 or wider, within the bound.
No kernel may reach another device: no remote copies, remote signals or barrier semaphores. Data moves between devices by JAX's collectives and lax.ppermute only.
A program may use at most 192 MiB of HBM per device.

```python
from functools import partial
import jax
import jax.numpy as jnp
from jax import lax

D = 1152
HEADS = 16
HD = 72
FF = 4608
PATCHES = 256
BLOCK = 512
KEPT_HALF = 128
GROUP = 2048
IMG_GRP = 8
IMAGES = 32
TOKENS = 8192


def bounded_normal(key, shape, spread, edge):
    values = jax.random.truncated_normal(key, -edge, edge, shape, jnp.float32)
    return (values * spread).astype(jnp.bfloat16)


def draw_lengths(key, part):
    key = jax.random.fold_in(key, 7)
    halves_key, group_key = jax.random.split(key)
    halves = jax.random.randint(halves_key, (IMAGES,), 0, 2)
    chosen = jax.random.randint(group_key, (), 0, IMAGES // IMG_GRP)
    owner_group = jnp.arange(IMAGES) // IMG_GRP
    halves = jnp.where(owner_group == chosen, 1, halves)
    return (KEPT_HALF + halves * KEPT_HALF).astype(jnp.int32)


def draw_conditioning(key, part):
    key = jax.random.fold_in(key, 11)
    return bounded_normal(key, (IMAGES, D), 1.0, 6.0)


def draw_w_ada(key, part):
    key = jax.random.fold_in(key, 13)
    return bounded_normal(key, (D, 6, D), D ** (-0.5), 6.0)


def draw_b_ada(key, part):
    key = jax.random.fold_in(key, 17)
    return bounded_normal(key, (6, D), 0.5, 6.0)


def draw_w_qkv(key, part):
    key = jax.random.fold_in(key, 19)
    return bounded_normal(key, (3, D, D), D ** (-0.5), 6.0)


def draw_b_qv(key, part):
    key = jax.random.fold_in(key, 23)
    return bounded_normal(key, (2, D), 0.5, 6.0)


def block_levels(rng, dims, cuts, low, high):
    loudness, own = 1.0, jax.random.fold_in(rng, 6)
    for position, parts in cuts:
        steps = jnp.exp(jax.random.uniform(jax.random.fold_in(own, position), (parts,), jnp.float32, low / len(cuts), high / len(cuts)))
        loudness = loudness * jnp.repeat(steps, dims[position] // parts).reshape([-1 if axis == position else 1 for axis in range(len(dims))])
    return loudness


def noise(rng, dims, width, most, cuts=(), kind=jnp.bfloat16):
    factor_of = block_levels(rng, dims, cuts, -0.22, 0.18) if cuts else 1.0
    array = jax.random.normal(rng, dims, jnp.float32) * width * factor_of
    return jnp.minimum(jnp.maximum(array, -most), most).astype(kind)


def setup_inputs(seed: int = 0) -> dict:
    key_list = jax.random.split(jax.random.key(seed), 15)
    return {
        "tokens": noise(key_list[0], (TOKENS, D), 1.0, 6.0, ((0, 32),)),
        "conditioning": draw_conditioning(jax.random.fold_in(key_list[14], 71), 0),
        "lengths": draw_lengths(jax.random.fold_in(key_list[14], 71), 0),
        "w_ada": draw_w_ada(jax.random.fold_in(key_list[14], 71), 0),
        "b_ada": draw_b_ada(jax.random.fold_in(key_list[14], 71), 0),
        "w_qkv": draw_w_qkv(jax.random.fold_in(key_list[14], 71), 0),
        "b_qv": draw_b_qv(jax.random.fold_in(key_list[14], 71), 0),
        "w_out": noise(key_list[7], (D, D), (D // 16) ** -0.5, 0.75, ((0, 8), (1, 4))),
        "b_out": noise(key_list[8], (D,), 0.5, 3.0),
        "w_up": noise(key_list[9], (D, FF), D ** -0.5, 0.1875, ((0, 4), (1, 8))),
        "b_up": noise(key_list[10], (FF,), 0.5, 3.0, ((0, 8),)),
        "w_down": noise(key_list[11], (FF, D), FF ** -0.5, 0.09375, ((0, 8), (1, 4))),
        "b_down": noise(key_list[12], (D,), 0.5, 3.0),
        "cotangent": noise(key_list[13], (TOKENS, D), 1.0, 6.0, ((0, 32),)),
    }


highest = lax.Precision.HIGHEST

@jax.custom_vjp
def low(v):
    return lax.optimization_barrier(v.astype(jnp.bfloat16)).astype(jnp.float32)

@jax.custom_vjp
def low_back(v):
    return v

def low_keep(v):
    return (low(v), None)

def low_pass(kept, grad):
    return (grad,)

def back_keep(v):
    return (v, None)

def back_low(kept, grad):
    return (low(grad),)
low.defvjp(low_keep, low_pass)
low_back.defvjp(back_keep, back_low)

def both_ways(values):
    return low_back(low(values))

def layer_norm(values):
    centred = values - lax.optimization_barrier(jnp.mean(values, axis=-1, keepdims=True))
    spread = lax.optimization_barrier(jnp.mean(centred * centred, axis=-1, keepdims=True))
    return centred * lax.rsqrt(spread + 1e-06)

def modulate(values, shift_by, scale_by):
    return layer_norm(values) * (1.0 + scale_by) + shift_by

def member_table(lengths, row_count):
    starts = (jnp.cumsum(lengths) - lengths).astype(jnp.int32)
    ends = (starts + lengths).astype(jnp.int32)
    row_index = jnp.arange(row_count, dtype=jnp.int32)
    inside = (row_index[:, None] >= starts[None, :]) & (row_index[:, None] < ends[None, :])
    number = jnp.arange(lengths.shape[0], dtype=jnp.int32)
    segment = lax.optimization_barrier(jnp.sum(jnp.where(inside, number[None, :], 0), axis=1)).astype(jnp.int32)
    segment = jnp.where(jnp.any(inside, axis=1), segment, lengths.shape[0] + row_index).astype(jnp.int32)
    return (inside.astype(jnp.float32), segment)

def attention(query_rows, key_rows, value_rows, segment):
    total_rows = query_rows.shape[0]
    factor = HD ** (-0.5)
    key_pad = jnp.pad(key_rows, ((PATCHES, PATCHES), (0, 0), (0, 0)))
    value_pad = jnp.pad(value_rows, ((PATCHES, PATCHES), (0, 0), (0, 0)))
    segment_pad = jnp.pad(segment, (PATCHES, PATCHES), constant_values=-1)
    window = BLOCK + 2 * PATCHES

    @jax.checkpoint
    def one_block(first_row):
        queries = lax.dynamic_slice_in_dim(query_rows, first_row, BLOCK, 0)
        query_seg = lax.dynamic_slice_in_dim(segment, first_row, BLOCK, 0)
        keys_blk = lax.dynamic_slice_in_dim(key_pad, first_row, window, 0)
        values_blk = lax.dynamic_slice_in_dim(value_pad, first_row, window, 0)
        key_seg = lax.dynamic_slice_in_dim(segment_pad, first_row, window, 0)
        scores = low_back(jnp.einsum('qhd,khd->hqk', queries, keys_blk, precision=highest) * factor)
        same = (query_seg[:, None] == key_seg[None, :])[None]
        scores = jnp.where(same, scores, -1e+30)
        row_max = lax.optimization_barrier(jnp.max(scores, axis=-1, keepdims=True))
        exp_scores = jnp.exp(scores - row_max)
        prob_rows = exp_scores / lax.optimization_barrier(jnp.sum(exp_scores, axis=-1, keepdims=True))
        return both_ways(jnp.einsum('hqk,khd->qhd', low(prob_rows), values_blk, precision=highest))
    firsts = jnp.arange(total_rows // BLOCK, dtype=jnp.int32) * BLOCK
    return lax.map(one_block, firsts).reshape(total_rows, HEADS * HD)

def one_group(inputs, weights):
    tokens_f, table, segment, modulation = inputs
    w_qkv, b_qv, w_out, b_out, w_up, b_up, w_down, b_down = weights
    row_count = tokens_f.shape[0]
    row_mod = jnp.einsum('gi,ikd->gkd', table, modulation, precision=highest)
    attn_input = low(modulate(tokens_f, row_mod[:, 0], row_mod[:, 1]))
    projected = jnp.einsum('gd,kdc->gkc', attn_input, w_qkv, precision=highest)
    query_rows = both_ways(projected[:, 0] + b_qv[0]).reshape(row_count, HEADS, HD)
    key_rows = both_ways(projected[:, 1]).reshape(row_count, HEADS, HD)
    value_rows = both_ways(projected[:, 2] + b_qv[1]).reshape(row_count, HEADS, HD)
    attended = attention(query_rows, key_rows, value_rows, segment)
    branch = low_back(jnp.dot(attended, w_out, precision=highest) + b_out)
    residual = tokens_f + row_mod[:, 2] * branch
    mlp_input = low(modulate(residual, row_mod[:, 3], row_mod[:, 4]))
    pre_act = low_back(jnp.dot(mlp_input, w_up, precision=highest) + b_up)
    act_rows = low(jax.nn.gelu(pre_act, approximate=True))
    mlp_out = low_back(jnp.dot(act_rows, w_down, precision=highest) + b_down)
    return residual + row_mod[:, 5] * mlp_out

def forward(tokens_f, cond_act, table, segment, w_ada, b_ada, w_qkv, b_qv, w_out, b_out, w_up, b_up, w_down, b_down):
    modulation = low_back(jnp.einsum('id,dkc->ikc', cond_act, w_ada, precision=highest) + b_ada[None])
    group_count = tokens_f.shape[0] // GROUP
    weights = (w_qkv, b_qv, w_out, b_out, w_up, b_up, w_down, b_down)
    grouped = (tokens_f.reshape(group_count, GROUP, D), table, segment, modulation.reshape(group_count, IMG_GRP, 6, D))
    outputs = lax.map(jax.checkpoint(lambda inputs: one_group(inputs, weights)), grouped)
    return outputs.reshape(tokens_f.shape[0], D)

def reference(tokens, conditioning, lengths, w_ada, b_ada, w_qkv, b_qv, w_out, b_out, w_up, b_up, w_down, b_down, cotangent):
    group_count = tokens.shape[0] // GROUP
    table, segment = jax.vmap(partial(member_table, row_count=GROUP))(lengths.reshape(group_count, IMG_GRP))
    cond_act = low(jax.nn.silu(conditioning.astype(jnp.float32)))
    params = [p.astype(jnp.float32) for p in (w_ada, b_ada, w_qkv, b_qv, w_out, b_out, w_up, b_up, w_down, b_down)]

    def wrapped(tokens_f, *weights_all):
        return forward(tokens_f, cond_act, table, segment, *weights_all)
    output, pull_back = jax.vjp(wrapped, tokens.astype(jnp.float32), *params)
    grads = pull_back(cotangent.astype(jnp.float32))
    return (output.astype(jnp.bfloat16), grads[0], grads[1], grads[2], grads[3], grads[4], grads[5], grads[6], grads[7], grads[8], grads[9], grads[10])
```

```python
import jax
import jax.numpy as jnp
from jax import lax
from jax.experimental import pallas as pl
from jax.experimental.pallas import tpu as pltpu
from jax.sharding import PartitionSpec as P

HD = 72
HALF = 128
LANE = 128
EPS = 1e-06
HIDE = -1e30

f32, bf16 = jnp.float32, jnp.bfloat16
highest = lax.Precision.HIGHEST

CORE, Y, X, Z1 = (1, 0), (2, 0), (0, 1), (0, 2)


def swap(values, even, odd=None):
    odd = even if odd is None else odd
    data_ways, model_ways = lax.axis_size("dp"), lax.axis_size("mp")
    pairs = []
    for d in range(data_ways):
        d_bits, m_bits = odd if d % 2 else even
        for m in range(model_ways):
            pairs.append((d * model_ways + m, (d ^ d_bits) * model_ways + (m ^ m_bits)))
    return lax.ppermute(values, ("dp", "mp"), pairs)


def bits_of(count):
    return count.bit_length() - 1


def pick(values, axis, index):
    low, high = (lax.index_in_dim(values, k, axis, keepdims=False) for k in (0, 1))
    return jnp.where(index == 0, low, high)


def nn(a, b):
    return jnp.dot(a, b, preferred_element_type=f32)


def nt(a, b):
    return lax.dot_general(a, b, (((1,), (1,)), ((), ())), preferred_element_type=f32)


def tn(a, b):
    return lax.dot_general(a, b, (((0,), (0,)), ((), ())), preferred_element_type=f32)


def head_windows(width):
    for head in range(width // HD):
        first, last = head * HD, head * HD + HD
        low = first // LANE * LANE
        high = -(-last // LANE) * LANE
        yield first, last, low, high


def lane_mask(first, last, low, high):
    lane = lax.broadcasted_iota(jnp.int32, (HALF, high - low), 1) + low
    return (lane >= first) & (lane < last)


def same_segment(paired, seated):
    row = lax.broadcasted_iota(jnp.int32, (HALF, 2 * HALF), 0)
    col = lax.broadcasted_iota(jnp.int32, (HALF, 2 * HALF), 1)
    own = (col < HALF) & ((row == col) | (seated > 0))
    return own | ((col >= HALF) & (paired > 0))


def attend_forward(facts, q_ref, k_ref, v_ref, o_ref, kk, vv):
    factor = HD ** (-0.5)
    for half in range(2):
        rows = pl.ds(half * HALF, HALF)
        own = pl.ds((half + 1) * HALF, HALF)
        other = pl.ds(pl.multiple_of(facts[3 * half] * HALF, HALF), HALF)
        kk[0:HALF], kk[HALF:] = k_ref[own], k_ref[other]
        vv[0:HALF], vv[HALF:] = v_ref[own], v_ref[other]
        same = same_segment(facts[3 * half + 1], facts[3 * half + 2])
        for first, last, low, high in head_windows(q_ref.shape[1]):
            window = slice(low, high)
            mask = lane_mask(first, last, low, high)
            query = jnp.where(mask, q_ref[rows, window], 0)
            scores = jnp.where(same, nt(query, kk[:, window]) * factor, HIDE)
            exp_scores = jnp.exp(scores - jnp.max(scores, axis=1, keepdims=True))
            prob = exp_scores / jnp.sum(exp_scores, axis=1, keepdims=True)
            mixed = nn(prob.astype(bf16), vv[:, window]).astype(bf16)
            o_ref[rows, window] = jnp.where(mask, mixed, o_ref[rows, window]) if first > low else mixed


def attend_backward(facts, q_ref, k_ref, v_ref, g_ref, dq_ref, dk_ref, dv_ref, kk, vv, dkk, dvv):
    factor = HD ** (-0.5)
    dk_ref[...] = jnp.zeros(dk_ref.shape, f32)
    dv_ref[...] = jnp.zeros(dv_ref.shape, f32)
    for half in range(2):
        rows = pl.ds(half * HALF, HALF)
        own = pl.ds((half + 1) * HALF, HALF)
        other = pl.ds(pl.multiple_of(facts[3 * half] * HALF, HALF), HALF)
        kk[0:HALF], kk[HALF:] = k_ref[own], k_ref[other]
        vv[0:HALF], vv[HALF:] = v_ref[own], v_ref[other]
        dkk[...] = jnp.zeros(dkk.shape, f32)
        dvv[...] = jnp.zeros(dvv.shape, f32)
        same = same_segment(facts[3 * half + 1], facts[3 * half + 2])
        for first, last, low, high in head_windows(q_ref.shape[1]):
            window = slice(low, high)
            mask = lane_mask(first, last, low, high)
            query = jnp.where(mask, q_ref[rows, window], 0)
            grad = jnp.where(mask, g_ref[rows, window], 0)
            scores = jnp.where(same, nt(query, kk[:, window]) * factor, HIDE)
            exp_scores = jnp.exp(scores - jnp.max(scores, axis=1, keepdims=True))
            prob = exp_scores / jnp.sum(exp_scores, axis=1, keepdims=True)
            grad_prob = nt(grad, vv[:, window])
            inner = jnp.sum(grad_prob * prob, axis=1, keepdims=True)
            grad_scores = (prob * (grad_prob - inner)).astype(bf16)
            dq = (nn(grad_scores, kk[:, window]) * factor).astype(bf16)
            dq_ref[rows, window] = jnp.where(mask, dq, dq_ref[rows, window]) if first > low else dq
            dkk[:, window] += tn(grad_scores, query) * factor
            dvv[:, window] += tn(prob.astype(bf16), grad)
        dk_ref[own] += dkk[0:HALF]
        dv_ref[own] += dvv[0:HALF]
        dk_ref[other] += dkk[HALF:]
        dv_ref[other] += dvv[HALF:]


VMEM = pl.BlockSpec(memory_space=pltpu.VMEM)
SMEM = pl.BlockSpec(memory_space=pltpu.SMEM)


def attention(facts, query, key, value):
    width = query.shape[1]
    return pl.pallas_call(
        attend_forward,
        out_shape=jax.ShapeDtypeStruct(query.shape, bf16),
        in_specs=[SMEM, VMEM, VMEM, VMEM],
        out_specs=VMEM,
        scratch_shapes=[pltpu.VMEM((2 * HALF, width), bf16)] * 2,
        compiler_params=pltpu.CompilerParams(vmem_limit_bytes=32 * 2**20),
        name="attention_forward",
    )(facts, query, key, value)


def attention_back(facts, query, key, value, grad):
    width = query.shape[1]
    return pl.pallas_call(
        attend_backward,
        out_shape=(
            jax.ShapeDtypeStruct(query.shape, bf16),
            jax.ShapeDtypeStruct(key.shape, f32),
            jax.ShapeDtypeStruct(key.shape, f32),
        ),
        in_specs=[SMEM, VMEM, VMEM, VMEM, VMEM],
        out_specs=(VMEM, VMEM, VMEM),
        scratch_shapes=[pltpu.VMEM((2 * HALF, width), bf16)] * 2
        + [pltpu.VMEM((2 * HALF, width), f32)] * 2,
        compiler_params=pltpu.CompilerParams(vmem_limit_bytes=32 * 2**20),
        name="attention_backward",
    )(facts, query, key, value, grad)


def normalize(values):
    centred = values - jnp.mean(values, axis=-1, keepdims=True)
    spread = jnp.mean(centred * centred, axis=-1, keepdims=True)
    root = lax.rsqrt(spread + EPS)
    return centred * root, root


def normalize_back(norm, root, upstream):
    return (
        upstream
        - jnp.mean(upstream, axis=-1, keepdims=True)
        - norm * jnp.mean(upstream * norm, axis=-1, keepdims=True)
    ) * root


def by_half(vectors):
    halves, width = vectors.shape
    return jnp.broadcast_to(vectors[:, None, :], (halves, HALF, width)).reshape(halves * HALF, width)


def half_sums(rows):
    return jnp.sum(rows.reshape(-1, HALF, rows.shape[1]), axis=1)


def rows_send(parts, level, data_index):
    bit = (data_index >> level) & 1
    axis = parts.ndim - 3
    return pick(parts, axis, bit), swap(pick(parts, axis, 1 - bit), (1 << level, 0))


def rows_join(keep, back, level, data_index):
    bit = (data_index >> level) & 1
    return jnp.where(bit == 0, jnp.concatenate([keep, back], -1), jnp.concatenate([back, keep], -1))


def lanes_send(block, level, data_index):
    bit = (data_index >> level) & 1
    width = block.shape[-1] // 2
    low, high = block[..., :width], block[..., width:]
    return jnp.where(bit == 0, low, high), swap(jnp.where(bit == 0, high, low), (1 << level, 0))


def lanes_join(keep, back, level, data_index, lead):
    bit = (data_index >> level) & 1
    return jnp.where(bit == 0, jnp.stack([keep, back], lead), jnp.stack([back, keep], lead))


def halves(buf, axis):
    size = buf.shape[axis] // 2
    return (lax.slice_in_dim(buf, k * size, (k + 1) * size, axis=axis) for k in (0, 1))


def added(keep, back):
    return (keep.astype(f32) + back.astype(f32)).astype(bf16)


def tie(*values):
    return lax.optimization_barrier(values) if len(values) > 1 else lax.optimization_barrier(values[0])


FEED = (((X, Y), (Y, Z1), (Z1, X)), ((Z1, Z1), (X, X), (Y, Y)))
THIRDS = ((Z1, Y, X), (X, Z1, Y), (Y, X, Z1))


def early_bits(data_bits, model_bits):
    return [(0, 1 << k) for k in range(2, model_bits)] + [(1 << k, 0) for k in range(2, data_bits)]


def feed_split(buf):
    count, rows, width = buf.shape
    cut = rows * 2 // 3
    return tuple(part.reshape(1, 1, 1, count, part.shape[1], width) for part in (buf[:, :cut], buf[:, cut:]))


def feed_swap(parts, stage):
    return tuple(swap(part, *table[stage]) for part, table in zip(parts, FEED))


def feed_grow(parts, backs, stage):
    return tuple(jnp.concatenate(pair, 2 - stage) for pair in zip(parts, backs))


def feed_whole(parts, twins):
    width = parts[0].shape[-1]
    return jnp.concatenate([side.reshape(-1, width) for pair in zip(parts, twins) for side in pair], 0)


def feed_sizes(rows, devices):
    cut = rows * 2 // 3
    return devices // 2 * cut, devices // 2 * (rows - cut)


def feed_twins(left, right, sizes):
    wide, narrow = sizes
    pieces = left[:, wide : 2 * wide], left[:, 2 * wide + narrow :]
    return tuple(tn(piece, right).astype(bf16) for piece in pieces)


def feed_mine(left, right, sizes, backs, count):
    wide, narrow = sizes
    pieces = left[:, :wide], left[:, 2 * wide : 2 * wide + narrow]
    sums = (
        (tn(piece, right) + back.astype(f32)).astype(bf16) for piece, back in zip(pieces, backs)
    )
    return tuple(part.reshape(2, 2, 2, count, -1, right.shape[1]) for part in sums)


def feed_halve(parts, stage):
    keeps, sends = zip(*(halves(part, 2 - stage) for part in parts))
    return keeps, feed_swap(sends, stage)


def add_all(keeps, backs):
    return tuple(added(*pair) for pair in zip(keeps, backs))


def feed_merge(parts):
    return jnp.concatenate([part.reshape(part.shape[-3:]) for part in parts], 1)


def early_halve(buf, bits, axis):
    keep, send = halves(buf, axis)
    return keep, swap(send, bits)


def mixed_axes(data_bits, model_bits):
    axes = {Y: 0}
    for k in reversed(range(model_bits)):
        axes[(0, 1 << k)] = len(axes)
    for k in reversed(range(2, data_bits)):
        axes[(1 << k, 0)] = len(axes)
    return axes


def mixed_split(buf):
    third = buf.shape[-1] // 3
    return tuple(buf[..., k * third : (k + 1) * third] for k in range(3))


def mixed_swap(parts, stage):
    return tuple(swap(part, order[stage]) for part, order in zip(parts, THIRDS))


def mixed_grow(parts, backs, stage, axes):
    return tuple(
        jnp.concatenate(pair, axes[order[stage]]) for pair, order in zip(zip(parts, backs), THIRDS)
    )


def mixed_whole(parts, twins, data_index):
    core, why = data_index & 1, (data_index >> 1) & 1
    whole = [[[], []], [[], []]]
    for part, twin in zip(parts, twins):
        for type_core in range(2):
            side = jnp.where(core == type_core, part, twin)
            for type_y in range(2):
                chosen = jnp.where(why == type_y, side[0], side[1])
                whole[type_y][type_core].append(chosen.reshape(-1, chosen.shape[-1]))
    return [[jnp.concatenate(whole[y][c], 1) for c in range(2)] for y in range(2)]


def relative(pairs, data_index):
    core, why = data_index & 1, (data_index >> 1) & 1
    by_core = [[jnp.where(core == 0, pairs[y][k], pairs[y][1 - k]) for k in range(2)] for y in range(2)]
    return [[jnp.where(why == 0, by_core[k][c], by_core[1 - k][c]) for c in range(2)] for k in range(2)]


def mixed_products(lefts, rights, side):
    third = rights[0][0].shape[1] // 3
    return tuple(
        jnp.concatenate(
            [tn(lefts[y][side], rights[y][side][:, k * third : (k + 1) * third]) for y in range(2)], 0
        )
        for k in range(3)
    )


def mixed_halve(parts, stage, axes):
    keeps, sends = zip(*(halves(part, axes[order[stage]]) for part, order in zip(parts, THIRDS)))
    return keeps, mixed_swap(sends, stage)


def reorder(here, there, width, block):
    source = lax.broadcasted_iota(jnp.int32, (width, width), 0)
    target = lax.broadcasted_iota(jnp.int32, (width, width), 1)
    wanted = ((target // block) ^ here ^ there) * block + target % block
    return (source == wanted).astype(bf16)


def on_device(
    tokens,
    conditioning,
    lengths,
    w_ada,
    b_ada,
    w_qkv,
    b_qv,
    w_out,
    b_out,
    w_up,
    b_up,
    w_down,
    b_down,
    cotangent,
):
    data_ways, model_ways = lax.axis_size("dp"), lax.axis_size("mp")
    data_index, model_index = lax.axis_index("dp"), lax.axis_index("mp")
    data_bits, model_bits = bits_of(data_ways), bits_of(model_ways)
    devices = data_ways * model_ways
    early = early_bits(data_bits, model_bits)
    early_count = 1 << len(early)
    axes = mixed_axes(data_bits, model_bits)
    local_rows, width = tokens.shape
    lanes = width // data_ways
    head_cols = w_qkv.shape[2]
    hidden = w_up.shape[1]
    subs = data_ways // 4
    images = lengths.shape[0]
    binary = (2,) * data_bits
    feed_count = hidden // data_ways
    sizes = feed_sizes(feed_count, devices)

    starts = jnp.cumsum(lengths) - lengths
    half_rows = (model_index * 2 + jnp.arange(-1, 3, dtype=jnp.int32)) * HALF
    inside = (half_rows[:, None] >= starts[None]) & (half_rows[:, None] < (starts + lengths)[None])
    seated = jnp.any(inside, axis=1)
    is_first = jnp.any(inside & (half_rows[:, None] == starts[None]), axis=1)
    paired = jnp.any(inside & (lengths[None] == 2 * HALF), axis=1)
    own_index = jnp.arange(4, dtype=jnp.int32)
    partner = jnp.where(is_first, own_index + 1, own_index - 1)
    facts = jnp.stack([partner, paired.astype(jnp.int32), seated.astype(jnp.int32)], 1)[1:3]
    facts = facts.reshape(6).astype(jnp.int32)
    table = inside.astype(f32)

    kinds = jnp.concatenate([jnp.swapaxes(w_qkv, 1, 2), w_out[None]], 0)
    kinds = kinds.reshape(4, subs, head_cols // subs, lanes)
    kinds = jnp.swapaxes(kinds, 0, 1).reshape(binary + (head_cols // subs, lanes))
    feed = jnp.stack([jnp.swapaxes(w_up, 0, 1), w_down], 0).reshape(2, data_ways, feed_count, lanes)
    feed = jnp.moveaxis(feed, 0, 1).reshape(binary + (2 * feed_count, lanes))
    cond = conditioning[None]
    for level in range(data_bits):
        keep, back = rows_send(kinds, level, data_index)
        feed_keep, feed_back = rows_send(feed, level, data_index)
        cond_back = swap(cond, (1 << level, 0))
        back, feed_back, cond_back = tie(back, feed_back, cond_back)
        kinds = rows_join(keep, back, level, data_index)
        feed = rows_join(feed_keep, feed_back, level, data_index)
        cond = jnp.concatenate([cond, cond_back], 0)

    def modulate():
        part = lax.dynamic_slice_in_dim(cond, data_index * lanes, lanes, 2).astype(f32)
        cond_act = jax.nn.silu(part).astype(bf16)
        mod = nn(cond_act.reshape(data_ways * images, lanes), w_ada.reshape(lanes, 6 * head_cols))
        mod = mod.reshape(binary + (images, 6 * head_cols))
        for level in reversed(range(data_bits)):
            back = swap(mod[1], (1 << level, 0))
            back = yield back
            mod = mod[0] + back
        mod = mod + b_ada.astype(f32).reshape(1, 6 * head_cols)
        biases = jnp.concatenate([b_qv.reshape(-1), b_up], 0).astype(f32)
        buf = jnp.concatenate([mod, biases[None]], 0)[None]
        for level in range(model_bits):
            back = swap(buf, (0, 1 << level))
            back = yield back
            buf = jnp.concatenate([buf, back], 0)
        yield (cond_act, buf)

    chain = modulate()
    small = next(chain)
    steps = data_bits + model_bits
    forth = [(k, k + 1) for k in range(model_ways - 1)]
    back_to = [(k + 1, k) for k in range(model_ways - 1)]

    mixed = kinds.reshape((1,) * len(axes) + kinds.shape)
    for bits in early:
        back, small = tie(swap(mixed, bits), small)
        small = chain.send(small)
        steps -= 1
        mixed = jnp.concatenate([mixed, back], axes[bits])
    mixed = mixed_split(mixed)
    up, down = feed[None, :feed_count], feed[None, feed_count:]
    before, after = lax.ppermute(tokens[HALF:], "mp", forth), lax.ppermute(tokens[:HALF], "mp", back_to)
    for bits in early[:-1]:
        up = jnp.concatenate([up, swap(up, bits)], 0)
        down = jnp.concatenate([down, swap(down, bits)], 0)
    up_back = swap(up, early[-1])
    for stage in range(2):
        backs, small = tie(mixed_swap(mixed, stage), small)
        small = chain.send(small)
        steps -= 1
        mixed = mixed_grow(mixed, backs, stage, axes)
    backs = mixed_swap(mixed, 2)
    down_back = swap(down, early[-1])
    for _ in range(steps):
        small = chain.send(small)
    cond_act, buf = small

    shifts = jnp.arange(model_ways, dtype=jnp.int32)
    flip = ((shifts[:, None] ^ model_index) == shifts[None]).astype(f32)
    whole = jnp.einsum("mr,rf->mf", flip, buf[:, :images].reshape(model_ways, -1), precision=highest)
    whole = whole.reshape(model_ways, images, 6, head_cols)
    half_mod = jnp.einsum("hi,mikc->khmc", table, whole, precision=highest).reshape(6, 4, width)
    shift1, scale1 = half_mod[0], 1.0 + half_mod[1]
    gate1, shift2, scale2, gate2 = (by_half(half_mod[k, 1:3]) for k in range(2, 6))
    scale2 = 1.0 + scale2
    bias_rel = buf[:, images]
    bias_q, bias_v = bias_rel[:, :head_cols].reshape(-1), bias_rel[:, head_cols : 2 * head_cols].reshape(-1)

    def feed_places(table_of):
        place = jnp.arange(devices, dtype=jnp.int32)
        top = bits_of(devices) - 1
        side = (place >> top) & 1
        order = (data_index & 1) ^ side
        rel_d, rel_m = side, jnp.zeros_like(place)
        for stage in range(3):
            bit = (place >> (top - 3 + stage)) & 1
            (even_d, even_m), (odd_d, odd_m) = table_of[stage]
            rel_d = rel_d ^ (bit * jnp.where(order == 0, even_d, odd_d))
            rel_m = rel_m ^ (bit * jnp.where(order == 0, even_m, odd_m))
        for level, (d_bits, m_bits) in enumerate(early):
            bit = (place >> level) & 1
            rel_d, rel_m = rel_d ^ (bit * d_bits), rel_m ^ (bit * m_bits)
        return rel_m, rel_d ^ data_index

    places = [feed_places(table_of) for table_of in FEED]
    cut = feed_count * 2 // 3
    cuts = (slice(0, cut), slice(cut, feed_count))
    targets = jnp.arange(devices, dtype=jnp.int32)
    blocks = bias_rel[:, 2 * head_cols :].reshape(devices, feed_count)
    bias_up = jnp.concatenate(
        [
            jnp.dot(((m * data_ways + d)[:, None] == targets[None]).astype(f32), blocks[:, rows], precision=highest).reshape(-1)
            for (m, d), rows in zip(places, cuts)
        ],
        0,
    )

    span = jnp.concatenate([before, tokens, after], 0).astype(f32)
    span_norm, span_root = normalize(span)
    span_input = (span_norm * by_half(scale1) + by_half(shift1)).astype(bf16)
    own = slice(HALF, HALF + local_rows)

    backs, up_back, span_input = tie(backs, up_back, span_input)
    mixed = mixed_grow(mixed, backs, 2, axes)
    twins = tuple(swap(part, CORE) for part in mixed)
    up = feed_split(jnp.concatenate([up, up_back], 0))
    up_backs = feed_swap(up, 0)
    twins, up_backs = tie(twins, up_backs)
    up = feed_grow(up, up_backs, 0)
    up_backs = feed_swap(up, 1)
    (wq, wk), (wv, wo) = mixed_whole(mixed, twins, data_index)
    attn_input, norm1, root1, tokens_f = span_input[own], span_norm[own], span_root[own], span[own]
    query = (nt(attn_input, wq) + bias_q).astype(bf16)
    key = nt(span_input, wk).astype(bf16)
    value = (nt(span_input, wv) + bias_v).astype(bf16)
    up_backs, query, key, value = tie(up_backs, query, key, value)
    up = feed_grow(up, up_backs, 1)
    up_backs = feed_swap(up, 2)
    attended = attention(facts, query, key, value)
    branch = nn(attended, wo) + b_out.astype(f32)
    residual = tokens_f + gate1 * branch
    norm2, root2 = normalize(residual)
    mlp_input = (norm2 * scale2 + shift2).astype(bf16)

    up_backs, down_back, mlp_input = tie(up_backs, down_back, mlp_input)
    up = feed_grow(up, up_backs, 2)
    up_twins = tuple(swap(part, CORE) for part in up)
    down = feed_split(jnp.concatenate([down, down_back], 0))
    down_backs = feed_swap(down, 0)
    up_twins, down_backs = tie(up_twins, down_backs)
    down = feed_grow(down, down_backs, 0)
    down_backs = feed_swap(down, 1)
    up = feed_whole(up, up_twins)
    down_backs, up = tie(down_backs, up)
    down = feed_grow(down, down_backs, 1)
    down_backs = feed_swap(down, 2)
    pre_act = nt(mlp_input, up) + bias_up
    inner = jnp.tanh(0.7978845608028654 * (pre_act + 0.044715 * pre_act * pre_act * pre_act))
    act = (0.5 * pre_act * (1.0 + inner)).astype(bf16)
    slope = 0.5 * (1.0 + inner) + 0.5 * pre_act * (1.0 - inner * inner) * (
        0.7978845608028654 * (1.0 + 3 * 0.044715 * pre_act * pre_act)
    )
    grad_output = cotangent.astype(f32)
    grad_mlp = (gate2 * grad_output).astype(bf16)
    sum_down = tuple(swap(part, CORE) for part in feed_twins(act, grad_mlp, sizes))
    down_backs, sum_down = tie(down_backs, sum_down)
    down = feed_grow(down, down_backs, 2)
    down_twins = tuple(swap(part, CORE) for part in down)
    sum_down = feed_mine(act, grad_mlp, sizes, sum_down, early_count)
    down_twins, sum_down = tie(down_twins, sum_down)
    keeps, backs = feed_halve(sum_down, 2)
    down = feed_whole(down, down_twins)
    mlp_out = nn(act, down) + b_down.astype(f32)
    output = (residual + gate2 * mlp_out).astype(bf16)
    grad_gate2 = grad_output * mlp_out
    grad_pre = (nt(grad_mlp, down) * slope).astype(bf16)
    sum_up = tuple(swap(part, CORE) for part in feed_twins(grad_pre, mlp_input, sizes))
    backs, sum_up, output = tie(backs, sum_up, output)
    sum_down = add_all(keeps, backs)
    keeps, backs = feed_halve(sum_down, 1)
    sum_up = feed_mine(grad_pre, mlp_input, sizes, sum_up, early_count)
    backs, sum_up = tie(backs, sum_up)
    sum_down = add_all(keeps, backs)
    keeps, backs = feed_halve(sum_down, 0)
    up_keeps, up_backs = feed_halve(sum_up, 2)
    grad_mlp_input = nn(grad_pre, up)
    grad_residual = grad_output + normalize_back(norm2, root2, grad_mlp_input * scale2)
    grad_gate1 = grad_residual * branch
    grad_branch = (gate1 * grad_residual).astype(bf16)
    grad_attended = nt(grad_branch, wo).astype(bf16)
    backs, up_backs, grad_attended = tie(backs, up_backs, grad_attended)
    sum_up = add_all(up_keeps, up_backs)
    up_keeps, up_backs = feed_halve(sum_up, 1)
    down_done = feed_merge(add_all(keeps, backs))
    for bits in reversed(early[1:]):
        down_done = added(*early_halve(down_done, bits, 0))
    down_keep, down_back = early_halve(down_done, early[0], 0)

    grad_query, grad_key, grad_value = attention_back(facts, query, key, value, grad_attended)
    up_backs, down_back, grad_query = tie(up_backs, down_back, grad_query)
    sum_up = add_all(up_keeps, up_backs)
    up_keeps, up_backs = feed_halve(sum_up, 0)
    down_done = added(down_keep, down_back)
    grad_kv = jnp.stack([grad_key, grad_value], 0)
    low_kv = grad_kv.astype(bf16)
    from_after = lax.ppermute(low_kv[:, :HALF], "mp", back_to)
    from_before = lax.ppermute(low_kv[:, HALF + local_rows :], "mp", forth)
    from_before = nn(from_before.reshape(2 * HALF, width), reorder(model_index, model_index - 1, width, head_cols))
    from_after = nn(from_after.reshape(2 * HALF, width), reorder(model_index, model_index + 1, width, head_cols))
    grad_kv = grad_kv[:, own] + jnp.concatenate(
        [part.reshape(2, HALF, width) for part in (from_before, from_after)], 1
    )
    grad_kv = grad_kv.astype(bf16)
    grad_key, grad_value = grad_kv[0], grad_kv[1]
    lefts = relative([[grad_query, grad_key], [grad_value, attended]], data_index)
    rights = relative([[attn_input, attn_input], [attn_input, grad_branch]], data_index)
    twins = tuple(swap(part.astype(bf16), CORE) for part in mixed_products(lefts, rights, 1))
    twins, up_backs = tie(twins, up_backs)
    mine = mixed_products(lefts, rights, 0)
    shape = (2,) * len(axes) + (head_cols // subs, width // 3)
    mine = tuple((a + b.astype(f32)).astype(bf16).reshape(shape) for a, b in zip(mine, twins))
    mine = tie(mine)
    up_done = feed_merge(add_all(up_keeps, up_backs))
    for bits in reversed(early[1:]):
        up_done = added(*early_halve(up_done, bits, 0))
    mixed_keeps, mixed_backs = mixed_halve(mine, 2, axes)
    up_keep, up_back = early_halve(up_done, early[0], 0)
    grad_attn_input = nn(grad_query, wq) + nn(grad_key, wk) + nn(grad_value, wv)
    own_scale1 = by_half(scale1[1:3])
    grad_tokens = grad_residual + normalize_back(norm1, root1, grad_attn_input * own_scale1)

    sums = jnp.stack(
        [
            half_sums(part)
            for part in (
                grad_attn_input,
                grad_attn_input * norm1,
                grad_gate1,
                grad_mlp_input,
                grad_mlp_input * norm2,
                grad_gate2,
            )
        ],
        1,
    )
    image_sums = jnp.einsum("hi,hkd->ikd", table[1:3], sums, precision=highest)
    image_sums = image_sums.reshape(images * 6, model_ways, head_cols)
    image_sums = jnp.einsum("rm,kmc->rkc", flip, image_sums, precision=highest)

    flat_up = jnp.sum(grad_pre, axis=0, dtype=f32)
    first = 0
    parts = []
    for (m, d), size, rows in zip(places, sizes, (cut, feed_count - cut)):
        part = flat_up[first : first + 2 * size].reshape(devices, rows)
        first += 2 * size
        hot = ((m * data_ways + d)[None] == targets[:, None]).astype(f32)
        parts.append(jnp.dot(hot, part, precision=highest))
    flat_up = jnp.concatenate(parts, 1).reshape(model_ways, hidden)
    flat_qv = [jnp.sum(part, axis=0, dtype=f32).reshape(model_ways, head_cols) for part in (grad_query, grad_value)]
    packed = jnp.concatenate([image_sums.reshape(model_ways, -1), *flat_qv, flat_up], 1)
    plain = jnp.stack([jnp.sum(grad_branch, axis=0, dtype=f32), jnp.sum(grad_mlp, axis=0, dtype=f32)], 0)

    def gather_sums():
        buf, rest = packed.reshape(model_ways, images + 1, 6 * head_cols), plain
        for level in reversed(range(model_bits)):
            keep, send = halves(buf, 0)
            backs = yield swap(send, (0, 1 << level)), swap(rest, (0, 1 << level))
            buf, rest = keep + backs[0], rest + backs[1]
        mods, bias = buf[0, :images].astype(bf16)[None], buf[0, images:]
        rest = jnp.concatenate([rest.reshape(-1), bias.reshape(-1)], 0)
        for level in range(data_bits):
            backs = yield swap(mods, (1 << level, 0)), swap(rest, (1 << level, 0))
            mods, rest = jnp.concatenate([mods, backs[0]], 0), rest + backs[1]
        yield mods, rest

    chain = gather_sums()
    steps = model_bits + data_bits
    small = next(chain)

    mixed_backs, up_back, small = tie(mixed_backs, up_back, small)
    small = chain.send(small)
    steps -= 1
    up_done = added(up_keep, up_back)
    mine = add_all(mixed_keeps, mixed_backs)
    mixed_keeps, mixed_backs = mixed_halve(mine, 1, axes)
    feed_back = jnp.concatenate([up_done[0], down_done[0]], 0)
    level = data_bits - 1
    feed_keep, feed_back = lanes_send(feed_back, level, data_index)
    mixed_backs, feed_back, small = tie(mixed_backs, feed_back, small)
    small = chain.send(small)
    steps -= 1
    feed_done = lanes_join(feed_keep, feed_back, level, data_index, 0)
    mine = add_all(mixed_keeps, mixed_backs)
    mixed_keeps, mixed_backs = mixed_halve(mine, 0, axes)
    for level in reversed(range(data_bits - 1)):
        feed_keep, feed_back = lanes_send(feed_done, level, data_index)
        if level == 0:
            mixed_backs, feed_back, small = tie(mixed_backs, feed_back, small)
        feed_done = lanes_join(feed_keep, feed_back, level, data_index, data_bits - 1 - level)
    small = chain.send(small)
    steps -= 1
    mine = add_all(mixed_keeps, mixed_backs)
    mine = jnp.concatenate(mine, -1)
    for bits in reversed(early):
        keep, back = early_halve(mine, bits, axes[bits])
        mine = added(keep, back)
    for _ in range(steps):
        small = chain.send(small)
    grad_modulation, rest = small
    grad_w_ada = tn(
        cond_act.reshape(data_ways * images, lanes),
        grad_modulation.reshape(data_ways * images, 6 * head_cols),
    )
    grad_w_ada = grad_w_ada.reshape(lanes, 6, head_cols)
    grad_b_ada = jnp.sum(grad_modulation, axis=(0, 1), dtype=f32).reshape(6, head_cols)
    grad_b_out, grad_b_down = rest[:width], rest[width : 2 * width]
    rest = rest[2 * width :]
    grad_b_qv, grad_b_up = rest[: 2 * head_cols].reshape(2, head_cols), rest[2 * head_cols :]

    feed_done = feed_done.reshape(data_ways, 2, feed_count, lanes).astype(f32)
    grad_w_up = jnp.swapaxes(feed_done[:, 0].reshape(hidden, lanes), 0, 1)
    grad_w_down = feed_done[:, 1].reshape(hidden, lanes)
    kinds = mine.reshape(head_cols // subs, width)
    for lead, level in enumerate(reversed(range(data_bits))):
        keep, back = lanes_send(kinds, level, data_index)
        kinds = lanes_join(keep, back, level, data_index, lead)
    kinds = kinds.reshape(subs, 4, head_cols // subs, lanes).astype(f32)
    kinds = jnp.swapaxes(kinds, 0, 1).reshape(4, head_cols, lanes)
    grad_w_qkv, grad_w_out = jnp.swapaxes(kinds[:3], 1, 2), kinds[3]
    return (
        output,
        grad_tokens,
        grad_w_ada,
        grad_b_ada,
        grad_w_qkv,
        grad_b_qv,
        grad_w_out,
        grad_b_out,
        grad_w_up,
        grad_b_up,
        grad_w_down,
        grad_b_down,
    )


def solution(mesh):
    in_specs = (
        P(("dp", "mp"), None),
        P("dp", None),
        P("dp"),
        P("dp", None, "mp"),
        P(None, "mp"),
        P(None, "dp", "mp"),
        P(None, "mp"),
        P("mp", "dp"),
        P(),
        P("dp", "mp"),
        P("mp"),
        P("mp", "dp"),
        P(),
        P(("dp", "mp"), None),
    )
    out_specs = (
        P(("dp", "mp"), None),
        P(("dp", "mp"), None),
        P("dp", None, "mp"),
        P(None, "mp"),
        P(None, "dp", "mp"),
        P(None, "mp"),
        P("mp", "dp"),
        P(),
        P("dp", "mp"),
        P("mp"),
        P("mp", "dp"),
        P(),
    )
    return jax.shard_map(
        on_device, mesh=mesh, in_specs=in_specs, out_specs=out_specs, check_vma=False
    )
```

```python
import itertools
import math

import jax
import jax.numpy as jnp
import numpy as np
from jax import lax
from jax.experimental import pallas as pl
from jax.experimental.pallas import tpu as pltpu
from jax.sharding import PartitionSpec as P

HD = 72
HALF = 128
LANE = 128
EPS = 1e-06
HIDE = -1e30

f32, bf16 = jnp.float32, jnp.bfloat16
highest = lax.Precision.HIGHEST

CORE, Y, X, Z1 = (1, 0), (2, 0), (0, 1), (0, 2)


def swap(values, even, odd=None):
    odd = even if odd is None else odd
    data_ways, model_ways = lax.axis_size("dp"), lax.axis_size("mp")
    pairs = []
    for d in range(data_ways):
        d_bits, m_bits = odd if d % 2 else even
        for m in range(model_ways):
            pairs.append((d * model_ways + m, (d ^ d_bits) * model_ways + (m ^ m_bits)))
    return lax.ppermute(values, ("dp", "mp"), pairs)


def bits_of(count):
    return count.bit_length() - 1


def pick(values, axis, index):
    low, high = (lax.index_in_dim(values, k, axis, keepdims=False) for k in (0, 1))
    return jnp.where(index == 0, low, high)


def nn(a, b):
    return jnp.dot(a, b, preferred_element_type=f32)


def nt(a, b):
    return lax.dot_general(a, b, (((1,), (1,)), ((), ())), preferred_element_type=f32)


def tn(a, b):
    return lax.dot_general(a, b, (((0,), (0,)), ((), ())), preferred_element_type=f32)


def head_windows(width):
    for head in range(width // HD):
        first, last = head * HD, head * HD + HD
        low = first // LANE * LANE
        high = -(-last // LANE) * LANE
        yield first, last, low, high


def lane_mask(first, last, low, high):
    lane = lax.broadcasted_iota(jnp.int32, (HALF, high - low), 1) + low
    return (lane >= first) & (lane < last)


def same_segment(paired, seated):
    row = lax.broadcasted_iota(jnp.int32, (HALF, 2 * HALF), 0)
    col = lax.broadcasted_iota(jnp.int32, (HALF, 2 * HALF), 1)
    own = (col < HALF) & ((row == col) | (seated > 0))
    return own | ((col >= HALF) & (paired > 0))


def same_segment_keys(paired, seated):
    key = lax.broadcasted_iota(jnp.int32, (2 * HALF, HALF), 0)
    col = lax.broadcasted_iota(jnp.int32, (2 * HALF, HALF), 1)
    own = (key < HALF) & ((key == col) | (seated > 0))
    return own | ((key >= HALF) & (paired > 0))


def split_rows(rows):
    return pl.ds(rows * HALF, HALF)


def row(vectors, kind, half):
    return vectors[4 * kind + half : 4 * kind + half + 1]


def normalize(values):
    centred = values - jnp.mean(values, axis=-1, keepdims=True)
    spread = jnp.mean(centred * centred, axis=-1, keepdims=True)
    root = lax.rsqrt(spread + EPS)
    return centred * root, root


def normalize_back(norm, root, upstream):
    return (
        upstream
        - jnp.mean(upstream, axis=-1, keepdims=True)
        - norm * jnp.mean(upstream * norm, axis=-1, keepdims=True)
    ) * root


def column_sum(values):
    return jnp.sum(values, axis=0, keepdims=True)


def span_kernel(before, tokens, after, vectors, out):
    for half in range(4):
        source = (before, tokens, tokens, after)[half]
        norm, _ = normalize(source[split_rows(half == 2)].astype(f32))
        out[split_rows(half)] = (norm * (1.0 + row(vectors, 1, half)) + row(vectors, 0, half)).astype(bf16)


def qkv_kernel(span, wq, wk, wv, bias_q, bias_v, query, key, value):
    query[...] = (nt(span[...], wq[...]) + bias_q[...]).astype(bf16)
    key[...] = nt(span[...], wk[...]).astype(bf16)
    value[...] = (nt(span[...], wv[...]) + bias_v[...]).astype(bf16)


def attend_forward(
    facts, q_ref, k_ref, v_ref, wo, b_out, tokens, vectors, o_ref, branch_ref, residual_ref, input_ref, kk, vv
):
    factor = HD ** (-0.5)
    for half in range(2):
        rows = split_rows(half)
        own = split_rows(half + 1)
        other = pl.ds(pl.multiple_of(facts[3 * half] * HALF, HALF), HALF)
        kk[0:HALF], kk[HALF:] = k_ref[own], k_ref[other]
        vv[0:HALF], vv[HALF:] = v_ref[own], v_ref[other]
        same = same_segment(facts[3 * half + 1], facts[3 * half + 2])
        for first, last, low, high in head_windows(q_ref.shape[1]):
            window = slice(low, high)
            mask = lane_mask(first, last, low, high)
            query = jnp.where(mask, q_ref[own, window], 0)
            scores = jnp.where(same, nt(query, kk[:, window]) * factor, HIDE)
            exp_scores = jnp.exp(scores - jnp.max(scores, axis=1, keepdims=True))
            prob = exp_scores / jnp.sum(exp_scores, axis=1, keepdims=True)
            mixed = nn(prob.astype(bf16), vv[:, window]).astype(bf16)
            o_ref[rows, window] = jnp.where(mask, mixed, o_ref[rows, window]) if first > low else mixed
    for half in range(2):
        rows = split_rows(half)
        branch = nn(o_ref[rows], wo[...]) + b_out[...]
        branch_ref[rows] = branch
        residual = tokens[rows].astype(f32) + row(vectors, 2, half + 1) * branch
        residual_ref[rows] = residual
        norm, _ = normalize(residual)
        input_ref[rows] = (norm * (1.0 + row(vectors, 4, half + 1)) + row(vectors, 3, half + 1)).astype(bf16)


def score_gradients(query, grad, keys, values, same):
    scores = nt(keys, query) * HD ** (-0.5)
    if same is not None:
        scores = jnp.where(same, scores, HIDE)
    exp_scores = jnp.exp(scores - jnp.max(scores, axis=0, keepdims=True))
    prob = exp_scores / jnp.sum(exp_scores, axis=0, keepdims=True)
    grad_prob = nt(values, grad)
    inner = jnp.sum(grad_prob * prob, axis=0, keepdims=True)
    return prob.astype(bf16), (prob * (grad_prob - inner)).astype(bf16)


def attend_backward(half, facts, q_ref, k_ref, v_ref, g_ref, *refs):
    earlier, refs = (refs[:3], refs[3:]) if half else (None, refs)
    dq_ref, own_k, own_v, kk, vv, dkk, dvv = refs
    factor = HD ** (-0.5)
    rows = split_rows(half)
    own = split_rows(half + 1)
    other = pl.ds(pl.multiple_of(facts[3 * half] * HALF, HALF), HALF)
    kk[0:HALF], kk[HALF:] = k_ref[own], k_ref[other]
    vv[0:HALF], vv[HALF:] = v_ref[own], v_ref[other]
    dkk[...] = jnp.zeros(dkk.shape, f32)
    dvv[...] = jnp.zeros(dvv.shape, f32)
    if half:
        dq_ref[0:HALF] = earlier[0][0:HALF]
    same = same_segment_keys(facts[3 * half + 1], facts[3 * half + 2])
    for first, last, low, high in head_windows(q_ref.shape[1]):
        window = slice(low, high)
        mask = lane_mask(first, last, low, high)
        query = jnp.where(mask, q_ref[own, window], 0)
        grad = jnp.where(mask, g_ref[rows, window], 0)
        prob, grad_scores = score_gradients(query, grad, kk[:, window], vv[:, window], same)
        dq = (tn(grad_scores, kk[:, window]) * factor).astype(bf16)
        dq_ref[rows, window] = jnp.where(mask, dq, dq_ref[rows, window]) if first > low else dq
        dkk[:, window] += nn(grad_scores, query) * factor
        dvv[:, window] += nn(prob, grad)
    inside = jnp.where(facts[3 * half] == 2 - half, 1.0, 0.0)
    for place, (total, mine) in enumerate(((dkk, own_k), (dvv, own_v))):
        mine_own, mine_other = total[0:HALF], total[HALF:] * inside
        if half:
            mine_own = mine_own + earlier[1 + place][split_rows(half)]
            mine_other = mine_other + earlier[1 + place][split_rows(1 - half)]
        mine[split_rows(half)], mine[split_rows(1 - half)] = mine_own, mine_other


def attend_outside(
    facts, q_ref, k_ref, v_ref, before, after, wo, own_k, own_v, key_ref, value_ref, kk, vv, grads, dk, dv
):
    factor = HD ** (-0.5)
    dk[...], dv[...] = own_k[...], own_v[...]
    for half, (outside, branch) in enumerate(((0, before), (3, after))):

        @pl.when((facts[3 * half] == outside) & (facts[3 * half + 1] > 0))
        def _():
            mine, theirs = split_rows(half), split_rows(outside)
            kk[0:HALF], kk[HALF:] = k_ref[theirs], k_ref[split_rows(half + 1)]
            vv[0:HALF], vv[HALF:] = v_ref[theirs], v_ref[split_rows(half + 1)]
            grads[...] = nt(branch[...], wo[...]).astype(bf16)
            for first, last, low, high in head_windows(q_ref.shape[1]):
                window = slice(low, high)
                mask = lane_mask(first, last, low, high)
                query = jnp.where(mask, q_ref[theirs, window], 0)
                grad = jnp.where(mask, grads[:, window], 0)
                prob, grad_scores = score_gradients(query, grad, kk[:, window], vv[:, window], None)
                dk[mine, window] += nn(grad_scores[HALF:], query) * factor
                dv[mine, window] += nn(prob[HALF:], grad)

    key_ref[...], value_ref[...] = dk[...].astype(bf16), dv[...].astype(bf16)


def middle_kernel(
    grad_input, residual, branch, cotangent, vectors, wo, grad_residual, grad_branch, grad_attended, sums
):
    sums[...] = jnp.zeros(sums.shape, f32)
    for half in range(2):
        rows = split_rows(half)
        norm, root = normalize(residual[rows])
        grad = grad_input[rows]
        total = cotangent[rows].astype(f32) + normalize_back(norm, root, grad * (1.0 + row(vectors, 4, half + 1)))
        grad_residual[rows] = total
        low = (row(vectors, 2, half + 1) * total).astype(bf16)
        grad_branch[rows] = low
        grad_attended[rows] = nt(low, wo[...]).astype(bf16)
        sums[half : half + 1] = column_sum(total * branch[rows])
        sums[2 + half : 3 + half] = column_sum(grad)
        sums[4 + half : 5 + half] = column_sum(grad * norm)
        sums[6:7] += column_sum(low.astype(f32))


def last_kernel(
    grad_query, grad_key, grad_value, wq, wk, wv, tokens, vectors, grad_residual, grad_tokens, sums
):
    sums[...] = jnp.zeros(sums.shape, f32)
    for half in range(2):
        rows = split_rows(half)
        norm, root = normalize(tokens[rows].astype(f32))
        grad = nn(grad_query[rows], wq[...]) + nn(grad_key[rows], wk[...]) + nn(grad_value[rows], wv[...])
        back = normalize_back(norm, root, grad * (1.0 + row(vectors, 1, half + 1)))
        grad_tokens[rows] = grad_residual[rows] + back
        sums[half : half + 1] = column_sum(grad)
        sums[2 + half : 3 + half] = column_sum(grad * norm)
        sums[4:5] += column_sum(grad_query[rows].astype(f32))
        sums[5:6] += column_sum(grad_value[rows].astype(f32))


VMEM = pl.BlockSpec(memory_space=pltpu.VMEM)
SMEM = pl.BlockSpec(memory_space=pltpu.SMEM)


CHUNK = 96
HINT = pl.CostEstimate(flops=1, bytes_accessed=1, transcendentals=0)


def call(kernel, outs, operands, name, scratch=(), smem=0):
    room = sum(math.prod(v.shape) * v.dtype.itemsize for v in (*scratch, *outs) if hasattr(v, "shape")) + 4 * 2**20
    return pl.pallas_call(
        kernel,
        out_shape=tuple(outs),
        in_specs=[SMEM] * smem + [VMEM] * (len(operands) - smem),
        out_specs=tuple(VMEM for _ in outs),
        scratch_shapes=list(scratch),
        compiler_params=pltpu.CompilerParams(vmem_limit_bytes=room),
        cost_estimate=HINT,
        name=name,
    )(*operands)


def like(rows, width, dtype=bf16):
    return jax.ShapeDtypeStruct((rows, width), dtype)


def grow_kernel(refs, axis=None):
    count = (len(refs) - (axis is not None)) // 3
    both, place = refs[-1], 0
    for own, back, out in zip(refs[:count], refs[count : 2 * count], refs[2 * count : 3 * count]):
        rows, lanes = own.shape
        out[:rows], out[rows:] = own[...], back[...]
        if axis == 0:
            both[place : place + rows], both[place + rows : place + 2 * rows] = own[...], back[...]
            place += 2 * rows
        if axis == 1:
            both[:rows, place : place + lanes], both[rows:, place : place + lanes] = own[...], back[...]
            place += lanes


def grow(parts, backs):
    outs = [like(2 * part.shape[0], part.shape[1]) for part in parts]
    return call(lambda *refs: grow_kernel(refs), outs, (*parts, *backs), "grow")


def grow_both(parts, backs, axis):
    outs = [like(2 * part.shape[0], part.shape[1]) for part in parts]
    if axis == 0:
        both = like(sum(out.shape[0] for out in outs), outs[0].shape[1])
    else:
        both = like(outs[0].shape[0], sum(out.shape[1] for out in outs))
    outs = call(lambda *refs: grow_kernel(refs, axis), [*outs, both], (*parts, *backs), "grow_both")
    return outs[:-1], outs[-1]


def row_sum(keep, back, first, last):
    return (keep[first:last].astype(f32) + back[first:last].astype(f32)).astype(bf16)


def halve_kernel(groups, *refs):
    count = len(refs) // 4
    for k in range(count):
        keep, back, low, high = refs[k], refs[count + k], refs[2 * count + 2 * k], refs[2 * count + 2 * k + 1]
        rows = keep.shape[0] // (2 * groups)
        for group in range(groups):
            for out, base in ((low, 2 * group * rows), (high, (2 * group + 1) * rows)):
                for first in range(0, rows, CHUNK):
                    last = min(first + CHUNK, rows)
                    out[group * rows + first : group * rows + last] = row_sum(keep, back, base + first, base + last)


def halve(keeps, backs, groups=1):
    outs = [like(keep.shape[0] // 2, keep.shape[1]) for keep in keeps for _ in range(2)]
    outs = call(lambda *refs: halve_kernel(groups, *refs), outs, (*keeps, *backs), "halve")
    return outs[0::2], outs[1::2]


def halve_join_kernel(*refs):
    count = len(refs) // 6
    keeps, backs, outs = refs[: 2 * count], refs[2 * count : 4 * count], refs[4 * count :]
    for k in range(count):
        for which in range(2):
            keep, back = keeps[which * count + k], backs[which * count + k]
            rows = keep.shape[0] // 2
            for out, base in ((outs[2 * k], 0), (outs[2 * k + 1], rows)):
                for first in range(0, rows, CHUNK):
                    last = min(first + CHUNK, rows)
                    out[which * rows + first : which * rows + last] = row_sum(keep, back, base + first, base + last)


def halve_join(keeps, backs):
    outs = [like(keep.shape[0], keep.shape[1]) for keep in keeps[: len(keeps) // 2] for _ in range(2)]
    outs = call(halve_join_kernel, outs, (*keeps, *backs), "halve_join")
    return outs[0::2], outs[1::2]


def merge_rows_kernel(*refs):
    count = (len(refs) - 2) // 2
    low, high = refs[2 * count :]
    rows, width = low.shape[0], low.shape[1] // 2
    for which in range(2):
        lanes = slice(which * width, (which + 1) * width)
        place = 0
        for keep, back in zip(refs[:count], refs[count : 2 * count]):
            first, end = which * keep.shape[0] // 2, (which + 1) * keep.shape[0] // 2
            while first < end:
                out, base = (low, 0) if place < rows else (high, rows)
                step = min(end - first, base + rows - place)
                out[place - base : place - base + step, lanes] = row_sum(keep, back, first, first + step)
                first, place = first + step, place + step


def merge_lanes_kernel(*refs):
    count = (len(refs) - 2) // 2
    low, high = refs[2 * count :]
    rows, lane = low.shape[0], 0
    for keep, back in zip(refs[:count], refs[count : 2 * count]):
        lanes = slice(lane, lane + keep.shape[1])
        lane += keep.shape[1]
        low[:, lanes], high[:, lanes] = row_sum(keep, back, 0, rows), row_sum(keep, back, rows, 2 * rows)


def merge(kernel, keeps, backs, rows, width):
    return call(kernel, [like(rows, width)] * 2, (*keeps, *backs), "merge")


def row_steps(weights):
    unit = 0
    for weight in weights:
        rows = weight.shape[0]
        step = 256 if rows % 256 == 0 else 384
        for first in range(0, rows, step):
            yield weight, first, first + step, unit + first
        unit += rows


def up_kernel(x_ref, bias_ref, *refs):
    weights, (act_ref, slope_ref) = refs[:-2], refs[-2:]
    for weight, first, last, unit in row_steps(weights):
        units = slice(unit, unit + last - first)
        pre = nt(x_ref[...], weight[first:last]) + bias_ref[:, units]
        square = pre * pre
        inner = jnp.tanh(0.7978845608028654 * pre * (1.0 + 0.044715 * square))
        outer = 0.5 * (1.0 + inner)
        act_ref[:, units] = (pre * outer).astype(bf16)
        rise = (0.5 * 0.7978845608028654) * pre * (1.0 + (3 * 0.044715) * square)
        slope_ref[:, units] = (outer + rise * (1.0 - inner * inner)).astype(bf16)


def pre_kernel(grad_ref, slope_ref, *refs):
    weights, (pre_ref, sum_ref) = refs[:-2], refs[-2:]
    for weight, first, last, unit in row_steps(weights):
        units = slice(unit, unit + last - first)
        pre = (nt(grad_ref[...], weight[first:last]) * slope_ref[:, units].astype(f32)).astype(bf16)
        pre_ref[:, units] = pre
        sum_ref[:, units] = jnp.sum(pre.astype(f32), axis=0, keepdims=True)


def back_kernel(left_ref, *refs):
    weights, out_ref = refs[:-1], refs[-1]
    unit = 0
    for weight in weights:
        rows = weight.shape[0]
        part = nn(left_ref[:, unit : unit + rows], weight[...])
        out_ref[...] = part if unit == 0 else out_ref[...] + part
        unit += rows


def output_kernel(act, residual, cotangent, vectors, b_down, grad_mlp, *refs):
    weights, (out, sums, total) = refs[:-3], refs[-3:]
    back_kernel(act, *weights, total)
    sums[...] = jnp.zeros(sums.shape, f32)
    for half in range(2):
        rows = split_rows(half)
        mlp = total[rows] + b_down[...]
        out[rows] = (residual[rows] + row(vectors, 5, half + 1) * mlp).astype(bf16)
        sums[half : half + 1] = column_sum(cotangent[rows].astype(f32) * mlp)
        sums[2:3] += column_sum(grad_mlp[rows].astype(f32))


def join_kernel(own, back, wide, narrow):
    rows = own.shape[0]
    more = wide.shape[0] - rows
    wide[:rows], wide[rows:] = own[...], back[:more]
    narrow[...] = back[more:]


def place_feed_kernel(done, grad_up, grad_down):
    ways, _, rows, lanes = done.shape
    for way in range(ways):
        grad_down[way * rows : (way + 1) * rows] = done[way, 1].astype(f32)
    whole = jnp.concatenate([done[way, 0] for way in range(ways)], 0).astype(f32)
    grad_up[...] = whole.T


def place_mixed_kernel(done, grad_qkv, grad_out):
    for kind in range(3):
        grad_qkv[kind] = done[kind].astype(f32).T
    grad_out[...] = done[3].astype(f32)


def gate_kernel(cotangent, vectors, out):
    for half in range(2):
        rows = split_rows(half)
        out[rows] = (row(vectors, 5, half + 1) * cotangent[rows].astype(f32)).astype(bf16)


def product_kernel(start, left_ref, right_ref, *refs):
    back, outs = (refs[0], refs[1:]) if len(refs) > 1 and refs[0].shape != refs[-1].shape else (None, refs)
    base = 0
    for out in outs:
        size = out.shape[0]
        step = 256 if size % 256 == 0 else 384
        for first in range(0, size, step):
            column = start + base + first
            part = tn(left_ref[:, column : column + step], right_ref[...])
            if back is not None:
                part = part + back[base + first : base + first + step].astype(f32)
            out[first : first + step] = part.astype(bf16)
        base += size


def products(left, right, start, counts, backs=()):
    outs = [like(size, right.shape[1]) for size in counts]
    return call(lambda *refs: product_kernel(start, *refs), outs, (left, right, *backs), "products")


def unit_of(third, y, z, x):
    return ((x, 2 * y + z), (y, 2 * z + x), (z, 2 * x + y))[third]


def assemble_kernel(spot, *refs):
    sides, outs = (refs[:4], refs[4:8]), refs[8:]
    unit = outs[0].shape[0] // 4
    width = outs[0].shape[1] // 3

    def place(core, why):
        for kind, out in enumerate(outs):
            side, y = (kind & 1) ^ core, (kind >> 1) ^ why
            for third in range(3):
                lanes = slice(third * width, (third + 1) * width)
                for z in range(2):
                    for x in range(2):
                        array, index = unit_of(third, y, z, x)
                        rows = slice(index * unit, (index + 1) * unit)
                        source = sides[side][1 + third][rows] if array else sides[side][0][rows, lanes]
                        out[(2 * z + x) * unit : (2 * z + x + 1) * unit, lanes] = source

    for core in range(2):
        for why in range(2):
            pl.when((spot[0] == core) & (spot[1] == why))(lambda core=core, why=why: place(core, why))


def assemble(spot, arrays, width):
    return call(assemble_kernel, [like(width, width)] * 4, (spot, *arrays), "assemble", smem=1)


def kinds_kernel(side, spot, *refs):
    lefts, rights, refs, left, right = refs[:4], refs[4:6], refs[6:-2], refs[-2], refs[-1]
    back, outs = (None, refs) if side else (refs[0], refs[1:])
    width = left.shape[1]
    unit, third_width = width // 4, width // 3
    for y in range(2):
        kind = (spot[1] ^ y) * 2 + (spot[0] ^ side)
        for k in range(4):

            @pl.when(kind == k)
            def _():
                left[...] = lefts[k][...]
                right[...] = rights[k == 3][...]

        for third in range(3):
            lanes = slice(third * third_width, (third + 1) * third_width)
            part = tn(left[...], right[:, lanes])
            for z in range(2):
                for x in range(2):
                    array, index = unit_of(third, y, z, x)
                    rows = slice(index * unit, (index + 1) * unit)
                    both_rows = slice(array * width + index * unit, array * width + (index + 1) * unit)
                    piece = part[(2 * z + x) * unit : (2 * z + x + 1) * unit]
                    if side:
                        outs[0][both_rows, lanes] = piece.astype(bf16)
                    else:
                        piece = piece + back[both_rows, lanes].astype(f32)
                        outs[2 * third + array][rows] = piece.astype(bf16)


def kind_products(side, spot, lefts, rights, backs=()):
    rows, width = lefts[0].shape
    return call(
        lambda *refs: kinds_kernel(side, *refs),
        [like(2 * width, width)] if side else [like(width, width // 3)] * 6,
        (spot, *lefts, *rights, *backs),
        "kind_products",
        scratch=[pltpu.VMEM((rows, width), bf16)] * 2,
        smem=1,
    )


def rows_send(parts, axis, level, data_index):
    bit = (data_index >> level) & 1
    return pick(parts, axis, bit), swap(pick(parts, axis, 1 - bit), (1 << level, 0))


def lanes_join(keep, back, level, data_index):
    bit = (data_index >> level) & 1
    return jnp.where(bit == 0, jnp.concatenate([keep, back], -1), jnp.concatenate([back, keep], -1))


def lanes_split(block, level, data_index):
    bit = (data_index >> level) & 1
    width = block.shape[-1] // 2
    low, high = block[..., :width], block[..., width:]
    return jnp.where(bit == 0, low, high), jnp.where(bit == 0, high, low)


def lanes_send(block, level, data_index):
    keep, send = lanes_split(block, level, data_index)
    return keep, swap(send, (1 << level, 0))


def lanes_sum(block, level, data_index):
    keep, send = lanes_split(block, level, data_index)
    return added(keep, swap(send, (1 << level, 0)))


def rows_join(keep, back, level, data_index, lead):
    bit = (data_index >> level) & 1
    return jnp.where(bit == 0, jnp.stack([keep, back], lead), jnp.stack([back, keep], lead))


def halves(buf):
    size = buf.shape[0] // 2
    return buf[:size], buf[size:]


def added(keep, back):
    return (keep.astype(f32) + back.astype(f32)).astype(bf16)


def tie(*values):
    return lax.optimization_barrier(values) if len(values) > 1 else lax.optimization_barrier(values[0])


FEED = (((X, Y), (Y, Z1), (Z1, X)), ((Z1, Z1), (X, X), (Y, Y)))
THIRDS = tuple(tuple((bits, bits) for bits in order) for order in ((Z1, Y, X), (X, Z1, Y), (Y, X, Z1)))


def early_bits(model_bits):
    return [(0, 1 << k) for k in range(2, model_bits)]


def stage_swap(parts, plan, stage):
    return tuple(swap(part, *table[stage]) for part, table in zip(parts, plan))


def core_swap(parts):
    return tuple(swap(part, CORE) for part in parts)


def early_join(buf, bits):
    return jnp.concatenate([buf, swap(buf, bits)], 0)


def join_order(model_bits):
    return [*range(2, model_bits), 0, 1]


def join_masks(model_bits):
    joins = join_order(model_bits)
    return [sum(((place >> k) & 1) << bit for k, bit in enumerate(joins)) for place in range(1 << model_bits)]


def feed_places(rows, model_bits):
    early = early_bits(model_bits)
    unit_rows = rows << len(early)
    cut = unit_rows * 2 // 3
    step = math.gcd(rows, cut)
    tables = []
    for core in range(2):
        places = []
        spans = range(0, cut, step), range(cut, unit_rows, step)
        for side, last, (table, span), *bits in itertools.product(
            range(2), range(2), list(zip(FEED, spans)), range(2), range(2)
        ):
            d, m = side, 0
            for bit, stage in zip((last, *bits), reversed(table)):
                d, m = d ^ bit * stage[core ^ side][0], m ^ bit * stage[core ^ side][1]
            for row in span:
                block, m_row = row // rows, m
                for level, (_, m_bits) in enumerate(early):
                    m_row = m_row ^ ((block >> level) & 1) * m_bits
                places.append((join_masks(model_bits).index(m_row), d, row % rows // step))
        tables.append(np.array(places, np.int32))
    return step, tables


def one_hot_rows(index, count):
    return (index[:, None] == jnp.arange(count, dtype=jnp.int32)[None]).astype(f32)


def on_device(
    tokens,
    conditioning,
    lengths,
    w_ada,
    b_ada,
    w_qkv,
    b_qv,
    w_out,
    b_out,
    w_up,
    b_up,
    w_down,
    b_down,
    cotangent,
):
    data_ways, model_ways = lax.axis_size("dp"), lax.axis_size("mp")
    data_index, model_index = lax.axis_index("dp"), lax.axis_index("mp")
    data_bits, model_bits = bits_of(data_ways), bits_of(model_ways)
    early = early_bits(model_bits)
    local_rows, width = tokens.shape
    lanes = width // data_ways
    head_cols = w_qkv.shape[2]
    hidden = w_up.shape[1]
    images = lengths.shape[0]
    binary = (2,) * data_bits
    feed_count = hidden // 4
    all_hidden = hidden * model_ways
    spot = jnp.stack([data_index & 1, (data_index >> 1) & 1]).astype(jnp.int32)
    forth = [(k, k + 1) for k in range(model_ways - 1)]
    back_to = [(k + 1, k) for k in range(model_ways - 1)]

    mixed = jnp.concatenate([jnp.swapaxes(w_qkv, 1, 2), w_out[None]], 0).reshape(2, 2, 1, head_cols, lanes)
    keep, back = rows_send(mixed, 1, 0, data_index)
    feed = jnp.stack([jnp.swapaxes(w_up, 0, 1), w_down], 0).reshape(2, 2, 2, feed_count, lanes)
    feed_keep, feed_back = rows_send(feed, 2, 0, data_index)
    others = [swap(conditioning, (d, 0)) for d in range(1, data_ways)]
    back, feed_back, others = tie(back, feed_back, others)
    cond = jnp.stack([conditioning, *others], 0)
    mixed = lanes_join(keep, back, 0, data_index)
    joins = join_order(model_bits)

    def modulate(cond):
        part = lax.dynamic_slice_in_dim(cond, data_index * lanes, lanes, 2).astype(f32)
        cond_act = jax.nn.silu(part).astype(bf16)
        mod = nn(cond_act.reshape(data_ways * images, lanes), w_ada.reshape(lanes, 6 * head_cols))
        mod = mod.reshape(data_ways, images, 6 * head_cols)
        backs = yield [swap(mod[d], (d, 0)) for d in range(1, data_ways)]
        mod = sum(backs, mod[0]) + b_ada.astype(f32).reshape(1, 6 * head_cols)
        biases = jnp.concatenate([b_qv.reshape(-1), b_up], 0).astype(f32)
        buf = jnp.concatenate([mod, biases[None]], 0)[None]
        for bit in joins:
            back = yield swap(buf, (0, 1 << bit))
            buf = jnp.concatenate([buf, back], 0)
        yield (cond_act, buf)

    steps = 1 + model_bits

    for k, bits in enumerate(early):
        back = swap(mixed, bits)
        if k == 0:
            feed = lanes_join(feed_keep, feed_back, 0, data_index)
            feed_keep, feed_back = rows_send(feed, 1, 1, data_index)
            chain = modulate(cond)
            small = next(chain)
            back, feed_back, small = tie(back, feed_back, small)
            small = chain.send(small)
            steps -= 1
        mixed = jnp.concatenate([mixed, back], 1)
    keep, back = rows_send(mixed, 0, 1, data_index)
    before, after = lax.ppermute(tokens[HALF:], "mp", forth), lax.ppermute(tokens[:HALF], "mp", back_to)
    back, small, lengths, before, after = tie(back, small, lengths, before, after)
    small = chain.send(small)
    steps -= 1
    mixed = lanes_join(keep, back, 1, data_index)
    for level in range(2, data_bits):
        mixed = lanes_join(mixed, swap(mixed, (1 << level, 0)), level, data_index)
    mixed = mixed.reshape(-1, width)
    third = width // 3
    mixed = tuple(mixed[:, k * third : (k + 1) * third] for k in range(3))
    feed = lanes_join(feed_keep, feed_back, 1, data_index)
    for level in range(2, data_bits):
        feed = lanes_join(feed, swap(feed, (1 << level, 0)), level, data_index)
    backs, small, feed = tie(stage_swap(mixed, THIRDS, 0), small, feed)
    for _ in range(steps - 1):
        small = chain.send(small)
    mixed = grow(mixed, backs)
    up, down = feed[0], feed[1]
    for bits in early[:-1]:
        up, down = early_join(up, bits), early_join(down, bits)

    starts = jnp.cumsum(lengths) - lengths
    half_rows = (model_index * 2 + jnp.arange(-1, 3, dtype=jnp.int32)) * HALF
    inside = (half_rows[:, None] >= starts[None]) & (half_rows[:, None] < (starts + lengths)[None])
    seated = jnp.any(inside, axis=1)
    is_first = jnp.any(inside & (half_rows[:, None] == starts[None]), axis=1)
    paired = jnp.any(inside & (lengths[None] == 2 * HALF), axis=1)
    own_index = jnp.arange(4, dtype=jnp.int32)
    partner = jnp.where(is_first, own_index + 1, own_index - 1)
    facts = jnp.stack([partner, paired.astype(jnp.int32), seated.astype(jnp.int32)], 1)[1:3]
    facts = facts.reshape(6).astype(jnp.int32)
    table = inside.astype(f32)

    backs, table, facts, small, up, down = tie(stage_swap(mixed, THIRDS, 1), table, facts, small, up, down)
    mixed, mixed_both = grow_both(mixed, backs, 1)
    backs = stage_swap(mixed, THIRDS, 2)
    cond_act, buf = chain.send(small)
    up_back = swap(up, early[-1])

    shifts = jnp.array(join_masks(model_bits), jnp.int32) ^ model_index
    flip = (shifts[None] == jnp.arange(model_ways, dtype=jnp.int32)[:, None]).astype(f32)
    whole = jnp.einsum("mr,rf->mf", flip, buf[:, :images].reshape(model_ways, -1), precision=highest)
    whole = whole.reshape(model_ways, images, 6, head_cols)
    vectors = jnp.einsum("hi,mikc->khmc", table, whole, precision=highest).reshape(24, width)
    bias_rel = buf[:, images]
    bias_q, bias_v = (bias_rel[:, k * head_cols : (k + 1) * head_cols].reshape(1, -1) for k in range(2))
    step, places = feed_places(feed_count, model_bits)
    place = jnp.where((data_index & 1) == 0, places[0], places[1])
    granules = all_hidden // step
    source = (place[:, 0] * 4 + (place[:, 1] ^ (data_index & 3))) * (feed_count // step) + place[:, 2]
    source = one_hot_rows(source, granules)
    bias_up = jnp.dot(source, bias_rel[:, 2 * head_cols :].reshape(granules, step), precision=highest)
    bias_up = bias_up.reshape(1, all_hidden)
    (grad_mlp,) = call(gate_kernel, [like(local_rows, width)], (cotangent, vectors), "grad_mlp")
    (span_input,) = call(
        span_kernel, [like(2 * local_rows, width)], (before, tokens, after, vectors), "attention_input"
    )
    b_out, b_down = b_out.astype(f32).reshape(1, width), b_down.astype(f32).reshape(1, width)
    own = slice(HALF, HALF + local_rows)
    near = swap(mixed_both, CORE)
    backs, up_back, near, span_input, bias_up, bias_q, bias_v, grad_mlp, b_out, b_down, vectors, source = tie(
        backs, up_back, near, span_input, bias_up, bias_q, bias_v, grad_mlp, b_out, b_down, vectors, source
    )
    cut = up.shape[0] * 4 // 3
    outs = [like(cut, width), like(cut // 2, width)]
    up = call(join_kernel, outs, (up, up_back), "join")
    up_backs = stage_swap(up, FEED, 0)
    far = core_swap(backs)
    up_backs, far, down = tie(up_backs, far, down)
    attn_input = span_input[own]

    up = grow(up, up_backs)
    up_backs = stage_swap(up, FEED, 1)
    down_back = swap(down, early[-1])
    wq, wk, wv, wo = assemble(spot, (mixed_both, *backs, near, *far), width)
    query, key, value = call(
        qkv_kernel,
        [like(2 * local_rows, width)] * 3,
        (span_input, wq, wk, wv, bias_q, bias_v),
        "query_key_value",
    )
    up_backs, down_back, query, key, value = tie(up_backs, down_back, query, key, value)
    up, up_both = grow_both(up, up_backs, 0)
    up_backs = stage_swap(up, FEED, 2)
    down = call(join_kernel, outs, (down, down_back), "join")
    down_backs = stage_swap(down, FEED, 0)
    up_near = swap(up_both, CORE)
    attended, branch, residual, mlp_input = call(
        attend_forward,
        [like(local_rows, width), like(local_rows, width, f32), like(local_rows, width, f32), like(local_rows, width)],
        (facts, query, key, value, wo, b_out, tokens, vectors),
        "attention_forward",
        scratch=[pltpu.VMEM((2 * HALF, width), bf16)] * 2,
        smem=1,
    )

    up_backs, up_near, down_backs, mlp_input = tie(up_backs, up_near, down_backs, mlp_input)
    up_far = core_swap(up_backs)
    down = grow(down, down_backs)
    down_backs = stage_swap(down, FEED, 1)
    up_far, down_backs, mlp_input = tie(up_far, down_backs, mlp_input)
    ups = up_both, *up_backs, up_near, *up_far
    act, slope = call(up_kernel, [like(local_rows, all_hidden)] * 2, (mlp_input, bias_up, *ups), "up")
    down, down_both = grow_both(down, down_backs, 0)
    down_backs = stage_swap(down, FEED, 2)
    down_near = swap(down_both, CORE)
    down_backs, down_near, act = tie(down_backs, down_near, act)
    down_far = core_swap(down_backs)
    other = all_hidden // 2
    sizes = (up[0].shape[0], up[1].shape[0]) * 2
    sum_down = products(act, grad_mlp, other, (other,))
    down_far, sum_down = tie(down_far, sum_down)
    sum_down = core_swap(sum_down)
    downs = down_both, *down_backs, down_near, *down_far
    grad_pre, grad_bias = call(
        pre_kernel,
        [like(local_rows, all_hidden), like(1, all_hidden, f32)],
        (grad_mlp, slope, *downs),
        "grad_pre",
    )
    (grad_mlp_input,) = call(back_kernel, [like(local_rows, width, f32)], (grad_pre, *ups), "grad_mlp_input")
    grad_residual, grad_branch, grad_attended, middle_sums = call(
        middle_kernel,
        [like(local_rows, width, f32), like(local_rows, width), like(local_rows, width), like(8, width, f32)],
        (grad_mlp_input, residual, branch, cotangent, vectors, wo),
        "grad_attended",
    )
    sum_up = products(grad_pre, mlp_input, other, (other,))
    sum_down, sum_up, grad_attended, grad_branch, grad_pre = tie(
        sum_down, sum_up, grad_attended, grad_branch, grad_pre
    )
    sum_up = core_swap(sum_up)
    from_after = lax.ppermute(grad_branch[:HALF], "mp", back_to)
    from_before = lax.ppermute(grad_branch[HALF:], "mp", forth)

    full, half_full = pltpu.VMEM((2 * HALF, width), f32), pltpu.VMEM((2 * HALF, width), bf16)

    def attention_back(half, *operands):
        return call(
            lambda *refs: attend_backward(half, *refs),
            [like(local_rows, width), like(local_rows, width, f32), like(local_rows, width, f32)],
            (facts, query, key, value, grad_attended, *operands),
            "attention_backward",
            scratch=[half_full, half_full, full, full],
            smem=1,
        )

    first_half = attention_back(0)
    sum_down = products(act, grad_mlp, 0, sizes, sum_down)
    down_keeps, down_sends = sum_down[:2], sum_down[2:]
    output, output_sums = call(
        output_kernel,
        [like(local_rows, width), like(8, width, f32)],
        (act, residual, cotangent, vectors, b_down, grad_mlp, *downs),
        "output",
        scratch=[pltpu.VMEM((local_rows, width), f32)],
    )
    sum_up, from_after, from_before, first_half, down_sends, output = tie(
        sum_up, from_after, from_before, first_half, down_sends, output
    )
    down_backs = stage_swap(down_sends, FEED, 2)
    sum_up = products(grad_pre, mlp_input, 0, sizes, sum_up)
    up_keeps, up_sends = sum_up[:2], sum_up[2:]
    grad_query, own_key, own_value = attention_back(1, *first_half)
    grad_key, grad_value = call(
        attend_outside,
        [like(local_rows, width)] * 2,
        (facts, query, key, value, from_before, from_after, wo, own_key, own_value),
        "attention_outside",
        scratch=[half_full, half_full, pltpu.VMEM((HALF, width), bf16), full, full],
        smem=1,
    )
    down_backs, up_sends, grad_key, grad_value = tie(down_backs, up_sends, grad_key, grad_value)
    up_backs = stage_swap(up_sends, FEED, 2)
    lefts, rights = (grad_query, grad_key, grad_value, attended), (attn_input, grad_branch)
    sum_mixed = kind_products(1, spot, lefts, rights)
    flat_up = lax.dot_general(
        source, grad_bias.reshape(granules, step), (((0,), (0,)), ((), ())), precision=highest
    ).reshape(model_ways, hidden)
    up_backs, sum_mixed, flat_up = tie(up_backs, sum_mixed, flat_up)
    sum_mixed = core_swap(sum_mixed)
    feed_keeps, feed_sends = halve_join((*up_keeps, *down_keeps), (*up_backs, *down_backs))
    feed_backs = stage_swap(feed_sends, FEED, 1)
    grad_tokens, last_sums = call(
        last_kernel,
        [like(local_rows, width, f32), like(8, width, f32)],
        (grad_query, grad_key, grad_value, wq, wk, wv, tokens, vectors, grad_residual),
        "grad_tokens",
    )
    sum_mixed, last_sums, feed_backs = tie(sum_mixed, last_sums, feed_backs)
    sum_mixed = kind_products(0, spot, lefts, rights, sum_mixed)
    mixed_keeps, mixed_sends = sum_mixed[0::2], sum_mixed[1::2]
    mixed_backs = stage_swap(mixed_sends, THIRDS, 2)
    feed_keeps, feed_sends = halve(feed_keeps, feed_backs, 2)
    feed_backs = stage_swap(feed_sends, FEED, 0)

    sums = jnp.concatenate([last_sums[:4], middle_sums[:6], output_sums[:2]], 0).reshape(6, 2, width)
    sums = jnp.swapaxes(sums, 0, 1)
    image_sums = jnp.einsum("hi,hkd->ikd", table[1:3], sums, precision=highest)
    image_sums = image_sums.reshape(images * 6, model_ways, head_cols)
    image_sums = jnp.einsum("mr,kmc->rkc", flip, image_sums, precision=highest)

    flat_qv = [last_sums[k].reshape(model_ways, head_cols) for k in (4, 5)]
    plain = jnp.stack([middle_sums[6], output_sums[2]], 0)
    packed = jnp.concatenate([image_sums.reshape(model_ways, -1), *flat_qv, flat_up], 1)

    def gather_sums():
        buf, rest = packed.reshape(model_ways, images + 1, 6 * head_cols), plain
        for bit in reversed(joins):
            keep, send = halves(buf)
            backs = yield swap(send, (0, 1 << bit)), swap(rest, (0, 1 << bit))
            buf, rest = keep + backs[0], rest + backs[1]
        mods, bias = buf[0, :images].astype(bf16)[None], buf[0, images:]
        rest = jnp.concatenate([rest.reshape(-1), bias.reshape(-1)], 0)
        for level in range(data_bits):
            backs = yield swap(mods, (1 << level, 0)), swap(rest, (1 << level, 0))
            mods, rest = jnp.concatenate([mods, backs[0]], 0), rest + backs[1]
        yield mods, rest

    mixed_backs, feed_backs, packed, plain = tie(mixed_backs, feed_backs, packed, plain)
    chain = gather_sums()
    steps = model_bits + data_bits
    small = next(chain)
    mixed_keeps, mixed_sends = halve(mixed_keeps, mixed_backs)
    mixed_backs = stage_swap(mixed_sends, THIRDS, 1)
    merged_rows = feed_count << len(early) - 1
    feed_keep, feed_send = merge(merge_rows_kernel, feed_keeps, feed_backs, merged_rows, 2 * width)
    feed_back = swap(feed_send, early[-1])
    mixed_backs, feed_back, small = tie(mixed_backs, feed_back, small)
    small = chain.send(small)
    steps -= 1
    mixed_keeps, mixed_sends = halve(mixed_keeps, mixed_backs)
    mixed_backs = stage_swap(mixed_sends, THIRDS, 0)
    feed_done = added(feed_keep, feed_back)
    for bits in reversed(early[:-1]):
        keep, send = halves(feed_done)
        feed_done = added(keep, swap(send, bits))
    feed_done = jnp.stack([feed_done[:, :width], feed_done[:, width:]], 0)
    for level in reversed(range(2, data_bits)):
        feed_done = lanes_sum(feed_done, level, data_index)
    mixed_backs, feed_done, small = tie(mixed_backs, feed_done, small)
    small = chain.send(small)
    steps -= 1
    merged_rows = head_cols << len(early) - 1
    mixed_keep, mixed_send = merge(merge_lanes_kernel, mixed_keeps, mixed_backs, merged_rows, width)
    mixed_back = swap(mixed_send, early[-1])
    feed_keep, feed_back = lanes_send(feed_done, 1, data_index)
    mixed_back, feed_back, small = tie(mixed_back, feed_back, small)
    small = chain.send(small)
    steps -= 1
    mixed_done = added(mixed_keep, mixed_back)
    for bits in reversed(early[:-1]):
        keep, send = halves(mixed_done)
        mixed_done = added(keep, swap(send, bits))
    for level in reversed(range(2, data_bits)):
        mixed_done = lanes_sum(mixed_done, level, data_index)
    keep, back = lanes_send(mixed_done, 1, data_index)
    feed_done = rows_join(feed_keep, feed_back, 1, data_index, 0)
    feed_keep, feed_back = lanes_send(feed_done, 0, data_index)
    back, feed_back, small = tie(back, feed_back, small)
    small = chain.send(small)
    steps -= 1
    mixed_done = rows_join(keep, back, 1, data_index, 0)
    keep, back = lanes_send(mixed_done, 0, data_index)
    feed_done = rows_join(feed_keep, feed_back, 0, data_index, 1).reshape(4, 2, feed_count, lanes)
    for _ in range(steps):
        small = chain.send(small)
    mixed_done = rows_join(keep, back, 0, data_index, 1).reshape(4, head_cols, lanes)
    grad_modulation, rest = small
    grad_w_ada = tn(
        cond_act.reshape(data_ways * images, lanes),
        grad_modulation.reshape(data_ways * images, 6 * head_cols),
    )
    grad_w_ada = grad_w_ada.reshape(lanes, 6, head_cols)
    grad_b_ada = jnp.sum(grad_modulation, axis=(0, 1), dtype=f32).reshape(6, head_cols)
    grad_b_out, grad_b_down = rest[:width], rest[width : 2 * width]
    rest = rest[2 * width :]
    grad_b_qv, grad_b_up = rest[: 2 * head_cols].reshape(2, head_cols), rest[2 * head_cols :]

    grad_w_up, grad_w_down = call(
        place_feed_kernel, [like(lanes, hidden, f32), like(hidden, lanes, f32)], (feed_done,), "place_feed_forward"
    )
    grad_w_qkv, grad_w_out = call(
        place_mixed_kernel,
        [jax.ShapeDtypeStruct(w_qkv.shape, f32), like(head_cols, lanes, f32)],
        (mixed_done,),
        "place_attention",
    )
    return (
        output,
        grad_tokens,
        grad_w_ada,
        grad_b_ada,
        grad_w_qkv,
        grad_b_qv,
        grad_w_out,
        grad_b_out,
        grad_w_up,
        grad_b_up,
        grad_w_down,
        grad_b_down,
    )


def solution(mesh):
    in_specs = (
        P(("dp", "mp"), None),
        P("dp", None),
        P("dp"),
        P("dp", None, "mp"),
        P(None, "mp"),
        P(None, "dp", "mp"),
        P(None, "mp"),
        P("mp", "dp"),
        P(),
        P("dp", "mp"),
        P("mp"),
        P("mp", "dp"),
        P(),
        P(("dp", "mp"), None),
    )
    out_specs = (
        P(("dp", "mp"), None),
        P(("dp", "mp"), None),
        P("dp", None, "mp"),
        P(None, "mp"),
        P(None, "dp", "mp"),
        P(None, "mp"),
        P("mp", "dp"),
        P(),
        P("dp", "mp"),
        P("mp"),
        P("mp", "dp"),
        P(),
    )
    return jax.shard_map(
        on_device, mesh=mesh, in_specs=in_specs, out_specs=out_specs, check_vma=False
    )
```

```python
import itertools
import math

import jax
import jax.numpy as jnp
import numpy as np
from jax import lax
from jax.experimental import pallas as pl
from jax.experimental.pallas import tpu as pltpu
from jax.sharding import PartitionSpec as P

HD = 72
HALF = 128
LANE = 128
EPS = 1e-06
HIDE = -1e30

f32, bf16 = jnp.float32, jnp.bfloat16
highest = lax.Precision.HIGHEST

CORE, Y, X, Z1 = (1, 0), (2, 0), (0, 1), (0, 2)


def swap(values, even, odd=None):
    odd = even if odd is None else odd
    data_ways, model_ways = lax.axis_size("dp"), lax.axis_size("mp")
    pairs = []
    for d in range(data_ways):
        d_bits, m_bits = odd if d % 2 else even
        for m in range(model_ways):
            pairs.append((d * model_ways + m, (d ^ d_bits) * model_ways + (m ^ m_bits)))
    return lax.ppermute(values, ("dp", "mp"), pairs)


def bits_of(count):
    return count.bit_length() - 1


def pick(values, axis, index):
    low, high = (lax.index_in_dim(values, k, axis, keepdims=False) for k in (0, 1))
    return jnp.where(index == 0, low, high)


def nn(a, b):
    return jnp.dot(a, b, preferred_element_type=f32)


def nt(a, b):
    return lax.dot_general(a, b, (((1,), (1,)), ((), ())), preferred_element_type=f32)


def tn(a, b):
    return lax.dot_general(a, b, (((0,), (0,)), ((), ())), preferred_element_type=f32)


def head_windows(width):
    for head in range(width // HD):
        first, last = head * HD, head * HD + HD
        low = first // LANE * LANE
        high = -(-last // LANE) * LANE
        yield first, last, low, high


def lane_mask(first, last, low, high):
    lane = lax.broadcasted_iota(jnp.int32, (HALF, high - low), 1) + low
    return (lane >= first) & (lane < last)


def same_segment(paired, seated):
    row = lax.broadcasted_iota(jnp.int32, (HALF, 2 * HALF), 0)
    col = lax.broadcasted_iota(jnp.int32, (HALF, 2 * HALF), 1)
    own = (col < HALF) & ((row == col) | (seated > 0))
    return own | ((col >= HALF) & (paired > 0))


def same_segment_keys(paired, seated):
    key = lax.broadcasted_iota(jnp.int32, (2 * HALF, HALF), 0)
    col = lax.broadcasted_iota(jnp.int32, (2 * HALF, HALF), 1)
    own = (key < HALF) & ((key == col) | (seated > 0))
    return own | ((key >= HALF) & (paired > 0))


def split_rows(rows):
    return pl.ds(rows * HALF, HALF)


def row(vectors, kind, half):
    return vectors[4 * kind + half : 4 * kind + half + 1]


def normalize(values):
    centred = values - jnp.mean(values, axis=-1, keepdims=True)
    spread = jnp.mean(centred * centred, axis=-1, keepdims=True)
    root = lax.rsqrt(spread + EPS)
    return centred * root, root


def normalize_back(norm, root, upstream):
    return (
        upstream
        - jnp.mean(upstream, axis=-1, keepdims=True)
        - norm * jnp.mean(upstream * norm, axis=-1, keepdims=True)
    ) * root


def column_sum(values):
    return jnp.sum(values, axis=0, keepdims=True)


def vectors_kernel(columns, images, shifts, buf, out, part):
    part[...] = jnp.zeros(part.shape, f32)
    for block in range(buf.shape[0]):
        for half in range(4):
            number = lax.broadcasted_iota(jnp.int32, buf.shape[1:], 0)
            vector = column_sum(jnp.where(number == images[half], buf[block], 0.0))
            for kind in range(6):
                part[4 * kind + half : 4 * kind + half + 1, :columns] = vector[:, kind * columns : (kind + 1) * columns]
        moved = pltpu.roll(part[...], shifts[block] * columns, 1)
        out[...] = moved if block == 0 else out[...] + moved


def pack_kernel(columns, images, shifts, last, middle, output, bias_up, out, plain, rows):
    count, _, lanes = out.shape
    bias_row = out.shape[1] - 1
    width = rows.shape[1]
    rows[...] = jnp.zeros(rows.shape, f32)
    rows[0:4], rows[4:10], rows[10:12] = last[0:4], middle[0:6], output[0:2]
    out[...] = jnp.zeros(out.shape, f32)
    plain[...] = jnp.zeros(plain.shape, f32)
    for block in range(count):
        moved = pltpu.roll(rows[...], jnp.where(shifts[block] > 0, width - shifts[block] * columns, 0), 1)
        number = lax.broadcasted_iota(jnp.int32, (out.shape[1], columns), 0)
        for kind in range(6):
            place = slice(kind * columns, (kind + 1) * columns)
            low, high = (moved[2 * kind + half : 2 * kind + half + 1, :columns] for half in range(2))
            out[block, :, place] = jnp.where(number == images[1], low, 0.0) + jnp.where(number == images[2], high, 0.0)
        mine = slice(block * columns, (block + 1) * columns)
        out[block, bias_row : bias_row + 1, :columns] = last[4:5, mine]
        out[block, bias_row : bias_row + 1, columns : 2 * columns] = last[5:6, mine]
        out[block, bias_row : bias_row + 1, 2 * columns : 6 * columns] = bias_up[block : block + 1]
    per = -(-width // lanes)
    for k, source in enumerate((middle[6:7], output[2:3])):
        for piece in range(per):
            size = min(lanes, width - piece * lanes)
            plain[0, k * per + piece : k * per + piece + 1, :size] = source[:, piece * lanes : piece * lanes + size]


def span_kernel(before, tokens, after, vectors, out):
    for half in range(4):
        source = (before, tokens, tokens, after)[half]
        norm, _ = normalize(source[split_rows(half == 2)].astype(f32))
        out[split_rows(half)] = (norm * (1.0 + row(vectors, 1, half)) + row(vectors, 0, half)).astype(bf16)


def qkv_kernel(span, wq, wk, wv, bias_q, bias_v, query, key, value):
    query[...] = (nt(span[...], wq[...]) + bias_q[...]).astype(bf16)
    key[...] = nt(span[...], wk[...]).astype(bf16)
    value[...] = (nt(span[...], wv[...]) + bias_v[...]).astype(bf16)


def attend_forward(
    facts, q_ref, k_ref, v_ref, wo, b_out, tokens, vectors, o_ref, branch_ref, residual_ref, input_ref, kk, vv
):
    factor = HD ** (-0.5)
    for half in range(2):
        rows = split_rows(half)
        own = split_rows(half + 1)
        other = pl.ds(pl.multiple_of(facts[3 * half] * HALF, HALF), HALF)
        kk[0:HALF], kk[HALF:] = k_ref[own], k_ref[other]
        vv[0:HALF], vv[HALF:] = v_ref[own], v_ref[other]
        same = same_segment(facts[3 * half + 1], facts[3 * half + 2])
        for first, last, low, high in head_windows(q_ref.shape[1]):
            window = slice(low, high)
            mask = lane_mask(first, last, low, high)
            query = jnp.where(mask, q_ref[own, window], 0)
            scores = jnp.where(same, nt(query, kk[:, window]) * factor, HIDE)
            exp_scores = jnp.exp(scores - jnp.max(scores, axis=1, keepdims=True))
            prob = exp_scores / jnp.sum(exp_scores, axis=1, keepdims=True)
            mixed = nn(prob.astype(bf16), vv[:, window]).astype(bf16)
            o_ref[rows, window] = jnp.where(mask, mixed, o_ref[rows, window]) if first > low else mixed
    for half in range(2):
        rows = split_rows(half)
        branch = nn(o_ref[rows], wo[...]) + b_out[...]
        branch_ref[rows] = branch
        residual = tokens[rows].astype(f32) + row(vectors, 2, half + 1) * branch
        residual_ref[rows] = residual
        norm, _ = normalize(residual)
        input_ref[rows] = (norm * (1.0 + row(vectors, 4, half + 1)) + row(vectors, 3, half + 1)).astype(bf16)


def score_gradients(query, grad, keys, values, same):
    scores = nt(keys, query) * HD ** (-0.5)
    if same is not None:
        scores = jnp.where(same, scores, HIDE)
    exp_scores = jnp.exp(scores - jnp.max(scores, axis=0, keepdims=True))
    prob = exp_scores / jnp.sum(exp_scores, axis=0, keepdims=True)
    grad_prob = nt(values, grad)
    inner = jnp.sum(grad_prob * prob, axis=0, keepdims=True)
    return prob.astype(bf16), (prob * (grad_prob - inner)).astype(bf16)


def attend_backward(half, facts, q_ref, k_ref, v_ref, g_ref, *refs):
    earlier, refs = (refs[:3], refs[3:]) if half else (None, refs)
    dq_ref, own_k, own_v, kk, vv, dkk, dvv = refs
    factor = HD ** (-0.5)
    rows = split_rows(half)
    own = split_rows(half + 1)
    other = pl.ds(pl.multiple_of(facts[3 * half] * HALF, HALF), HALF)
    kk[0:HALF], kk[HALF:] = k_ref[own], k_ref[other]
    vv[0:HALF], vv[HALF:] = v_ref[own], v_ref[other]
    dkk[...] = jnp.zeros(dkk.shape, f32)
    dvv[...] = jnp.zeros(dvv.shape, f32)
    if half:
        dq_ref[0:HALF] = earlier[0][0:HALF]
    same = same_segment_keys(facts[3 * half + 1], facts[3 * half + 2])
    for first, last, low, high in head_windows(q_ref.shape[1]):
        window = slice(low, high)
        mask = lane_mask(first, last, low, high)
        query = jnp.where(mask, q_ref[own, window], 0)
        grad = jnp.where(mask, g_ref[rows, window], 0)
        prob, grad_scores = score_gradients(query, grad, kk[:, window], vv[:, window], same)
        dq = (tn(grad_scores, kk[:, window]) * factor).astype(bf16)
        dq_ref[rows, window] = jnp.where(mask, dq, dq_ref[rows, window]) if first > low else dq
        dkk[:, window] += nn(grad_scores, query) * factor
        dvv[:, window] += nn(prob, grad)
    inside = jnp.where(facts[3 * half] == 2 - half, 1.0, 0.0)
    for place, (total, mine) in enumerate(((dkk, own_k), (dvv, own_v))):
        mine_own, mine_other = total[0:HALF], total[HALF:] * inside
        if half:
            mine_own = mine_own + earlier[1 + place][split_rows(half)]
            mine_other = mine_other + earlier[1 + place][split_rows(1 - half)]
        mine[split_rows(half)], mine[split_rows(1 - half)] = mine_own, mine_other


def attend_outside(
    facts, q_ref, k_ref, v_ref, before, after, wo, own_k, own_v, key_ref, value_ref, kk, vv, grads, dk, dv
):
    factor = HD ** (-0.5)
    dk[...], dv[...] = own_k[...], own_v[...]
    for half, (outside, branch) in enumerate(((0, before), (3, after))):

        @pl.when((facts[3 * half] == outside) & (facts[3 * half + 1] > 0))
        def _():
            mine, theirs = split_rows(half), split_rows(outside)
            kk[0:HALF], kk[HALF:] = k_ref[theirs], k_ref[split_rows(half + 1)]
            vv[0:HALF], vv[HALF:] = v_ref[theirs], v_ref[split_rows(half + 1)]
            grads[...] = nt(branch[...], wo[...]).astype(bf16)
            for first, last, low, high in head_windows(q_ref.shape[1]):
                window = slice(low, high)
                mask = lane_mask(first, last, low, high)
                query = jnp.where(mask, q_ref[theirs, window], 0)
                grad = jnp.where(mask, grads[:, window], 0)
                prob, grad_scores = score_gradients(query, grad, kk[:, window], vv[:, window], None)
                dk[mine, window] += nn(grad_scores[HALF:], query) * factor
                dv[mine, window] += nn(prob[HALF:], grad)

    key_ref[...], value_ref[...] = dk[...].astype(bf16), dv[...].astype(bf16)


def middle_kernel(
    grad_input, residual, branch, cotangent, vectors, wo, grad_residual, grad_branch, grad_attended, sums
):
    sums[...] = jnp.zeros(sums.shape, f32)
    for half in range(2):
        rows = split_rows(half)
        norm, root = normalize(residual[rows])
        grad = grad_input[rows]
        total = cotangent[rows].astype(f32) + normalize_back(norm, root, grad * (1.0 + row(vectors, 4, half + 1)))
        grad_residual[rows] = total
        low = (row(vectors, 2, half + 1) * total).astype(bf16)
        grad_branch[rows] = low
        grad_attended[rows] = nt(low, wo[...]).astype(bf16)
        sums[half : half + 1] = column_sum(total * branch[rows])
        sums[2 + half : 3 + half] = column_sum(grad)
        sums[4 + half : 5 + half] = column_sum(grad * norm)
        sums[6:7] += column_sum(low.astype(f32))


def last_kernel(
    grad_query, grad_key, grad_value, wq, wk, wv, tokens, vectors, grad_residual, grad_tokens, sums
):
    sums[...] = jnp.zeros(sums.shape, f32)
    for half in range(2):
        rows = split_rows(half)
        norm, root = normalize(tokens[rows].astype(f32))
        grad = nn(grad_query[rows], wq[...]) + nn(grad_key[rows], wk[...]) + nn(grad_value[rows], wv[...])
        back = normalize_back(norm, root, grad * (1.0 + row(vectors, 1, half + 1)))
        grad_tokens[rows] = grad_residual[rows] + back
        sums[half : half + 1] = column_sum(grad)
        sums[2 + half : 3 + half] = column_sum(grad * norm)
        sums[4:5] += column_sum(grad_query[rows].astype(f32))
        sums[5:6] += column_sum(grad_value[rows].astype(f32))


VMEM = pl.BlockSpec(memory_space=pltpu.VMEM)
SMEM = pl.BlockSpec(memory_space=pltpu.SMEM)


CHUNK = 96
HINT = pl.CostEstimate(flops=1, bytes_accessed=1, transcendentals=0)


def call(kernel, outs, operands, name, scratch=(), smem=0):
    room = sum(math.prod(v.shape) * v.dtype.itemsize for v in (*scratch, *outs) if hasattr(v, "shape")) + 4 * 2**20
    return pl.pallas_call(
        kernel,
        out_shape=tuple(outs),
        in_specs=[SMEM] * smem + [VMEM] * (len(operands) - smem),
        out_specs=tuple(VMEM for _ in outs),
        scratch_shapes=list(scratch),
        compiler_params=pltpu.CompilerParams(vmem_limit_bytes=room),
        cost_estimate=HINT,
        name=name,
    )(*operands)


def like(rows, width, dtype=bf16):
    return jax.ShapeDtypeStruct((rows, width), dtype)


def grow_kernel(refs, axis=None):
    count = (len(refs) - (axis is not None)) // 3
    both, place = refs[-1], 0
    for own, back, out in zip(refs[:count], refs[count : 2 * count], refs[2 * count : 3 * count]):
        rows, lanes = own.shape
        out[:rows], out[rows:] = own[...], back[...]
        if axis == 0:
            both[place : place + rows], both[place + rows : place + 2 * rows] = own[...], back[...]
            place += 2 * rows
        if axis == 1:
            both[:rows, place : place + lanes], both[rows:, place : place + lanes] = own[...], back[...]
            place += lanes


def grow(parts, backs):
    outs = [like(2 * part.shape[0], part.shape[1]) for part in parts]
    return call(lambda *refs: grow_kernel(refs), outs, (*parts, *backs), "grow")


def grow_both(parts, backs, axis):
    outs = [like(2 * part.shape[0], part.shape[1]) for part in parts]
    if axis == 0:
        both = like(sum(out.shape[0] for out in outs), outs[0].shape[1])
    else:
        both = like(outs[0].shape[0], sum(out.shape[1] for out in outs))
    outs = call(lambda *refs: grow_kernel(refs, axis), [*outs, both], (*parts, *backs), "grow_both")
    return outs[:-1], outs[-1]


def row_sum(keep, back, first, last):
    return keep[first:last] + back[first:last]


def halve_kernel(groups, side, *refs):
    count = len(refs) // 3
    for keep, back, out in zip(refs[:count], refs[count : 2 * count], refs[2 * count :]):
        rows = keep.shape[0] // (2 * groups)
        for group in range(groups):
            base = (2 * group + side) * rows
            for first in range(0, rows, CHUNK):
                last = min(first + CHUNK, rows)
                out[group * rows + first : group * rows + last] = row_sum(keep, back, base + first, base + last)


def halve(keeps, backs, groups=1):
    outs = [like(keep.shape[0] // 2, keep.shape[1]) for keep in keeps]
    high, low = (
        call(lambda *refs, side=side: halve_kernel(groups, side, *refs), outs, (*keeps, *backs), "halve")
        for side in (1, 0)
    )
    return low, high


def halve_join_kernel(side, *refs):
    count = len(refs) // 5
    keeps, backs, outs = refs[: 2 * count], refs[2 * count : 4 * count], refs[4 * count :]
    for k in range(count):
        for which in range(2):
            keep, back = keeps[which * count + k], backs[which * count + k]
            rows = keep.shape[0] // 2
            for first in range(0, rows, CHUNK):
                last = min(first + CHUNK, rows)
                outs[k][which * rows + first : which * rows + last] = row_sum(
                    keep, back, side * rows + first, side * rows + last
                )


def halve_join(keeps, backs):
    outs = [like(keep.shape[0], keep.shape[1]) for keep in keeps[: len(keeps) // 2]]
    high, low = (
        call(lambda *refs, side=side: halve_join_kernel(side, *refs), outs, (*keeps, *backs), "halve_join")
        for side in (1, 0)
    )
    return low, high


def merge_rows_kernel(*refs):
    count = (len(refs) - 2) // 2
    low, high = refs[2 * count :]
    rows, width = low.shape[0], low.shape[1] // 2
    for which in range(2):
        lanes = slice(which * width, (which + 1) * width)
        place = 0
        for keep, back in zip(refs[:count], refs[count : 2 * count]):
            first, end = which * keep.shape[0] // 2, (which + 1) * keep.shape[0] // 2
            while first < end:
                out, base = (low, 0) if place < rows else (high, rows)
                step = min(end - first, base + rows - place)
                out[place - base : place - base + step, lanes] = row_sum(keep, back, first, first + step)
                first, place = first + step, place + step


def merge_lanes_kernel(*refs):
    count = (len(refs) - 2) // 2
    low, high = refs[2 * count :]
    rows, lane = low.shape[0], 0
    for keep, back in zip(refs[:count], refs[count : 2 * count]):
        lanes = slice(lane, lane + keep.shape[1])
        lane += keep.shape[1]
        low[:, lanes], high[:, lanes] = row_sum(keep, back, 0, rows), row_sum(keep, back, rows, 2 * rows)


def merge(kernel, keeps, backs, rows, width):
    return call(kernel, [like(rows, width)] * 2, (*keeps, *backs), "merge")


def row_steps(weights):
    unit = 0
    for weight in weights:
        rows = weight.shape[0]
        step = 256 if rows % 256 == 0 else 384
        for first in range(0, rows, step):
            yield weight, first, first + step, unit + first
        unit += rows


def up_kernel(x_ref, bias_ref, *refs):
    weights, (act_ref, slope_ref) = refs[:-2], refs[-2:]
    for weight, first, last, unit in row_steps(weights):
        units = slice(unit, unit + last - first)
        pre = nt(x_ref[...], weight[first:last]) + bias_ref[:, units]
        square = pre * pre
        inner = jnp.tanh(0.7978845608028654 * pre * (1.0 + 0.044715 * square))
        outer = 0.5 * (1.0 + inner)
        act_ref[:, units] = (pre * outer).astype(bf16)
        rise = (0.5 * 0.7978845608028654) * pre * (1.0 + (3 * 0.044715) * square)
        slope_ref[:, units] = (outer + rise * (1.0 - inner * inner)).astype(bf16)


def down_kernel(grad_mlp, slope, act, residual, cotangent, vectors, b_down, *refs):
    weights, (pre_ref, sum_ref, out, sums, total) = refs[:-5], refs[-5:]
    for weight, first, last, unit in row_steps(weights):
        units = slice(unit, unit + last - first)
        pre = (nt(grad_mlp[...], weight[first:last]) * slope[:, units].astype(f32)).astype(bf16)
        pre_ref[:, units] = pre
        sum_ref[:, units] = column_sum(pre.astype(f32))
    back_kernel(act, *weights, total)
    sums[...] = jnp.zeros(sums.shape, f32)
    for half in range(2):
        rows = split_rows(half)
        mlp = total[rows] + b_down[...]
        out[rows] = (residual[rows] + row(vectors, 5, half + 1) * mlp).astype(bf16)
        sums[half : half + 1] = column_sum(cotangent[rows].astype(f32) * mlp)
        sums[2:3] += column_sum(grad_mlp[rows].astype(f32))


def back_kernel(left_ref, *refs):
    weights, out_ref = refs[:-1], refs[-1]
    unit = 0
    for weight in weights:
        rows = weight.shape[0]
        part = nn(left_ref[:, unit : unit + rows], weight[...])
        out_ref[...] = part if unit == 0 else out_ref[...] + part
        unit += rows


def join_kernel(own, back, wide, narrow):
    rows = own.shape[0]
    more = wide.shape[0] - rows
    wide[:rows], wide[rows:] = own[...], back[:more]
    narrow[...] = back[more:]


def place_feed_kernel(done, grad_up, grad_down):
    for which, out in enumerate((grad_up, grad_down)):
        out[...] = jnp.concatenate([done[way, which] for way in range(done.shape[0])], 0).astype(f32).T


def gate_kernel(cotangent, vectors, out):
    for half in range(2):
        rows = split_rows(half)
        out[rows] = (row(vectors, 5, half + 1) * cotangent[rows].astype(f32)).astype(bf16)


def product_kernel(start, left_ref, right_ref, *refs):
    back, outs = (refs[0], refs[1:]) if len(refs) > 1 and refs[0].shape != refs[-1].shape else (None, refs)
    base = 0
    for out in outs:
        size = out.shape[0]
        step = 256 if size % 256 == 0 else 384
        for first in range(0, size, step):
            column = start + base + first
            part = tn(left_ref[:, column : column + step], right_ref[...])
            if back is not None:
                part = part + back[base + first : base + first + step].astype(f32)
            out[first : first + step] = part.astype(bf16)
        base += size


def products(left, right, start, counts, backs=()):
    outs = [like(size, right.shape[1]) for size in counts]
    return call(lambda *refs: product_kernel(start, *refs), outs, (left, right, *backs), "products")


def unit_of(third, y, z, x):
    return ((x, 2 * y + z), (y, 2 * z + x), (z, 2 * x + y))[third]


def assemble_kernel(spot, *refs):
    sides, outs = (refs[:4], refs[4:8]), refs[8:]
    unit = outs[0].shape[0] // 4
    width = outs[0].shape[1] // 3

    def place(core, why):
        for kind, out in enumerate(outs):
            side, y = (kind & 1) ^ core, (kind >> 1) ^ why
            for third in range(3):
                lanes = slice(third * width, (third + 1) * width)
                for z in range(2):
                    for x in range(2):
                        array, index = unit_of(third, y, z, x)
                        rows = slice(index * unit, (index + 1) * unit)
                        source = sides[side][1 + third][rows] if array else sides[side][0][rows, lanes]
                        out[(2 * z + x) * unit : (2 * z + x + 1) * unit, lanes] = source

    for core in range(2):
        for why in range(2):
            pl.when((spot[0] == core) & (spot[1] == why))(lambda core=core, why=why: place(core, why))


def assemble(spot, arrays, width):
    return call(assemble_kernel, [like(width, width)] * 4, (spot, *arrays), "assemble", smem=1)


def kinds_kernel(side, spot, *refs):
    lefts, rights, refs, left, right = refs[:4], refs[4:6], refs[6:-2], refs[-2], refs[-1]
    back, outs = (None, refs) if side else (refs[0], refs[1:])
    width = left.shape[1]
    unit, third_width = width // 4, width // 3
    for y in range(2):
        kind = (spot[1] ^ y) * 2 + (spot[0] ^ side)
        for k in range(4):

            @pl.when(kind == k)
            def _():
                left[...] = lefts[k][...]
                right[...] = rights[k == 3][...]

        for third in range(3):
            lanes = slice(third * third_width, (third + 1) * third_width)
            part = tn(left[...], right[:, lanes])
            for z in range(2):
                for x in range(2):
                    array, index = unit_of(third, y, z, x)
                    rows = slice(index * unit, (index + 1) * unit)
                    both_rows = slice(array * width + index * unit, array * width + (index + 1) * unit)
                    piece = part[(2 * z + x) * unit : (2 * z + x + 1) * unit]
                    if side:
                        outs[0][both_rows, lanes] = piece.astype(bf16)
                    else:
                        piece = piece + back[both_rows, lanes].astype(f32)
                        outs[2 * third + array][rows] = piece.astype(bf16)


def kind_products(side, spot, lefts, rights, backs=()):
    rows, width = lefts[0].shape
    return call(
        lambda *refs: kinds_kernel(side, *refs),
        [like(2 * width, width)] if side else [like(width, width // 3)] * 6,
        (spot, *lefts, *rights, *backs),
        "kind_products",
        scratch=[pltpu.VMEM((rows, width), bf16)] * 2,
        smem=1,
    )


def rows_send(parts, axis, level, data_index):
    bit = (data_index >> level) & 1
    return pick(parts, axis, bit), swap(pick(parts, axis, 1 - bit), (1 << level, 0))


def lanes_join(keep, back, level, data_index):
    bit = (data_index >> level) & 1
    return jnp.where(bit == 0, jnp.concatenate([keep, back], -1), jnp.concatenate([back, keep], -1))


def lanes_split(block, level, data_index):
    bit = (data_index >> level) & 1
    width = block.shape[-1] // 2
    low, high = block[..., :width], block[..., width:]
    return jnp.where(bit == 0, low, high), jnp.where(bit == 0, high, low)


def lanes_send(block, level, data_index):
    keep, send = lanes_split(block, level, data_index)
    return keep, swap(send, (1 << level, 0))


def lanes_sum(block, level, data_index):
    keep, send = lanes_split(block, level, data_index)
    return added(keep, swap(send, (1 << level, 0)))


def rows_join(keep, back, level, data_index, lead):
    bit = (data_index >> level) & 1
    return jnp.where(bit == 0, jnp.stack([keep, back], lead), jnp.stack([back, keep], lead))


def halves(buf):
    size = buf.shape[0] // 2
    return buf[:size], buf[size:]


def added(keep, back):
    return (keep.astype(f32) + back.astype(f32)).astype(bf16)


def tie(*values):
    return lax.optimization_barrier(values) if len(values) > 1 else lax.optimization_barrier(values[0])


FEED = (((X, Y), (Y, Z1), (Z1, X)), ((Z1, Z1), (X, X), (Y, Y)))
THIRDS = tuple(tuple((bits, bits) for bits in order) for order in ((Z1, Y, X), (X, Z1, Y), (Y, X, Z1)))


def early_bits(model_bits):
    return [(0, 1 << k) for k in range(2, model_bits)]


def stage_swap(parts, plan, stage):
    return tuple(swap(part, *table[stage]) for part, table in zip(parts, plan))


def core_swap(parts):
    return tuple(swap(part, CORE) for part in parts)


def early_join(buf, bits):
    return jnp.concatenate([buf, swap(buf, bits)], 0)


def join_order(model_bits):
    return [*range(2, model_bits), 0, 1]


def join_masks(model_bits):
    joins = join_order(model_bits)
    return [sum(((place >> k) & 1) << bit for k, bit in enumerate(joins)) for place in range(1 << model_bits)]


def feed_places(rows, model_bits):
    early = early_bits(model_bits)
    unit_rows = rows << len(early)
    cut = unit_rows * 2 // 3
    step = math.gcd(rows, cut)
    tables = []
    for core in range(2):
        places = []
        spans = range(0, cut, step), range(cut, unit_rows, step)
        for side, last, (table, span), *bits in itertools.product(
            range(2), range(2), list(zip(FEED, spans)), range(2), range(2)
        ):
            d, m = side, 0
            for bit, stage in zip((last, *bits), reversed(table)):
                d, m = d ^ bit * stage[core ^ side][0], m ^ bit * stage[core ^ side][1]
            for row in span:
                block, m_row = row // rows, m
                for level, (_, m_bits) in enumerate(early):
                    m_row = m_row ^ ((block >> level) & 1) * m_bits
                places.append((join_masks(model_bits).index(m_row), d, row % rows // step))
        tables.append(np.array(places, np.int32))
    return step, tables


def one_hot_rows(index, count):
    return (index[:, None] == jnp.arange(count, dtype=jnp.int32)[None]).astype(f32)


def on_device(
    tokens,
    conditioning,
    lengths,
    w_ada,
    b_ada,
    w_qkv,
    b_qv,
    w_out,
    b_out,
    w_up,
    b_up,
    w_down,
    b_down,
    cotangent,
):
    data_ways, model_ways = lax.axis_size("dp"), lax.axis_size("mp")
    data_index, model_index = lax.axis_index("dp"), lax.axis_index("mp")
    data_bits, model_bits = bits_of(data_ways), bits_of(model_ways)
    early = early_bits(model_bits)
    local_rows, width = tokens.shape
    lanes = width // data_ways
    head_cols = w_qkv.shape[2]
    hidden = w_up.shape[1]
    images = lengths.shape[0]
    binary = (2,) * data_bits
    feed_count = hidden // 4
    all_hidden = hidden * model_ways
    spot = jnp.stack([data_index & 1, (data_index >> 1) & 1]).astype(jnp.int32)
    forth = [(k, k + 1) for k in range(model_ways - 1)]
    back_to = [(k + 1, k) for k in range(model_ways - 1)]

    mixed = jnp.concatenate([jnp.swapaxes(w_qkv, 1, 2), w_out[None]], 0).reshape(2, 2, 1, head_cols, lanes)
    keep, back = rows_send(mixed, 1, 0, data_index)
    feed = jnp.stack([jnp.swapaxes(w_up, 0, 1), w_down], 0).reshape(2, 2, 2, feed_count, lanes)
    feed_keep, feed_back = rows_send(feed, 2, 0, data_index)
    others = [swap(conditioning, (d, 0)) for d in range(1, data_ways)]
    back, feed_back, others = tie(back, feed_back, others)
    cond = jnp.stack([conditioning, *others], 0)
    mixed = lanes_join(keep, back, 0, data_index)
    joins = join_order(model_bits)
    small_rows, small_lanes = -(-(images + 1) // 8) * 8, -(-6 * head_cols // LANE) * LANE

    def modulate(cond):
        part = lax.dynamic_slice_in_dim(cond, data_index * lanes, lanes, 2).astype(f32)
        cond_act = jax.nn.silu(part).astype(bf16)
        mod = nn(cond_act.reshape(data_ways * images, lanes), w_ada.reshape(lanes, 6 * head_cols))
        mod = mod.reshape(data_ways, images, 6 * head_cols)
        backs = yield [swap(mod[d], (d, 0)) for d in range(1, data_ways)]
        mod = sum(backs, mod[0]) + b_ada.astype(f32).reshape(1, 6 * head_cols)
        biases = jnp.concatenate([b_qv.reshape(-1), b_up], 0).astype(f32)
        buf = jnp.pad(mod, ((0, small_rows - images), (0, small_lanes - 6 * head_cols)))
        bias = jnp.pad(biases[None], ((small_rows - 1, 0), (0, small_lanes - 6 * head_cols)))
        buf = (buf + bias)[None]
        for bit in joins:
            back = yield swap(buf, (0, 1 << bit))
            buf = jnp.concatenate([buf, back], 0)
        yield (cond_act, buf)

    steps = 1 + model_bits

    for k, bits in enumerate(early):
        back = swap(mixed, bits)
        if k == 0:
            feed = lanes_join(feed_keep, feed_back, 0, data_index)
            feed_keep, feed_back = rows_send(feed, 1, 1, data_index)
            chain = modulate(cond)
            small = next(chain)
            back, feed_back, small = tie(back, feed_back, small)
            small = chain.send(small)
            steps -= 1
        mixed = jnp.concatenate([mixed, back], 1)
    keep, back = rows_send(mixed, 0, 1, data_index)
    before, after = lax.ppermute(tokens[HALF:], "mp", forth), lax.ppermute(tokens[:HALF], "mp", back_to)
    back, small, lengths, before, after = tie(back, small, lengths, before, after)
    small = chain.send(small)
    steps -= 1
    mixed = lanes_join(keep, back, 1, data_index)
    for level in range(2, data_bits):
        mixed = lanes_join(mixed, swap(mixed, (1 << level, 0)), level, data_index)
    mixed = mixed.reshape(-1, width)
    third = width // 3
    mixed = tuple(mixed[:, k * third : (k + 1) * third] for k in range(3))
    feed = lanes_join(feed_keep, feed_back, 1, data_index)
    for level in range(2, data_bits):
        feed = lanes_join(feed, swap(feed, (1 << level, 0)), level, data_index)
    backs, small, feed = tie(stage_swap(mixed, THIRDS, 0), small, feed)
    for _ in range(steps - 1):
        small = chain.send(small)
    mixed = grow(mixed, backs)
    up, down = feed[0], feed[1]
    for bits in early[:-1]:
        up, down = early_join(up, bits), early_join(down, bits)

    starts = jnp.cumsum(lengths) - lengths
    half_rows = (model_index * 2 + jnp.arange(-1, 3, dtype=jnp.int32)) * HALF
    inside = (half_rows[:, None] >= starts[None]) & (half_rows[:, None] < (starts + lengths)[None])
    seated = jnp.any(inside, axis=1)
    is_first = jnp.any(inside & (half_rows[:, None] == starts[None]), axis=1)
    paired = jnp.any(inside & (lengths[None] == 2 * HALF), axis=1)
    own_index = jnp.arange(4, dtype=jnp.int32)
    partner = jnp.where(is_first, own_index + 1, own_index - 1)
    facts = jnp.stack([partner, paired.astype(jnp.int32), seated.astype(jnp.int32)], 1)[1:3]
    facts = facts.reshape(6).astype(jnp.int32)
    table = inside.astype(f32)
    number = jnp.sum(jnp.where(inside, jnp.arange(images, dtype=jnp.int32)[None], 0), axis=1)
    number = jnp.where(seated, number, -1)

    backs, table, facts, number, small, up, down = tie(
        stage_swap(mixed, THIRDS, 1), table, facts, number, small, up, down
    )
    mixed, mixed_both = grow_both(mixed, backs, 1)
    backs = stage_swap(mixed, THIRDS, 2)
    cond_act, buf = chain.send(small)
    up_back = swap(up, early[-1])

    shifts = jnp.array(join_masks(model_bits), jnp.int32) ^ model_index
    flip = (shifts[None] == jnp.arange(model_ways, dtype=jnp.int32)[:, None]).astype(f32)
    (vectors,) = call(
        lambda *refs: vectors_kernel(head_cols, *refs),
        [like(24, width, f32)],
        (number, shifts, buf),
        "modulation_vectors",
        scratch=[pltpu.VMEM((24, width), f32)],
        smem=2,
    )
    bias_rel = buf[:, -1, : 6 * head_cols]
    bias_q, bias_v = (bias_rel[:, k * head_cols : (k + 1) * head_cols].reshape(1, -1) for k in range(2))
    step, places = feed_places(feed_count, model_bits)
    place = jnp.where((data_index & 1) == 0, places[0], places[1])
    granules = all_hidden // step
    source = (place[:, 0] * 4 + (place[:, 1] ^ (data_index & 3))) * (feed_count // step) + place[:, 2]
    source = one_hot_rows(source, granules)
    bias_up = jnp.dot(source, bias_rel[:, 2 * head_cols :].reshape(granules, step), precision=highest)
    bias_up = bias_up.reshape(1, all_hidden)
    (grad_mlp,) = call(gate_kernel, [like(local_rows, width)], (cotangent, vectors), "grad_mlp")
    (span_input,) = call(
        span_kernel, [like(2 * local_rows, width)], (before, tokens, after, vectors), "attention_input"
    )
    b_out, b_down = b_out.astype(f32).reshape(1, width), b_down.astype(f32).reshape(1, width)
    own = slice(HALF, HALF + local_rows)
    near = swap(mixed_both, CORE)
    backs, up_back, near, span_input, bias_up, bias_q, bias_v, grad_mlp, b_out, b_down, vectors, source = tie(
        backs, up_back, near, span_input, bias_up, bias_q, bias_v, grad_mlp, b_out, b_down, vectors, source
    )
    cut = up.shape[0] * 4 // 3
    outs = [like(cut, width), like(cut // 2, width)]
    up = call(join_kernel, outs, (up, up_back), "join")
    up_backs = stage_swap(up, FEED, 0)
    far = core_swap(backs)
    up_backs, far, down = tie(up_backs, far, down)
    attn_input = span_input[own]

    up = grow(up, up_backs)
    up_backs = stage_swap(up, FEED, 1)
    down_back = swap(down, early[-1])
    wq, wk, wv, wo = assemble(spot, (mixed_both, *backs, near, *far), width)
    query, key, value = call(
        qkv_kernel,
        [like(2 * local_rows, width)] * 3,
        (span_input, wq, wk, wv, bias_q, bias_v),
        "query_key_value",
    )
    up_backs, down_back, query, key, value = tie(up_backs, down_back, query, key, value)
    up, up_both = grow_both(up, up_backs, 0)
    up_backs = stage_swap(up, FEED, 2)
    down = call(join_kernel, outs, (down, down_back), "join")
    down_backs = stage_swap(down, FEED, 0)
    up_near = swap(up_both, CORE)
    attended, branch, residual, mlp_input = call(
        attend_forward,
        [like(local_rows, width), like(local_rows, width, f32), like(local_rows, width, f32), like(local_rows, width)],
        (facts, query, key, value, wo, b_out, tokens, vectors),
        "attention_forward",
        scratch=[pltpu.VMEM((2 * HALF, width), bf16)] * 2,
        smem=1,
    )

    up_backs, up_near, down_backs, mlp_input = tie(up_backs, up_near, down_backs, mlp_input)
    up_far = core_swap(up_backs)
    down = grow(down, down_backs)
    down_backs = stage_swap(down, FEED, 1)
    up_far, down_backs, mlp_input = tie(up_far, down_backs, mlp_input)
    ups = up_both, *up_backs, up_near, *up_far
    act, slope = call(up_kernel, [like(local_rows, all_hidden)] * 2, (mlp_input, bias_up, *ups), "up")
    down, down_both = grow_both(down, down_backs, 0)
    down_backs = stage_swap(down, FEED, 2)
    down_near = swap(down_both, CORE)
    down_backs, down_near, act = tie(down_backs, down_near, act)
    down_far = core_swap(down_backs)
    other = all_hidden // 2
    sizes = (up[0].shape[0], up[1].shape[0]) * 2
    sum_down = products(act, grad_mlp, other, (other,))
    down_far, sum_down = tie(down_far, sum_down)
    sum_down = core_swap(sum_down)
    downs = down_both, *down_backs, down_near, *down_far
    grad_pre, grad_bias, output, output_sums = call(
        down_kernel,
        [like(local_rows, all_hidden), like(1, all_hidden, f32), like(local_rows, width), like(8, width, f32)],
        (grad_mlp, slope, act, residual, cotangent, vectors, b_down, *downs),
        "down",
        scratch=[pltpu.VMEM((local_rows, width), f32)],
    )
    (grad_mlp_input,) = call(back_kernel, [like(local_rows, width, f32)], (grad_pre, *ups), "grad_mlp_input")
    grad_residual, grad_branch, grad_attended, middle_sums = call(
        middle_kernel,
        [like(local_rows, width, f32), like(local_rows, width), like(local_rows, width), like(8, width, f32)],
        (grad_mlp_input, residual, branch, cotangent, vectors, wo),
        "grad_attended",
    )
    sum_up = products(grad_pre, mlp_input, other, (other,))
    sum_down, sum_up, grad_attended, grad_branch, grad_pre = tie(
        sum_down, sum_up, grad_attended, grad_branch, grad_pre
    )
    sum_up = core_swap(sum_up)
    from_after = lax.ppermute(grad_branch[:HALF], "mp", back_to)
    from_before = lax.ppermute(grad_branch[HALF:], "mp", forth)

    full, half_full = pltpu.VMEM((2 * HALF, width), f32), pltpu.VMEM((2 * HALF, width), bf16)

    def attention_back(half, *operands):
        return call(
            lambda *refs: attend_backward(half, *refs),
            [like(local_rows, width), like(local_rows, width, f32), like(local_rows, width, f32)],
            (facts, query, key, value, grad_attended, *operands),
            "attention_backward",
            scratch=[half_full, half_full, full, full],
            smem=1,
        )

    first_half = attention_back(0)
    sum_down = products(act, grad_mlp, 0, sizes, sum_down)
    down_keeps, down_sends = sum_down[:2], sum_down[2:]
    grad_query, own_key, own_value = attention_back(1, *first_half)
    sum_up, from_after, from_before, grad_query, down_sends = tie(
        sum_up, from_after, from_before, grad_query, down_sends
    )
    down_backs = stage_swap(down_sends, FEED, 2)
    sum_up = products(grad_pre, mlp_input, 0, sizes, sum_up)
    up_keeps, up_sends = sum_up[:2], sum_up[2:]
    grad_key, grad_value = call(
        attend_outside,
        [like(local_rows, width)] * 2,
        (facts, query, key, value, from_before, from_after, wo, own_key, own_value),
        "attention_outside",
        scratch=[half_full, half_full, pltpu.VMEM((HALF, width), bf16), full, full],
        smem=1,
    )
    down_backs, up_sends, grad_key, grad_value = tie(down_backs, up_sends, grad_key, grad_value)
    up_backs = stage_swap(up_sends, FEED, 2)
    lefts, rights = (grad_query, grad_key, grad_value, attended), (attn_input, grad_branch)
    sum_mixed = kind_products(1, spot, lefts, rights)
    flat_up = lax.dot_general(
        source, grad_bias.reshape(granules, step), (((0,), (0,)), ((), ())), precision=highest
    ).reshape(model_ways, hidden)
    up_backs, sum_mixed, flat_up = tie(up_backs, sum_mixed, flat_up)
    sum_mixed = core_swap(sum_mixed)
    feed_keeps, feed_sends = halve_join((*up_keeps, *down_keeps), (*up_backs, *down_backs))
    feed_backs = stage_swap(feed_sends, FEED, 1)
    grad_tokens, last_sums = call(
        last_kernel,
        [like(local_rows, width, f32), like(8, width, f32)],
        (grad_query, grad_key, grad_value, wq, wk, wv, tokens, vectors, grad_residual),
        "grad_tokens",
    )
    sum_mixed = kind_products(0, spot, lefts, rights, sum_mixed)
    mixed_keeps, mixed_sends = sum_mixed[0::2], sum_mixed[1::2]
    mixed_sends, last_sums, feed_backs = tie(mixed_sends, last_sums, feed_backs)
    mixed_backs = stage_swap(mixed_sends, THIRDS, 2)
    feed_keeps, feed_sends = halve(feed_keeps, feed_backs, 2)
    feed_backs = stage_swap(feed_sends, FEED, 0)

    packed, plain = call(
        lambda *refs: pack_kernel(head_cols, *refs),
        [jax.ShapeDtypeStruct((model_ways, small_rows, small_lanes), f32), jax.ShapeDtypeStruct((1, 8, small_lanes), f32)],
        (number, shifts, last_sums, middle_sums, output_sums, flat_up),
        "pack_sums",
        scratch=[pltpu.VMEM((16, width), f32)],
        smem=2,
    )
    plain = jnp.pad(plain, ((0, 0), (0, small_rows - 8), (0, 0)))

    def gather_sums():
        buf, rest = packed.reshape((2,) * model_bits + (small_rows, small_lanes)), plain
        for bit in (0, 1, *range(2, model_bits)):
            axis = model_bits - 1 - joins.index(bit)
            keep, send = (lax.slice_in_dim(buf, k, k + 1, axis=axis) for k in (0, 1))
            send = jnp.concatenate([send.reshape(-1, small_rows, small_lanes), rest], 0)
            back = yield swap(send, (0, 1 << bit))
            buf, rest = keep + back[:-1].reshape(keep.shape), rest + back[-1:]
        buf = buf.reshape(small_rows, small_lanes)
        mods, rest = buf[:images].astype(bf16), jnp.concatenate([rest[0, :8], buf[-8:]], 0)
        mods = mods.reshape((1,) * data_bits + mods.shape)
        for level in reversed(range(data_bits)):
            backs = yield swap(mods, (1 << level, 0)), swap(rest, (1 << level, 0))
            mods, rest = jnp.concatenate([mods, backs[0]], data_bits - 1 - level), rest + backs[1]
        yield mods[..., : 6 * head_cols], rest

    mixed_backs, feed_backs, packed, plain = tie(mixed_backs, feed_backs, packed, plain)
    chain = gather_sums()
    steps = model_bits + data_bits
    small = next(chain)
    mixed_keeps, mixed_sends = halve(mixed_keeps, mixed_backs)
    mixed_backs = stage_swap(mixed_sends, THIRDS, 1)
    merged_rows = feed_count << len(early) - 1
    feed_keep, feed_send = merge(merge_rows_kernel, feed_keeps, feed_backs, merged_rows, 2 * width)
    feed_back = swap(feed_send, early[-1])
    mixed_backs, small = tie(mixed_backs, small)
    small = chain.send(small)
    steps -= 1
    mixed_keeps, mixed_sends = halve(mixed_keeps, mixed_backs)
    mixed_backs = stage_swap(mixed_sends, THIRDS, 0)
    feed_done = added(feed_keep, feed_back)
    for bits in reversed(early[:-1]):
        keep, send = halves(feed_done)
        feed_done = added(keep, swap(send, bits))
    feed_done = jnp.stack([feed_done[:, :width], feed_done[:, width:]], 0)
    for level in reversed(range(2, data_bits)):
        feed_done = lanes_sum(feed_done, level, data_index)
    mixed_backs, feed_done, small = tie(mixed_backs, feed_done, small)
    small = chain.send(small)
    steps -= 1
    merged_rows = head_cols << len(early) - 1
    mixed_keep, mixed_send = merge(merge_lanes_kernel, mixed_keeps, mixed_backs, merged_rows, width)
    mixed_back = swap(mixed_send, early[-1])
    feed_keep, feed_back = lanes_send(feed_done, 1, data_index)
    mixed_back, feed_back, small = tie(mixed_back, feed_back, small)
    small = chain.send(small)
    steps -= 1
    mixed_done = added(mixed_keep, mixed_back)
    for bits in reversed(early[:-1]):
        keep, send = halves(mixed_done)
        mixed_done = added(keep, swap(send, bits))
    for level in reversed(range(2, data_bits)):
        mixed_done = lanes_sum(mixed_done, level, data_index)
    keep, back = lanes_send(mixed_done, 1, data_index)
    feed_done = rows_join(feed_keep, feed_back, 1, data_index, 0)
    feed_keep, feed_back = lanes_send(feed_done, 0, data_index)
    back, feed_back, small = tie(back, feed_back, small)
    small = chain.send(small)
    steps -= 1
    mixed_done = rows_join(keep, back, 1, data_index, 0)
    keep, back = lanes_send(mixed_done, 0, data_index)
    feed_done = rows_join(feed_keep, feed_back, 0, data_index, 1).reshape(4, 2, feed_count, lanes)
    for _ in range(steps):
        small = chain.send(small)
    mixed_done = rows_join(keep, back, 0, data_index, 1).reshape(4, head_cols, lanes)
    grad_modulation, rest = small
    grad_w_ada = tn(
        cond_act.reshape(data_ways * images, lanes),
        grad_modulation.reshape(data_ways * images, 6 * head_cols),
    )
    grad_w_ada = grad_w_ada.reshape(lanes, 6, head_cols)
    grad_b_ada = jnp.sum(grad_modulation.reshape(-1, 6 * head_cols), axis=0, dtype=f32).reshape(6, head_cols)
    per = -(-width // small_lanes)
    grad_b_out, grad_b_down = (rest[k * per : (k + 1) * per].reshape(-1)[:width] for k in range(2))
    own_bias = rest[-1, : 6 * head_cols]
    grad_b_qv, grad_b_up = own_bias[: 2 * head_cols].reshape(2, head_cols), own_bias[2 * head_cols :]

    grad_w_up, grad_w_down = call(
        place_feed_kernel, [like(lanes, hidden, f32)] * 2, (feed_done,), "place_feed_forward"
    )
    grad_w_down = jnp.swapaxes(grad_w_down, 0, 1)
    mixed_done = mixed_done.astype(f32)
    grad_w_qkv, grad_w_out = jnp.swapaxes(mixed_done[:3], 1, 2), mixed_done[3]
    return (
        output,
        grad_tokens,
        grad_w_ada,
        grad_b_ada,
        grad_w_qkv,
        grad_b_qv,
        grad_w_out,
        grad_b_out,
        grad_w_up,
        grad_b_up,
        grad_w_down,
        grad_b_down,
    )


def solution(mesh):
    in_specs = (
        P(("dp", "mp"), None),
        P("dp", None),
        P("dp"),
        P("dp", None, "mp"),
        P(None, "mp"),
        P(None, "dp", "mp"),
        P(None, "mp"),
        P("mp", "dp"),
        P(),
        P("dp", "mp"),
        P("mp"),
        P("mp", "dp"),
        P(),
        P(("dp", "mp"), None),
    )
    out_specs = (
        P(("dp", "mp"), None),
        P(("dp", "mp"), None),
        P("dp", None, "mp"),
        P(None, "mp"),
        P(None, "dp", "mp"),
        P(None, "mp"),
        P("mp", "dp"),
        P(),
        P("dp", "mp"),
        P("mp"),
        P("mp", "dp"),
        P(),
    )
    return jax.shard_map(
        on_device, mesh=mesh, in_specs=in_specs, out_specs=out_specs, check_vma=False
    )
```

```python
import itertools
import math

import jax
import jax.numpy as jnp
import numpy as np
from jax import lax
from jax.experimental import pallas as pl
from jax.experimental.pallas import tpu as pltpu
from jax.sharding import PartitionSpec as P

HD = 72
HALF = 128
LANE = 128
EPS = 1e-06
HIDE = -1e30

f32, bf16 = jnp.float32, jnp.bfloat16
highest = lax.Precision.HIGHEST

CORE, Y, X, Z1 = (1, 0), (2, 0), (0, 1), (0, 2)


def swap(values, even, odd=None):
    odd = even if odd is None else odd
    data_ways, model_ways = lax.axis_size("dp"), lax.axis_size("mp")
    pairs = []
    for d in range(data_ways):
        d_bits, m_bits = odd if d % 2 else even
        for m in range(model_ways):
            pairs.append((d * model_ways + m, (d ^ d_bits) * model_ways + (m ^ m_bits)))
    return lax.ppermute(values, ("dp", "mp"), pairs)


def bits_of(count):
    return count.bit_length() - 1


def pick(values, axis, index):
    low, high = (lax.index_in_dim(values, k, axis, keepdims=False) for k in (0, 1))
    return jnp.where(index == 0, low, high)


def nn(a, b):
    return jnp.dot(a, b, preferred_element_type=f32)


def nt(a, b):
    return lax.dot_general(a, b, (((1,), (1,)), ((), ())), preferred_element_type=f32)


def tn(a, b):
    return lax.dot_general(a, b, (((0,), (0,)), ((), ())), preferred_element_type=f32)


def head_windows(width):
    for head in range(width // HD):
        first, last = head * HD, head * HD + HD
        low = first // LANE * LANE
        high = -(-last // LANE) * LANE
        yield first, last, low, high


def lane_mask(first, last, low, high):
    lane = lax.broadcasted_iota(jnp.int32, (HALF, high - low), 1) + low
    return (lane >= first) & (lane < last)


def same_segment(paired, seated):
    row = lax.broadcasted_iota(jnp.int32, (HALF, 2 * HALF), 0)
    col = lax.broadcasted_iota(jnp.int32, (HALF, 2 * HALF), 1)
    own = (col < HALF) & ((row == col) | (seated > 0))
    return own | ((col >= HALF) & (paired > 0))


def same_segment_keys(paired, seated):
    key = lax.broadcasted_iota(jnp.int32, (2 * HALF, HALF), 0)
    col = lax.broadcasted_iota(jnp.int32, (2 * HALF, HALF), 1)
    own = (key < HALF) & ((key == col) | (seated > 0))
    return own | ((key >= HALF) & (paired > 0))


def split_rows(rows):
    return pl.ds(rows * HALF, HALF)


def row(vectors, kind, half):
    return vectors[4 * kind + half : 4 * kind + half + 1]


def normalize(values):
    centred = values - jnp.mean(values, axis=-1, keepdims=True)
    spread = jnp.mean(centred * centred, axis=-1, keepdims=True)
    root = lax.rsqrt(spread + EPS)
    return centred * root, root


def normalize_back(norm, root, upstream):
    return (
        upstream
        - jnp.mean(upstream, axis=-1, keepdims=True)
        - norm * jnp.mean(upstream * norm, axis=-1, keepdims=True)
    ) * root


def column_sum(values):
    return jnp.sum(values, axis=0, keepdims=True)


def vectors_kernel(columns, images, shifts, buf, out, part):
    part[...] = jnp.zeros(part.shape, f32)
    for block in range(buf.shape[0]):
        for half in range(4):
            number = lax.broadcasted_iota(jnp.int32, buf.shape[1:], 0)
            vector = column_sum(jnp.where(number == images[half], buf[block], 0.0))
            for kind in range(6):
                part[4 * kind + half : 4 * kind + half + 1, :columns] = vector[:, kind * columns : (kind + 1) * columns]
        moved = pltpu.roll(part[...], shifts[block] * columns, 1)
        out[...] = moved if block == 0 else out[...] + moved


def pack_kernel(columns, images, shifts, last, middle, output, bias_up, out, plain, rows):
    count, _, lanes = out.shape
    bias_row = out.shape[1] - 1
    width = rows.shape[1]
    rows[...] = jnp.zeros(rows.shape, f32)
    rows[0:4], rows[4:10], rows[10:12] = last[0:4], middle[0:6], output[0:2]
    out[...] = jnp.zeros(out.shape, f32)
    plain[...] = jnp.zeros(plain.shape, f32)
    for block in range(count):
        moved = pltpu.roll(rows[...], jnp.where(shifts[block] > 0, width - shifts[block] * columns, 0), 1)
        number = lax.broadcasted_iota(jnp.int32, (out.shape[1], columns), 0)
        for kind in range(6):
            place = slice(kind * columns, (kind + 1) * columns)
            low, high = (moved[2 * kind + half : 2 * kind + half + 1, :columns] for half in range(2))
            out[block, :, place] = jnp.where(number == images[1], low, 0.0) + jnp.where(number == images[2], high, 0.0)
        mine = slice(block * columns, (block + 1) * columns)
        out[block, bias_row : bias_row + 1, :columns] = last[4:5, mine]
        out[block, bias_row : bias_row + 1, columns : 2 * columns] = last[5:6, mine]
        out[block, bias_row : bias_row + 1, 2 * columns : 6 * columns] = bias_up[block : block + 1]
    per = -(-width // lanes)
    for k, source in enumerate((middle[6:7], output[2:3])):
        for piece in range(per):
            size = min(lanes, width - piece * lanes)
            plain[0, k * per + piece : k * per + piece + 1, :size] = source[:, piece * lanes : piece * lanes + size]


def span_kernel(before, tokens, after, vectors, out):
    for half in range(4):
        source = (before, tokens, tokens, after)[half]
        norm, _ = normalize(source[split_rows(half == 2)].astype(f32))
        out[split_rows(half)] = (norm * (1.0 + row(vectors, 1, half)) + row(vectors, 0, half)).astype(bf16)


def qkv_kernel(span, wq, wk, wv, bias_q, bias_v, query, key, value):
    query[...] = (nt(span[...], wq[...]) + bias_q[...]).astype(bf16)
    key[...] = nt(span[...], wk[...]).astype(bf16)
    value[...] = (nt(span[...], wv[...]) + bias_v[...]).astype(bf16)


def attend_forward(
    facts, q_ref, k_ref, v_ref, wo, b_out, tokens, vectors, o_ref, branch_ref, residual_ref, input_ref, kk, vv
):
    factor = HD ** (-0.5)
    for half in range(2):
        rows = split_rows(half)
        own = split_rows(half + 1)
        other = pl.ds(pl.multiple_of(facts[3 * half] * HALF, HALF), HALF)
        kk[0:HALF], kk[HALF:] = k_ref[own], k_ref[other]
        vv[0:HALF], vv[HALF:] = v_ref[own], v_ref[other]
        same = same_segment(facts[3 * half + 1], facts[3 * half + 2])
        for first, last, low, high in head_windows(q_ref.shape[1]):
            window = slice(low, high)
            mask = lane_mask(first, last, low, high)
            query = jnp.where(mask, q_ref[own, window], 0)
            scores = jnp.where(same, nt(query, kk[:, window]) * factor, HIDE)
            exp_scores = jnp.exp(scores - jnp.max(scores, axis=1, keepdims=True))
            prob = exp_scores / jnp.sum(exp_scores, axis=1, keepdims=True)
            mixed = nn(prob.astype(bf16), vv[:, window]).astype(bf16)
            o_ref[rows, window] = jnp.where(mask, mixed, o_ref[rows, window]) if first > low else mixed
    for half in range(2):
        rows = split_rows(half)
        branch = nn(o_ref[rows], wo[...]) + b_out[...]
        branch_ref[rows] = branch
        residual = tokens[rows].astype(f32) + row(vectors, 2, half + 1) * branch
        residual_ref[rows] = residual
        norm, _ = normalize(residual)
        input_ref[rows] = (norm * (1.0 + row(vectors, 4, half + 1)) + row(vectors, 3, half + 1)).astype(bf16)


def score_gradients(query, grad, keys, values, same):
    scores = nt(keys, query) * HD ** (-0.5)
    if same is not None:
        scores = jnp.where(same, scores, HIDE)
    exp_scores = jnp.exp(scores - jnp.max(scores, axis=0, keepdims=True))
    prob = exp_scores / jnp.sum(exp_scores, axis=0, keepdims=True)
    grad_prob = nt(values, grad)
    inner = jnp.sum(grad_prob * prob, axis=0, keepdims=True)
    return prob.astype(bf16), (prob * (grad_prob - inner)).astype(bf16)


def attend_backward(half, facts, q_ref, k_ref, v_ref, g_ref, *refs):
    earlier, refs = (refs[:3], refs[3:]) if half else (None, refs)
    dq_ref, own_k, own_v, kk, vv, dkk, dvv = refs
    factor = HD ** (-0.5)
    rows = split_rows(half)
    own = split_rows(half + 1)
    other = pl.ds(pl.multiple_of(facts[3 * half] * HALF, HALF), HALF)
    kk[0:HALF], kk[HALF:] = k_ref[own], k_ref[other]
    vv[0:HALF], vv[HALF:] = v_ref[own], v_ref[other]
    dkk[...] = jnp.zeros(dkk.shape, f32)
    dvv[...] = jnp.zeros(dvv.shape, f32)
    if half:
        dq_ref[0:HALF] = earlier[0][0:HALF]
    same = same_segment_keys(facts[3 * half + 1], facts[3 * half + 2])
    for first, last, low, high in head_windows(q_ref.shape[1]):
        window = slice(low, high)
        mask = lane_mask(first, last, low, high)
        query = jnp.where(mask, q_ref[own, window], 0)
        grad = jnp.where(mask, g_ref[rows, window], 0)
        prob, grad_scores = score_gradients(query, grad, kk[:, window], vv[:, window], same)
        dq = (tn(grad_scores, kk[:, window]) * factor).astype(bf16)
        dq_ref[rows, window] = jnp.where(mask, dq, dq_ref[rows, window]) if first > low else dq
        dkk[:, window] += nn(grad_scores, query) * factor
        dvv[:, window] += nn(prob, grad)
    inside = jnp.where(facts[3 * half] == 2 - half, 1.0, 0.0)
    for place, (total, mine) in enumerate(((dkk, own_k), (dvv, own_v))):
        mine_own, mine_other = total[0:HALF], total[HALF:] * inside
        if half:
            mine_own = mine_own + earlier[1 + place][split_rows(half)]
            mine_other = mine_other + earlier[1 + place][split_rows(1 - half)]
        mine[split_rows(half)], mine[split_rows(1 - half)] = mine_own, mine_other


def attend_outside(
    facts, q_ref, k_ref, v_ref, before, after, wo, own_k, own_v, key_ref, value_ref, kk, vv, grads, dk, dv
):
    factor = HD ** (-0.5)
    dk[...], dv[...] = own_k[...], own_v[...]
    for half, (outside, branch) in enumerate(((0, before), (3, after))):

        @pl.when((facts[3 * half] == outside) & (facts[3 * half + 1] > 0))
        def _():
            mine, theirs = split_rows(half), split_rows(outside)
            kk[0:HALF], kk[HALF:] = k_ref[theirs], k_ref[split_rows(half + 1)]
            vv[0:HALF], vv[HALF:] = v_ref[theirs], v_ref[split_rows(half + 1)]
            grads[...] = nt(branch[...], wo[...]).astype(bf16)
            for first, last, low, high in head_windows(q_ref.shape[1]):
                window = slice(low, high)
                mask = lane_mask(first, last, low, high)
                query = jnp.where(mask, q_ref[theirs, window], 0)
                grad = jnp.where(mask, grads[:, window], 0)
                prob, grad_scores = score_gradients(query, grad, kk[:, window], vv[:, window], None)
                dk[mine, window] += nn(grad_scores[HALF:], query) * factor
                dv[mine, window] += nn(prob[HALF:], grad)

    key_ref[...], value_ref[...] = dk[...].astype(bf16), dv[...].astype(bf16)


def middle_kernel(
    grad_input, residual, branch, cotangent, vectors, wo, grad_residual, grad_branch, grad_attended, sums
):
    sums[...] = jnp.zeros(sums.shape, f32)
    for half in range(2):
        rows = split_rows(half)
        norm, root = normalize(residual[rows])
        grad = grad_input[rows]
        total = cotangent[rows].astype(f32) + normalize_back(norm, root, grad * (1.0 + row(vectors, 4, half + 1)))
        grad_residual[rows] = total
        low = (row(vectors, 2, half + 1) * total).astype(bf16)
        grad_branch[rows] = low
        grad_attended[rows] = nt(low, wo[...]).astype(bf16)
        sums[half : half + 1] = column_sum(total * branch[rows])
        sums[2 + half : 3 + half] = column_sum(grad)
        sums[4 + half : 5 + half] = column_sum(grad * norm)
        sums[6:7] += column_sum(low.astype(f32))


def last_kernel(
    grad_query, grad_key, grad_value, wq, wk, wv, tokens, vectors, grad_residual, grad_tokens, sums
):
    sums[...] = jnp.zeros(sums.shape, f32)
    for half in range(2):
        rows = split_rows(half)
        norm, root = normalize(tokens[rows].astype(f32))
        grad = nn(grad_query[rows], wq[...]) + nn(grad_key[rows], wk[...]) + nn(grad_value[rows], wv[...])
        back = normalize_back(norm, root, grad * (1.0 + row(vectors, 1, half + 1)))
        grad_tokens[rows] = grad_residual[rows] + back
        sums[half : half + 1] = column_sum(grad)
        sums[2 + half : 3 + half] = column_sum(grad * norm)
        sums[4:5] += column_sum(grad_query[rows].astype(f32))
        sums[5:6] += column_sum(grad_value[rows].astype(f32))


VMEM = pl.BlockSpec(memory_space=pltpu.VMEM)
SMEM = pl.BlockSpec(memory_space=pltpu.SMEM)


CHUNK = 96
HINT = pl.CostEstimate(flops=1, bytes_accessed=1, transcendentals=0)


def call(kernel, outs, operands, name, scratch=(), smem=0):
    room = sum(math.prod(v.shape) * v.dtype.itemsize for v in (*scratch, *outs) if hasattr(v, "shape")) + 4 * 2**20
    return pl.pallas_call(
        kernel,
        out_shape=tuple(outs),
        in_specs=[SMEM] * smem + [VMEM] * (len(operands) - smem),
        out_specs=tuple(VMEM for _ in outs),
        scratch_shapes=list(scratch),
        compiler_params=pltpu.CompilerParams(vmem_limit_bytes=room),
        cost_estimate=HINT,
        name=name,
    )(*operands)


def like(rows, width, dtype=bf16):
    return jax.ShapeDtypeStruct((rows, width), dtype)


def grow_kernel(refs, axis=None):
    count = (len(refs) - (axis is not None)) // 3
    both, place = refs[-1], 0
    for own, back, out in zip(refs[:count], refs[count : 2 * count], refs[2 * count : 3 * count]):
        rows, lanes = own.shape
        out[:rows], out[rows:] = own[...], back[...]
        if axis == 0:
            both[place : place + rows], both[place + rows : place + 2 * rows] = own[...], back[...]
            place += 2 * rows
        if axis == 1:
            both[:rows, place : place + lanes], both[rows:, place : place + lanes] = own[...], back[...]
            place += lanes


def grow(parts, backs):
    outs = [like(2 * part.shape[0], part.shape[1]) for part in parts]
    return call(lambda *refs: grow_kernel(refs), outs, (*parts, *backs), "grow")


def grow_both(parts, backs, axis):
    outs = [like(2 * part.shape[0], part.shape[1]) for part in parts]
    if axis == 0:
        both = like(sum(out.shape[0] for out in outs), outs[0].shape[1])
    else:
        both = like(outs[0].shape[0], sum(out.shape[1] for out in outs))
    outs = call(lambda *refs: grow_kernel(refs, axis), [*outs, both], (*parts, *backs), "grow_both")
    return outs[:-1], outs[-1]


def row_sum(keep, back, first, last):
    return keep[first:last] + back[first:last]


def halve_kernel(groups, side, *refs):
    count = len(refs) // 3
    for keep, back, out in zip(refs[:count], refs[count : 2 * count], refs[2 * count :]):
        rows = keep.shape[0] // (2 * groups)
        for group in range(groups):
            base = (2 * group + side) * rows
            for first in range(0, rows, CHUNK):
                last = min(first + CHUNK, rows)
                out[group * rows + first : group * rows + last] = row_sum(keep, back, base + first, base + last)


def halve(keeps, backs, groups=1):
    outs = [like(keep.shape[0] // 2, keep.shape[1]) for keep in keeps]
    high, low = (
        call(lambda *refs, side=side: halve_kernel(groups, side, *refs), outs, (*keeps, *backs), "halve")
        for side in (1, 0)
    )
    return low, high


def halve_join_kernel(side, *refs):
    count = len(refs) // 5
    keeps, backs, outs = refs[: 2 * count], refs[2 * count : 4 * count], refs[4 * count :]
    for k in range(count):
        for which in range(2):
            keep, back = keeps[which * count + k], backs[which * count + k]
            rows = keep.shape[0] // 2
            for first in range(0, rows, CHUNK):
                last = min(first + CHUNK, rows)
                outs[k][which * rows + first : which * rows + last] = row_sum(
                    keep, back, side * rows + first, side * rows + last
                )


def halve_join(keeps, backs):
    outs = [like(keep.shape[0], keep.shape[1]) for keep in keeps[: len(keeps) // 2]]
    high, low = (
        call(lambda *refs, side=side: halve_join_kernel(side, *refs), outs, (*keeps, *backs), "halve_join")
        for side in (1, 0)
    )
    return low, high


def merge_rows_kernel(*refs):
    count = (len(refs) - 2) // 2
    low, high = refs[2 * count :]
    rows, width = low.shape[0], low.shape[1] // 2
    for which in range(2):
        lanes = slice(which * width, (which + 1) * width)
        place = 0
        for keep, back in zip(refs[:count], refs[count : 2 * count]):
            first, end = which * keep.shape[0] // 2, (which + 1) * keep.shape[0] // 2
            while first < end:
                out, base = (low, 0) if place < rows else (high, rows)
                step = min(end - first, base + rows - place)
                out[place - base : place - base + step, lanes] = row_sum(keep, back, first, first + step)
                first, place = first + step, place + step


def merge_lanes_kernel(*refs):
    count = (len(refs) - 2) // 2
    low, high = refs[2 * count :]
    rows, lane = low.shape[0], 0
    for keep, back in zip(refs[:count], refs[count : 2 * count]):
        lanes = slice(lane, lane + keep.shape[1])
        lane += keep.shape[1]
        low[:, lanes], high[:, lanes] = row_sum(keep, back, 0, rows), row_sum(keep, back, rows, 2 * rows)


def merge(kernel, keeps, backs, rows, width):
    return call(kernel, [like(rows, width)] * 2, (*keeps, *backs), "merge")


def row_steps(weights):
    unit = 0
    for weight in weights:
        rows = weight.shape[0]
        step = 256 if rows % 256 == 0 else 384
        for first in range(0, rows, step):
            yield weight, first, first + step, unit + first
        unit += rows


def up_kernel(x_ref, bias_ref, *refs):
    weights, (act_ref, slope_ref) = refs[:-2], refs[-2:]
    for weight, first, last, unit in row_steps(weights):
        units = slice(unit, unit + last - first)
        pre = nt(x_ref[...], weight[first:last]) + bias_ref[:, units]
        square = pre * pre
        inner = jnp.tanh(0.7978845608028654 * pre * (1.0 + 0.044715 * square))
        outer = 0.5 * (1.0 + inner)
        act_ref[:, units] = (pre * outer).astype(bf16)
        rise = (0.5 * 0.7978845608028654) * pre * (1.0 + (3 * 0.044715) * square)
        slope_ref[:, units] = (outer + rise * (1.0 - inner * inner)).astype(bf16)


def down_kernel(grad_mlp, slope, act, residual, cotangent, vectors, b_down, *refs):
    weights, (pre_ref, sum_ref, out, sums, total) = refs[:-5], refs[-5:]
    for weight, first, last, unit in row_steps(weights):
        units = slice(unit, unit + last - first)
        pre = (nt(grad_mlp[...], weight[first:last]) * slope[:, units].astype(f32)).astype(bf16)
        pre_ref[:, units] = pre
        sum_ref[:, units] = column_sum(pre.astype(f32))
    back_kernel(act, *weights, total)
    sums[...] = jnp.zeros(sums.shape, f32)
    for half in range(2):
        rows = split_rows(half)
        mlp = total[rows] + b_down[...]
        out[rows] = (residual[rows] + row(vectors, 5, half + 1) * mlp).astype(bf16)
        sums[half : half + 1] = column_sum(cotangent[rows].astype(f32) * mlp)
        sums[2:3] += column_sum(grad_mlp[rows].astype(f32))


def back_kernel(left_ref, *refs):
    weights, out_ref = refs[:-1], refs[-1]
    unit = 0
    for weight in weights:
        rows = weight.shape[0]
        part = nn(left_ref[:, unit : unit + rows], weight[...])
        out_ref[...] = part if unit == 0 else out_ref[...] + part
        unit += rows


def join_kernel(own, back, wide, narrow):
    rows = own.shape[0]
    more = wide.shape[0] - rows
    wide[:rows], wide[rows:] = own[...], back[:more]
    narrow[...] = back[more:]


def place_feed_kernel(done, grad_up, grad_down):
    for which, out in enumerate((grad_up, grad_down)):
        out[...] = jnp.concatenate([done[way, which] for way in range(done.shape[0])], 0).astype(f32).T


def gate_kernel(cotangent, vectors, out):
    for half in range(2):
        rows = split_rows(half)
        out[rows] = (row(vectors, 5, half + 1) * cotangent[rows].astype(f32)).astype(bf16)


def product_kernel(start, left_ref, right_ref, *refs):
    back, outs = (refs[0], refs[1:]) if len(refs) > 1 and refs[0].shape != refs[-1].shape else (None, refs)
    base = 0
    for out in outs:
        size = out.shape[0]
        step = 256 if size % 256 == 0 else 384
        for first in range(0, size, step):
            column = start + base + first
            part = tn(left_ref[:, column : column + step], right_ref[...])
            if back is not None:
                part = part + back[base + first : base + first + step].astype(f32)
            out[first : first + step] = part.astype(bf16)
        base += size


def products(left, right, start, counts, backs=()):
    outs = [like(size, right.shape[1]) for size in counts]
    return call(lambda *refs: product_kernel(start, *refs), outs, (left, right, *backs), "products")


def unit_of(third, y, z, x):
    return ((x, 2 * y + z), (y, 2 * z + x), (z, 2 * x + y))[third]


def assemble_kernel(spot, *refs):
    sides, outs = (refs[:4], refs[4:8]), refs[8:]
    unit = outs[0].shape[0] // 4
    width = outs[0].shape[1] // 3

    def place(core, why):
        for kind, out in enumerate(outs):
            side, y = (kind & 1) ^ core, (kind >> 1) ^ why
            for third in range(3):
                lanes = slice(third * width, (third + 1) * width)
                for z in range(2):
                    for x in range(2):
                        array, index = unit_of(third, y, z, x)
                        rows = slice(index * unit, (index + 1) * unit)
                        source = sides[side][1 + third][rows] if array else sides[side][0][rows, lanes]
                        out[(2 * z + x) * unit : (2 * z + x + 1) * unit, lanes] = source

    for core in range(2):
        for why in range(2):
            pl.when((spot[0] == core) & (spot[1] == why))(lambda core=core, why=why: place(core, why))


def assemble(spot, arrays, width):
    return call(assemble_kernel, [like(width, width)] * 4, (spot, *arrays), "assemble", smem=1)


def kinds_kernel(side, spot, *refs):
    lefts, rights, refs, left, right = refs[:4], refs[4:6], refs[6:-2], refs[-2], refs[-1]
    back, outs = (None, refs) if side else (refs[0], refs[1:])
    width = left.shape[1]
    unit, third_width = width // 4, width // 3
    for y in range(2):
        kind = (spot[1] ^ y) * 2 + (spot[0] ^ side)
        for k in range(4):

            @pl.when(kind == k)
            def _():
                left[...] = lefts[k][...]
                right[...] = rights[k == 3][...]

        for third in range(3):
            lanes = slice(third * third_width, (third + 1) * third_width)
            part = tn(left[...], right[:, lanes])
            for z in range(2):
                for x in range(2):
                    array, index = unit_of(third, y, z, x)
                    rows = slice(index * unit, (index + 1) * unit)
                    both_rows = slice(array * width + index * unit, array * width + (index + 1) * unit)
                    piece = part[(2 * z + x) * unit : (2 * z + x + 1) * unit]
                    if side:
                        outs[0][both_rows, lanes] = piece.astype(bf16)
                    else:
                        piece = piece + back[both_rows, lanes].astype(f32)
                        outs[2 * third + array][rows] = piece.astype(bf16)


def kind_products(side, spot, lefts, rights, backs=()):
    rows, width = lefts[0].shape
    return call(
        lambda *refs: kinds_kernel(side, *refs),
        [like(2 * width, width)] if side else [like(width, width // 3)] * 6,
        (spot, *lefts, *rights, *backs),
        "kind_products",
        scratch=[pltpu.VMEM((rows, width), bf16)] * 2,
        smem=1,
    )


def rows_send(parts, axis, level, data_index):
    bit = (data_index >> level) & 1
    return pick(parts, axis, bit), swap(pick(parts, axis, 1 - bit), (1 << level, 0))


def lanes_join(keep, back, level, data_index):
    bit = (data_index >> level) & 1
    return jnp.where(bit == 0, jnp.concatenate([keep, back], -1), jnp.concatenate([back, keep], -1))


def lanes_split(block, level, data_index):
    bit = (data_index >> level) & 1
    width = block.shape[-1] // 2
    low, high = block[..., :width], block[..., width:]
    return jnp.where(bit == 0, low, high), jnp.where(bit == 0, high, low)


def lanes_send(block, level, data_index):
    keep, send = lanes_split(block, level, data_index)
    return keep, swap(send, (1 << level, 0))


def lanes_sum(block, level, data_index):
    keep, send = lanes_split(block, level, data_index)
    return added(keep, swap(send, (1 << level, 0)))


def rows_join(keep, back, level, data_index, lead):
    bit = (data_index >> level) & 1
    return jnp.where(bit == 0, jnp.stack([keep, back], lead), jnp.stack([back, keep], lead))


def halves(buf):
    size = buf.shape[0] // 2
    return buf[:size], buf[size:]


def added(keep, back):
    return (keep.astype(f32) + back.astype(f32)).astype(bf16)


def tree_sum(values):
    while values.shape[0] > 1:
        half = values.shape[0] // 2
        values = values[:half] + values[half:]
    return values[0]


def tie(*values):
    return lax.optimization_barrier(values) if len(values) > 1 else lax.optimization_barrier(values[0])


FEED = (((X, Y), (Y, Z1), (Z1, X)), ((Z1, Z1), (X, X), (Y, Y)))
THIRDS = tuple(tuple((bits, bits) for bits in order) for order in ((Z1, Y, X), (X, Z1, Y), (Y, X, Z1)))


def early_bits(model_bits):
    return [(0, 1 << k) for k in range(2, model_bits)]


def stage_swap(parts, plan, stage):
    return tuple(swap(part, *table[stage]) for part, table in zip(parts, plan))


def core_swap(parts):
    return tuple(swap(part, CORE) for part in parts)


def early_join(buf, bits):
    return jnp.concatenate([buf, swap(buf, bits)], 0)


def join_order(model_bits):
    return [*range(2, model_bits), 0, 1]


def join_masks(model_bits):
    joins = join_order(model_bits)
    return [sum(((place >> k) & 1) << bit for k, bit in enumerate(joins)) for place in range(1 << model_bits)]


def feed_places(rows, model_bits):
    early = early_bits(model_bits)
    unit_rows = rows << len(early)
    cut = unit_rows * 2 // 3
    step = math.gcd(rows, cut)
    tables = []
    for core in range(2):
        places = []
        spans = range(0, cut, step), range(cut, unit_rows, step)
        for side, last, (table, span), *bits in itertools.product(
            range(2), range(2), list(zip(FEED, spans)), range(2), range(2)
        ):
            d, m = side, 0
            for bit, stage in zip((last, *bits), reversed(table)):
                d, m = d ^ bit * stage[core ^ side][0], m ^ bit * stage[core ^ side][1]
            for row in span:
                block, m_row = row // rows, m
                for level, (_, m_bits) in enumerate(early):
                    m_row = m_row ^ ((block >> level) & 1) * m_bits
                places.append((join_masks(model_bits).index(m_row), d, row % rows // step))
        tables.append(np.array(places, np.int32))
    return step, tables


def one_hot_rows(index, count):
    return (index[:, None] == jnp.arange(count, dtype=jnp.int32)[None]).astype(f32)


def on_device(
    tokens,
    conditioning,
    lengths,
    w_ada,
    b_ada,
    w_qkv,
    b_qv,
    w_out,
    b_out,
    w_up,
    b_up,
    w_down,
    b_down,
    cotangent,
):
    data_ways, model_ways = lax.axis_size("dp"), lax.axis_size("mp")
    data_index, model_index = lax.axis_index("dp"), lax.axis_index("mp")
    data_bits, model_bits = bits_of(data_ways), bits_of(model_ways)
    early = early_bits(model_bits)
    local_rows, width = tokens.shape
    lanes = width // data_ways
    head_cols = w_qkv.shape[2]
    hidden = w_up.shape[1]
    images = lengths.shape[0]
    binary = (2,) * data_bits
    feed_count = hidden // 4
    all_hidden = hidden * model_ways
    spot = jnp.stack([data_index & 1, (data_index >> 1) & 1]).astype(jnp.int32)
    forth = [(k, k + 1) for k in range(model_ways - 1)]
    back_to = [(k + 1, k) for k in range(model_ways - 1)]

    mixed = jnp.concatenate([jnp.swapaxes(w_qkv, 1, 2), w_out[None]], 0).reshape(2, 2, 1, head_cols, lanes)
    keep, back = rows_send(mixed, 1, 0, data_index)
    feed = jnp.stack([jnp.swapaxes(w_up, 0, 1), w_down], 0).reshape(2, 2, 2, feed_count, lanes)
    feed_keep, feed_back = rows_send(feed, 2, 0, data_index)
    others = [swap(conditioning, (d, 0)) for d in range(1, data_ways)]
    back, feed_back, others = tie(back, feed_back, others)
    cond = jnp.stack([conditioning, *others], 0)
    mixed = lanes_join(keep, back, 0, data_index)
    joins = join_order(model_bits)
    small_rows, small_lanes = -(-(images + 1) // 8) * 8, -(-6 * head_cols // LANE) * LANE

    def modulate(cond):
        part = lax.dynamic_slice_in_dim(cond, data_index * lanes, lanes, 2).astype(f32)
        cond_act = jax.nn.silu(part).astype(bf16)
        mod = nn(cond_act.reshape(data_ways * images, lanes), w_ada.reshape(lanes, 6 * head_cols))
        mod = mod.reshape(data_ways, images, 6 * head_cols)
        backs = yield [swap(mod[d], (d, 0)) for d in range(1, data_ways)]
        mod = sum(backs, mod[0]) + b_ada.astype(f32).reshape(1, 6 * head_cols)
        biases = jnp.concatenate([b_qv.reshape(-1), b_up], 0).astype(f32)
        buf = jnp.pad(mod, ((0, small_rows - images), (0, small_lanes - 6 * head_cols)))
        bias = jnp.pad(biases[None], ((small_rows - 1, 0), (0, small_lanes - 6 * head_cols)))
        buf = (buf + bias)[None]
        for bit in joins:
            back = yield swap(buf, (0, 1 << bit))
            buf = jnp.concatenate([buf, back], 0)
        yield (cond_act, buf)

    steps = 1 + model_bits

    for k, bits in enumerate(early):
        back = swap(mixed, bits)
        if k == 0:
            feed = lanes_join(feed_keep, feed_back, 0, data_index)
            feed_keep, feed_back = rows_send(feed, 1, 1, data_index)
            chain = modulate(cond)
            small = next(chain)
            back, feed_back, small = tie(back, feed_back, small)
            small = chain.send(small)
            steps -= 1
        mixed = jnp.concatenate([mixed, back], 1)
    keep, back = rows_send(mixed, 0, 1, data_index)
    before, after = lax.ppermute(tokens[HALF:], "mp", forth), lax.ppermute(tokens[:HALF], "mp", back_to)
    back, small, lengths, before, after = tie(back, small, lengths, before, after)
    small = chain.send(small)
    steps -= 1
    mixed = lanes_join(keep, back, 1, data_index)
    for level in range(2, data_bits):
        mixed = lanes_join(mixed, swap(mixed, (1 << level, 0)), level, data_index)
    mixed = mixed.reshape(-1, width)
    third = width // 3
    mixed = tuple(mixed[:, k * third : (k + 1) * third] for k in range(3))
    feed = lanes_join(feed_keep, feed_back, 1, data_index)
    for level in range(2, data_bits):
        feed = lanes_join(feed, swap(feed, (1 << level, 0)), level, data_index)
    backs, small, feed = tie(stage_swap(mixed, THIRDS, 0), small, feed)
    for _ in range(steps - 1):
        small = chain.send(small)
    mixed = grow(mixed, backs)
    up, down = feed[0], feed[1]
    for bits in early[:-1]:
        up, down = early_join(up, bits), early_join(down, bits)

    starts = jnp.cumsum(lengths) - lengths
    half_rows = (model_index * 2 + jnp.arange(-1, 3, dtype=jnp.int32)) * HALF
    inside = (half_rows[:, None] >= starts[None]) & (half_rows[:, None] < (starts + lengths)[None])
    seated = jnp.any(inside, axis=1)
    is_first = jnp.any(inside & (half_rows[:, None] == starts[None]), axis=1)
    paired = jnp.any(inside & (lengths[None] == 2 * HALF), axis=1)
    own_index = jnp.arange(4, dtype=jnp.int32)
    partner = jnp.where(is_first, own_index + 1, own_index - 1)
    facts = jnp.stack([partner, paired.astype(jnp.int32), seated.astype(jnp.int32)], 1)[1:3]
    facts = facts.reshape(6).astype(jnp.int32)
    table = inside.astype(f32)
    number = jnp.sum(jnp.where(inside, jnp.arange(images, dtype=jnp.int32)[None], 0), axis=1)
    number = jnp.where(seated, number, -1)

    backs, table, facts, number, small, up, down = tie(
        stage_swap(mixed, THIRDS, 1), table, facts, number, small, up, down
    )
    mixed, mixed_both = grow_both(mixed, backs, 1)
    backs = stage_swap(mixed, THIRDS, 2)
    cond_act, buf = chain.send(small)
    up_back = swap(up, early[-1])

    shifts = jnp.array(join_masks(model_bits), jnp.int32) ^ model_index
    flip = (shifts[None] == jnp.arange(model_ways, dtype=jnp.int32)[:, None]).astype(f32)
    (vectors,) = call(
        lambda *refs: vectors_kernel(head_cols, *refs),
        [like(24, width, f32)],
        (number, shifts, buf),
        "modulation_vectors",
        scratch=[pltpu.VMEM((24, width), f32)],
        smem=2,
    )
    bias_rel = buf[:, -1, : 6 * head_cols]
    bias_q, bias_v = (bias_rel[:, k * head_cols : (k + 1) * head_cols].reshape(1, -1) for k in range(2))
    step, places = feed_places(feed_count, model_bits)
    place = jnp.where((data_index & 1) == 0, places[0], places[1])
    granules = all_hidden // step
    source = (place[:, 0] * 4 + (place[:, 1] ^ (data_index & 3))) * (feed_count // step) + place[:, 2]
    source = one_hot_rows(source, granules)
    bias_up = jnp.dot(source, bias_rel[:, 2 * head_cols :].reshape(granules, step), precision=highest)
    bias_up = bias_up.reshape(1, all_hidden)
    (grad_mlp,) = call(gate_kernel, [like(local_rows, width)], (cotangent, vectors), "grad_mlp")
    (span_input,) = call(
        span_kernel, [like(2 * local_rows, width)], (before, tokens, after, vectors), "attention_input"
    )
    b_out, b_down = b_out.astype(f32).reshape(1, width), b_down.astype(f32).reshape(1, width)
    own = slice(HALF, HALF + local_rows)
    near = swap(mixed_both, CORE)
    backs, up_back, near, span_input, bias_up, bias_q, bias_v, grad_mlp, b_out, b_down, vectors, source = tie(
        backs, up_back, near, span_input, bias_up, bias_q, bias_v, grad_mlp, b_out, b_down, vectors, source
    )
    cut = up.shape[0] * 4 // 3
    outs = [like(cut, width), like(cut // 2, width)]
    up = call(join_kernel, outs, (up, up_back), "join")
    up_backs = stage_swap(up, FEED, 0)
    far = core_swap(backs)
    up_backs, far, down = tie(up_backs, far, down)
    attn_input = span_input[own]

    up = grow(up, up_backs)
    up_backs = stage_swap(up, FEED, 1)
    down_back = swap(down, early[-1])
    wq, wk, wv, wo = assemble(spot, (mixed_both, *backs, near, *far), width)
    query, key, value = call(
        qkv_kernel,
        [like(2 * local_rows, width)] * 3,
        (span_input, wq, wk, wv, bias_q, bias_v),
        "query_key_value",
    )
    up_backs, down_back, query, key, value = tie(up_backs, down_back, query, key, value)
    up, up_both = grow_both(up, up_backs, 0)
    up_backs = stage_swap(up, FEED, 2)
    down = call(join_kernel, outs, (down, down_back), "join")
    down_backs = stage_swap(down, FEED, 0)
    up_near = swap(up_both, CORE)
    attended, branch, residual, mlp_input = call(
        attend_forward,
        [like(local_rows, width), like(local_rows, width, f32), like(local_rows, width, f32), like(local_rows, width)],
        (facts, query, key, value, wo, b_out, tokens, vectors),
        "attention_forward",
        scratch=[pltpu.VMEM((2 * HALF, width), bf16)] * 2,
        smem=1,
    )

    up_backs, up_near, down_backs, mlp_input = tie(up_backs, up_near, down_backs, mlp_input)
    up_far = core_swap(up_backs)
    down = grow(down, down_backs)
    down_backs = stage_swap(down, FEED, 1)
    up_far, down_backs, mlp_input = tie(up_far, down_backs, mlp_input)
    ups = up_both, *up_backs, up_near, *up_far
    act, slope = call(up_kernel, [like(local_rows, all_hidden)] * 2, (mlp_input, bias_up, *ups), "up")
    down, down_both = grow_both(down, down_backs, 0)
    down_backs = stage_swap(down, FEED, 2)
    down_near = swap(down_both, CORE)
    down_backs, down_near, act = tie(down_backs, down_near, act)
    down_far = core_swap(down_backs)
    other = all_hidden // 2
    sizes = (up[0].shape[0], up[1].shape[0]) * 2
    sum_down = products(act, grad_mlp, other, (other,))
    down_far, sum_down = tie(down_far, sum_down)
    sum_down = core_swap(sum_down)
    downs = down_both, *down_backs, down_near, *down_far
    grad_pre, grad_bias, output, output_sums = call(
        down_kernel,
        [like(local_rows, all_hidden), like(1, all_hidden, f32), like(local_rows, width), like(8, width, f32)],
        (grad_mlp, slope, act, residual, cotangent, vectors, b_down, *downs),
        "down",
        scratch=[pltpu.VMEM((local_rows, width), f32)],
    )
    (grad_mlp_input,) = call(back_kernel, [like(local_rows, width, f32)], (grad_pre, *ups), "grad_mlp_input")
    grad_residual, grad_branch, grad_attended, middle_sums = call(
        middle_kernel,
        [like(local_rows, width, f32), like(local_rows, width), like(local_rows, width), like(8, width, f32)],
        (grad_mlp_input, residual, branch, cotangent, vectors, wo),
        "grad_attended",
    )
    sum_up = products(grad_pre, mlp_input, other, (other,))
    sum_down, sum_up, grad_attended, grad_branch, grad_pre = tie(
        sum_down, sum_up, grad_attended, grad_branch, grad_pre
    )
    sum_up = core_swap(sum_up)
    from_after = lax.ppermute(grad_branch[:HALF], "mp", back_to)
    from_before = lax.ppermute(grad_branch[HALF:], "mp", forth)

    full, half_full = pltpu.VMEM((2 * HALF, width), f32), pltpu.VMEM((2 * HALF, width), bf16)

    def attention_back(half, *operands):
        return call(
            lambda *refs: attend_backward(half, *refs),
            [like(local_rows, width), like(local_rows, width, f32), like(local_rows, width, f32)],
            (facts, query, key, value, grad_attended, *operands),
            "attention_backward",
            scratch=[half_full, half_full, full, full],
            smem=1,
        )

    first_half = attention_back(0)
    sum_down = products(act, grad_mlp, 0, sizes, sum_down)
    down_keeps, down_sends = sum_down[:2], sum_down[2:]
    grad_query, own_key, own_value = attention_back(1, *first_half)
    sum_up, from_after, from_before, grad_query, down_sends = tie(
        sum_up, from_after, from_before, grad_query, down_sends
    )
    down_backs = stage_swap(down_sends, FEED, 2)
    sum_up = products(grad_pre, mlp_input, 0, sizes, sum_up)
    up_keeps, up_sends = sum_up[:2], sum_up[2:]
    grad_key, grad_value = call(
        attend_outside,
        [like(local_rows, width)] * 2,
        (facts, query, key, value, from_before, from_after, wo, own_key, own_value),
        "attention_outside",
        scratch=[half_full, half_full, pltpu.VMEM((HALF, width), bf16), full, full],
        smem=1,
    )
    down_backs, up_sends, grad_key, grad_value = tie(down_backs, up_sends, grad_key, grad_value)
    up_backs = stage_swap(up_sends, FEED, 2)
    lefts, rights = (grad_query, grad_key, grad_value, attended), (attn_input, grad_branch)
    sum_mixed = kind_products(1, spot, lefts, rights)
    flat_up = lax.dot_general(
        source, grad_bias.reshape(granules, step), (((0,), (0,)), ((), ())), precision=highest
    ).reshape(model_ways, hidden)
    up_backs, sum_mixed, flat_up = tie(up_backs, sum_mixed, flat_up)
    sum_mixed = core_swap(sum_mixed)
    feed_keeps, feed_sends = halve_join((*up_keeps, *down_keeps), (*up_backs, *down_backs))
    feed_backs = stage_swap(feed_sends, FEED, 1)
    grad_tokens, last_sums = call(
        last_kernel,
        [like(local_rows, width, f32), like(8, width, f32)],
        (grad_query, grad_key, grad_value, wq, wk, wv, tokens, vectors, grad_residual),
        "grad_tokens",
    )
    sum_mixed = kind_products(0, spot, lefts, rights, sum_mixed)
    mixed_keeps, mixed_sends = sum_mixed[0::2], sum_mixed[1::2]
    mixed_sends, last_sums = tie(mixed_sends, last_sums)
    feed_backs = lax.optimization_barrier((feed_backs, mixed_sends))[0]
    mixed_backs = stage_swap(mixed_sends, THIRDS, 2)
    feed_keeps, feed_sends = halve(feed_keeps, feed_backs, 2)
    feed_backs = stage_swap(feed_sends, FEED, 0)

    packed, plain = call(
        lambda *refs: pack_kernel(head_cols, *refs),
        [jax.ShapeDtypeStruct((model_ways, small_rows, small_lanes), f32), jax.ShapeDtypeStruct((1, 8, small_lanes), f32)],
        (number, shifts, last_sums, middle_sums, output_sums, flat_up),
        "pack_sums",
        scratch=[pltpu.VMEM((16, width), f32)],
        smem=2,
    )
    plain = jnp.pad(plain, ((0, 0), (0, small_rows - 8), (0, 0)))

    def gather_sums():
        buf, rest = packed.reshape((2,) * model_bits + (small_rows, small_lanes)), plain
        for bit in (0, 1, *range(2, model_bits)):
            axis = model_bits - 1 - joins.index(bit)
            keep, send = (lax.slice_in_dim(buf, k, k + 1, axis=axis) for k in (0, 1))
            send = jnp.concatenate([send.reshape(-1, small_rows, small_lanes), rest], 0).astype(bf16)
            back = yield swap(send, (0, 1 << bit))
            back = back.astype(f32)
            buf = keep + back[:-1].reshape(keep.shape)
            rest = send[-1:].astype(f32) + back[-1:]
        own = jnp.concatenate([buf.reshape(small_rows, small_lanes), rest[0, :8]], 0).astype(bf16)
        others = yield [swap(own, (d, 0)) for d in range(1, data_ways)]
        yield jnp.stack([own, *others], 0)

    mixed_backs, packed, plain = tie(mixed_backs, packed, plain)
    chain = gather_sums()
    steps = model_bits + 1
    small = next(chain)
    mixed_keeps, mixed_sends = halve(mixed_keeps, mixed_backs)
    mixed_backs = stage_swap(mixed_sends, THIRDS, 1)
    merged_rows = feed_count << len(early) - 1
    feed_keep, feed_send = merge(merge_rows_kernel, feed_keeps, feed_backs, merged_rows, 2 * width)
    feed_back = swap(feed_send, early[-1])
    mixed_backs, small = tie(mixed_backs, small)
    small = chain.send(small)
    steps -= 1
    mixed_keeps, mixed_sends = halve(mixed_keeps, mixed_backs)
    mixed_backs = stage_swap(mixed_sends, THIRDS, 0)
    feed_done = added(feed_keep, feed_back)
    for bits in reversed(early[:-1]):
        keep, send = halves(feed_done)
        feed_done = added(keep, swap(send, bits))
    feed_done = jnp.stack([feed_done[:, :width], feed_done[:, width:]], 0)
    for level in reversed(range(2, data_bits)):
        feed_done = lanes_sum(feed_done, level, data_index)
    mixed_backs, feed_done, small = tie(mixed_backs, feed_done, small)
    small = chain.send(small)
    steps -= 1
    merged_rows = head_cols << len(early) - 1
    mixed_keep, mixed_send = merge(merge_lanes_kernel, mixed_keeps, mixed_backs, merged_rows, width)
    mixed_back = swap(mixed_send, early[-1])
    feed_keep, feed_back = lanes_send(feed_done, 1, data_index)
    mixed_back, feed_back, small = tie(mixed_back, feed_back, small)
    small = chain.send(small)
    steps -= 1
    mixed_done = added(mixed_keep, mixed_back)
    for bits in reversed(early[:-1]):
        keep, send = halves(mixed_done)
        mixed_done = added(keep, swap(send, bits))
    for level in reversed(range(2, data_bits)):
        mixed_done = lanes_sum(mixed_done, level, data_index)
    keep, back = lanes_send(mixed_done, 1, data_index)
    feed_done = rows_join(feed_keep, feed_back, 1, data_index, 0)
    feed_keep, feed_back = lanes_send(feed_done, 0, data_index)
    back, feed_back, small = tie(back, feed_back, small)
    small = chain.send(small)
    steps -= 1
    mixed_done = rows_join(keep, back, 1, data_index, 0)
    keep, back = lanes_send(mixed_done, 0, data_index)
    feed_done = rows_join(feed_keep, feed_back, 0, data_index, 1).reshape(4, 2, feed_count, lanes)
    for _ in range(steps):
        small = chain.send(small)
    mixed_done = rows_join(keep, back, 0, data_index, 1).reshape(4, head_cols, lanes)
    grad_modulation = small[:, :images, : 6 * head_cols]
    rest = tree_sum(small[:, small_rows - 1 :].astype(f32))
    grad_w_ada = tn(
        cond_act.reshape(data_ways * images, lanes),
        grad_modulation.reshape(data_ways * images, 6 * head_cols),
    )
    grad_w_ada = grad_w_ada.reshape(lanes, 6, head_cols)
    grad_b_ada = tree_sum(jnp.sum(grad_modulation, axis=1, dtype=f32)).reshape(6, head_cols)
    per = -(-width // small_lanes)
    grad_b_out, grad_b_down = (rest[1 + k * per : 1 + (k + 1) * per].reshape(-1)[:width] for k in range(2))
    own_bias = rest[0, : 6 * head_cols]
    grad_b_qv, grad_b_up = own_bias[: 2 * head_cols].reshape(2, head_cols), own_bias[2 * head_cols :]

    grad_w_up, grad_w_down = call(
        place_feed_kernel, [like(lanes, hidden, f32)] * 2, (feed_done,), "place_feed_forward"
    )
    grad_w_down = jnp.swapaxes(grad_w_down, 0, 1)
    mixed_done = mixed_done.astype(f32)
    grad_w_qkv, grad_w_out = jnp.swapaxes(mixed_done[:3], 1, 2), mixed_done[3]
    return (
        output,
        grad_tokens,
        grad_w_ada,
        grad_b_ada,
        grad_w_qkv,
        grad_b_qv,
        grad_w_out,
        grad_b_out,
        grad_w_up,
        grad_b_up,
        grad_w_down,
        grad_b_down,
    )


def solution(mesh):
    in_specs = (
        P(("dp", "mp"), None),
        P("dp", None),
        P("dp"),
        P("dp", None, "mp"),
        P(None, "mp"),
        P(None, "dp", "mp"),
        P(None, "mp"),
        P("mp", "dp"),
        P(),
        P("dp", "mp"),
        P("mp"),
        P("mp", "dp"),
        P(),
        P(("dp", "mp"), None),
    )
    out_specs = (
        P(("dp", "mp"), None),
        P(("dp", "mp"), None),
        P("dp", None, "mp"),
        P(None, "mp"),
        P(None, "dp", "mp"),
        P(None, "mp"),
        P("mp", "dp"),
        P(),
        P("dp", "mp"),
        P("mp"),
        P("mp", "dp"),
        P(),
    )
    return jax.shard_map(
        on_device, mesh=mesh, in_specs=in_specs, out_specs=out_specs, check_vma=False
    )
```

```python
import itertools
import math

import jax
import jax.numpy as jnp
import numpy as np
from jax import lax
from jax.experimental import pallas as pl
from jax.experimental.pallas import tpu as pltpu
from jax.sharding import PartitionSpec as P

HD = 72
HALF = 128
LANE = 128
EPS = 1e-06
HIDE = -1e30

f32, bf16 = jnp.float32, jnp.bfloat16
highest = lax.Precision.HIGHEST

CORE, Y, X, Z1 = (1, 0), (2, 0), (0, 1), (0, 2)


def swap(values, even, odd=None):
    odd = even if odd is None else odd
    data_ways, model_ways = lax.axis_size("dp"), lax.axis_size("mp")
    pairs = []
    for d in range(data_ways):
        d_bits, m_bits = odd if d % 2 else even
        for m in range(model_ways):
            pairs.append((d * model_ways + m, (d ^ d_bits) * model_ways + (m ^ m_bits)))
    return lax.ppermute(values, ("dp", "mp"), pairs)


def bits_of(count):
    return count.bit_length() - 1


def pick(values, axis, index):
    low, high = (lax.index_in_dim(values, k, axis, keepdims=False) for k in (0, 1))
    return jnp.where(index == 0, low, high)


def nn(a, b):
    return jnp.dot(a, b, preferred_element_type=f32)


def nt(a, b):
    return lax.dot_general(a, b, (((1,), (1,)), ((), ())), preferred_element_type=f32)


def tn(a, b):
    return lax.dot_general(a, b, (((0,), (0,)), ((), ())), preferred_element_type=f32)


def head_windows(width):
    for head in range(width // HD):
        first, last = head * HD, head * HD + HD
        low = first // LANE * LANE
        high = -(-last // LANE) * LANE
        yield first, last, low, high


def lane_mask(first, last, low, high):
    lane = lax.broadcasted_iota(jnp.int32, (HALF, high - low), 1) + low
    return (lane >= first) & (lane < last)


def same_segment(paired, seated):
    row = lax.broadcasted_iota(jnp.int32, (HALF, 2 * HALF), 0)
    col = lax.broadcasted_iota(jnp.int32, (HALF, 2 * HALF), 1)
    own = (col < HALF) & ((row == col) | (seated > 0))
    return own | ((col >= HALF) & (paired > 0))


def same_segment_keys(paired, seated):
    key = lax.broadcasted_iota(jnp.int32, (2 * HALF, HALF), 0)
    col = lax.broadcasted_iota(jnp.int32, (2 * HALF, HALF), 1)
    own = (key < HALF) & ((key == col) | (seated > 0))
    return own | ((key >= HALF) & (paired > 0))


def split_rows(rows):
    return pl.ds(rows * HALF, HALF)


def row(vectors, kind, half):
    return vectors[4 * kind + half : 4 * kind + half + 1]


def normalize(values):
    centred = values - jnp.mean(values, axis=-1, keepdims=True)
    spread = jnp.mean(centred * centred, axis=-1, keepdims=True)
    root = lax.rsqrt(spread + EPS)
    return centred * root, root


def normalize_back(norm, root, upstream):
    return (
        upstream
        - jnp.mean(upstream, axis=-1, keepdims=True)
        - norm * jnp.mean(upstream * norm, axis=-1, keepdims=True)
    ) * root


def column_sum(values):
    return jnp.sum(values, axis=0, keepdims=True)


def vectors_kernel(columns, images, shifts, buf, out, part):
    part[...] = jnp.zeros(part.shape, f32)
    for block in range(buf.shape[0]):
        for half in range(4):
            number = lax.broadcasted_iota(jnp.int32, buf.shape[1:], 0)
            vector = column_sum(jnp.where(number == images[half], buf[block], 0.0))
            for kind in range(6):
                part[4 * kind + half : 4 * kind + half + 1, :columns] = vector[:, kind * columns : (kind + 1) * columns]
        moved = pltpu.roll(part[...], shifts[block] * columns, 1)
        out[...] = moved if block == 0 else out[...] + moved


def pack_kernel(columns, images, shifts, last, middle, output, bias_up, out, plain, rows):
    count, _, lanes = out.shape
    bias_row = out.shape[1] - 1
    width = rows.shape[1]
    rows[...] = jnp.zeros(rows.shape, f32)
    rows[0:4], rows[4:10], rows[10:12] = last[0:4], middle[0:6], output[0:2]
    out[...] = jnp.zeros(out.shape, f32)
    plain[...] = jnp.zeros(plain.shape, f32)
    for block in range(count):
        moved = pltpu.roll(rows[...], jnp.where(shifts[block] > 0, width - shifts[block] * columns, 0), 1)
        number = lax.broadcasted_iota(jnp.int32, (out.shape[1], columns), 0)
        for kind in range(6):
            place = slice(kind * columns, (kind + 1) * columns)
            low, high = (moved[2 * kind + half : 2 * kind + half + 1, :columns] for half in range(2))
            out[block, :, place] = jnp.where(number == images[1], low, 0.0) + jnp.where(number == images[2], high, 0.0)
        mine = slice(block * columns, (block + 1) * columns)
        out[block, bias_row : bias_row + 1, :columns] = last[4:5, mine]
        out[block, bias_row : bias_row + 1, columns : 2 * columns] = last[5:6, mine]
        out[block, bias_row : bias_row + 1, 2 * columns : 6 * columns] = bias_up[block : block + 1]
    per = -(-width // lanes)
    for k, source in enumerate((middle[6:7], output[2:3])):
        for piece in range(per):
            size = min(lanes, width - piece * lanes)
            plain[0, k * per + piece : k * per + piece + 1, :size] = source[:, piece * lanes : piece * lanes + size]


def span_kernel(before, tokens, after, vectors, out):
    for half in range(4):
        source = (before, tokens, tokens, after)[half]
        norm, _ = normalize(source[split_rows(half == 2)].astype(f32))
        out[split_rows(half)] = (norm * (1.0 + row(vectors, 1, half)) + row(vectors, 0, half)).astype(bf16)


def qkv_kernel(span, wq, wk, wv, bias_q, bias_v, query, key, value):
    query[...] = (nt(span[...], wq[...]) + bias_q[...]).astype(bf16)
    key[...] = nt(span[...], wk[...]).astype(bf16)
    value[...] = (nt(span[...], wv[...]) + bias_v[...]).astype(bf16)


def attend_forward(
    facts, q_ref, k_ref, v_ref, wo, b_out, tokens, vectors, o_ref, branch_ref, residual_ref, input_ref, kk, vv
):
    factor = HD ** (-0.5)
    for half in range(2):
        rows = split_rows(half)
        own = split_rows(half + 1)
        other = pl.ds(pl.multiple_of(facts[3 * half] * HALF, HALF), HALF)
        kk[0:HALF], kk[HALF:] = k_ref[own], k_ref[other]
        vv[0:HALF], vv[HALF:] = v_ref[own], v_ref[other]
        same = same_segment(facts[3 * half + 1], facts[3 * half + 2])
        for first, last, low, high in head_windows(q_ref.shape[1]):
            window = slice(low, high)
            mask = lane_mask(first, last, low, high)
            query = jnp.where(mask, q_ref[own, window], 0)
            scores = jnp.where(same, nt(query, kk[:, window]) * factor, HIDE)
            exp_scores = jnp.exp(scores - jnp.max(scores, axis=1, keepdims=True))
            prob = exp_scores / jnp.sum(exp_scores, axis=1, keepdims=True)
            mixed = nn(prob.astype(bf16), vv[:, window]).astype(bf16)
            o_ref[rows, window] = jnp.where(mask, mixed, o_ref[rows, window]) if first > low else mixed
    for half in range(2):
        rows = split_rows(half)
        branch = nn(o_ref[rows], wo[...]) + b_out[...]
        branch_ref[rows] = branch
        residual = tokens[rows].astype(f32) + row(vectors, 2, half + 1) * branch
        residual_ref[rows] = residual
        norm, _ = normalize(residual)
        input_ref[rows] = (norm * (1.0 + row(vectors, 4, half + 1)) + row(vectors, 3, half + 1)).astype(bf16)


def score_gradients(query, grad, keys, values, same):
    scores = nt(keys, query) * HD ** (-0.5)
    if same is not None:
        scores = jnp.where(same, scores, HIDE)
    exp_scores = jnp.exp(scores - jnp.max(scores, axis=0, keepdims=True))
    prob = exp_scores / jnp.sum(exp_scores, axis=0, keepdims=True)
    grad_prob = nt(values, grad)
    inner = jnp.sum(grad_prob * prob, axis=0, keepdims=True)
    return prob.astype(bf16), (prob * (grad_prob - inner)).astype(bf16)


def attend_backward(half, facts, q_ref, k_ref, v_ref, g_ref, *refs):
    earlier, refs = (refs[:3], refs[3:]) if half else (None, refs)
    dq_ref, own_k, own_v, kk, vv, dkk, dvv = refs
    factor = HD ** (-0.5)
    rows = split_rows(half)
    own = split_rows(half + 1)
    other = pl.ds(pl.multiple_of(facts[3 * half] * HALF, HALF), HALF)
    kk[0:HALF], kk[HALF:] = k_ref[own], k_ref[other]
    vv[0:HALF], vv[HALF:] = v_ref[own], v_ref[other]
    dkk[...] = jnp.zeros(dkk.shape, f32)
    dvv[...] = jnp.zeros(dvv.shape, f32)
    if half:
        dq_ref[0:HALF] = earlier[0][0:HALF]
    same = same_segment_keys(facts[3 * half + 1], facts[3 * half + 2])
    for first, last, low, high in head_windows(q_ref.shape[1]):
        window = slice(low, high)
        mask = lane_mask(first, last, low, high)
        query = jnp.where(mask, q_ref[own, window], 0)
        grad = jnp.where(mask, g_ref[rows, window], 0)
        prob, grad_scores = score_gradients(query, grad, kk[:, window], vv[:, window], same)
        dq = (tn(grad_scores, kk[:, window]) * factor).astype(bf16)
        dq_ref[rows, window] = jnp.where(mask, dq, dq_ref[rows, window]) if first > low else dq
        dkk[:, window] += nn(grad_scores, query) * factor
        dvv[:, window] += nn(prob, grad)
    inside = jnp.where(facts[3 * half] == 2 - half, 1.0, 0.0)
    for place, (total, mine) in enumerate(((dkk, own_k), (dvv, own_v))):
        mine_own, mine_other = total[0:HALF], total[HALF:] * inside
        if half:
            mine_own = mine_own + earlier[1 + place][split_rows(half)]
            mine_other = mine_other + earlier[1 + place][split_rows(1 - half)]
        mine[split_rows(half)], mine[split_rows(1 - half)] = mine_own, mine_other


def attend_outside(
    facts, q_ref, k_ref, v_ref, before, after, wo, own_k, own_v, key_ref, value_ref, kk, vv, grads, dk, dv
):
    factor = HD ** (-0.5)
    dk[...], dv[...] = own_k[...], own_v[...]
    for half, (outside, branch) in enumerate(((0, before), (3, after))):

        @pl.when((facts[3 * half] == outside) & (facts[3 * half + 1] > 0))
        def _():
            mine, theirs = split_rows(half), split_rows(outside)
            kk[0:HALF], kk[HALF:] = k_ref[theirs], k_ref[split_rows(half + 1)]
            vv[0:HALF], vv[HALF:] = v_ref[theirs], v_ref[split_rows(half + 1)]
            grads[...] = nt(branch[...], wo[...]).astype(bf16)
            for first, last, low, high in head_windows(q_ref.shape[1]):
                window = slice(low, high)
                mask = lane_mask(first, last, low, high)
                query = jnp.where(mask, q_ref[theirs, window], 0)
                grad = jnp.where(mask, grads[:, window], 0)
                prob, grad_scores = score_gradients(query, grad, kk[:, window], vv[:, window], None)
                dk[mine, window] += nn(grad_scores[HALF:], query) * factor
                dv[mine, window] += nn(prob[HALF:], grad)

    key_ref[...], value_ref[...] = dk[...].astype(bf16), dv[...].astype(bf16)


def middle_kernel(
    grad_input, residual, branch, cotangent, vectors, wo, grad_residual, grad_branch, grad_attended, sums
):
    sums[...] = jnp.zeros(sums.shape, f32)
    for half in range(2):
        rows = split_rows(half)
        norm, root = normalize(residual[rows])
        grad = grad_input[rows]
        total = cotangent[rows].astype(f32) + normalize_back(norm, root, grad * (1.0 + row(vectors, 4, half + 1)))
        grad_residual[rows] = total
        low = (row(vectors, 2, half + 1) * total).astype(bf16)
        grad_branch[rows] = low
        grad_attended[rows] = nt(low, wo[...]).astype(bf16)
        sums[half : half + 1] = column_sum(total * branch[rows])
        sums[2 + half : 3 + half] = column_sum(grad)
        sums[4 + half : 5 + half] = column_sum(grad * norm)
        sums[6:7] += column_sum(low.astype(f32))


def last_kernel(
    grad_query, grad_key, grad_value, wq, wk, wv, tokens, vectors, grad_residual, grad_tokens, sums
):
    sums[...] = jnp.zeros(sums.shape, f32)
    for half in range(2):
        rows = split_rows(half)
        norm, root = normalize(tokens[rows].astype(f32))
        grad = nn(grad_query[rows], wq[...]) + nn(grad_key[rows], wk[...]) + nn(grad_value[rows], wv[...])
        back = normalize_back(norm, root, grad * (1.0 + row(vectors, 1, half + 1)))
        grad_tokens[rows] = grad_residual[rows] + back
        sums[half : half + 1] = column_sum(grad)
        sums[2 + half : 3 + half] = column_sum(grad * norm)
        sums[4:5] += column_sum(grad_query[rows].astype(f32))
        sums[5:6] += column_sum(grad_value[rows].astype(f32))


VMEM = pl.BlockSpec(memory_space=pltpu.VMEM)
SMEM = pl.BlockSpec(memory_space=pltpu.SMEM)


CHUNK = 96
HINT = pl.CostEstimate(flops=1, bytes_accessed=1, transcendentals=0)


def call(kernel, outs, operands, name, scratch=(), smem=0):
    room = sum(math.prod(v.shape) * v.dtype.itemsize for v in (*scratch, *outs) if hasattr(v, "shape")) + 4 * 2**20
    return pl.pallas_call(
        kernel,
        out_shape=tuple(outs),
        in_specs=[SMEM] * smem + [VMEM] * (len(operands) - smem),
        out_specs=tuple(VMEM for _ in outs),
        scratch_shapes=list(scratch),
        compiler_params=pltpu.CompilerParams(vmem_limit_bytes=room),
        cost_estimate=HINT,
        name=name,
    )(*operands)


def like(rows, width, dtype=bf16):
    return jax.ShapeDtypeStruct((rows, width), dtype)


def grow_kernel(refs, axis=None):
    count = (len(refs) - (axis is not None)) // 3
    both, place = refs[-1], 0
    for own, back, out in zip(refs[:count], refs[count : 2 * count], refs[2 * count : 3 * count]):
        rows, lanes = own.shape
        out[:rows], out[rows:] = own[...], back[...]
        if axis == 0:
            both[place : place + rows], both[place + rows : place + 2 * rows] = own[...], back[...]
            place += 2 * rows
        if axis == 1:
            both[:rows, place : place + lanes], both[rows:, place : place + lanes] = own[...], back[...]
            place += lanes


def grow(parts, backs):
    outs = [like(2 * part.shape[0], part.shape[1]) for part in parts]
    return call(lambda *refs: grow_kernel(refs), outs, (*parts, *backs), "grow")


def grow_both(parts, backs, axis):
    outs = [like(2 * part.shape[0], part.shape[1]) for part in parts]
    if axis == 0:
        both = like(sum(out.shape[0] for out in outs), outs[0].shape[1])
    else:
        both = like(outs[0].shape[0], sum(out.shape[1] for out in outs))
    outs = call(lambda *refs: grow_kernel(refs, axis), [*outs, both], (*parts, *backs), "grow_both")
    return outs[:-1], outs[-1]


def row_sum(keep, back, first, last):
    return keep[first:last] + back[first:last]


def halve_kernel(groups, side, *refs):
    count = len(refs) // 3
    for keep, back, out in zip(refs[:count], refs[count : 2 * count], refs[2 * count :]):
        rows = keep.shape[0] // (2 * groups)
        for group in range(groups):
            base = (2 * group + side) * rows
            for first in range(0, rows, CHUNK):
                last = min(first + CHUNK, rows)
                out[group * rows + first : group * rows + last] = row_sum(keep, back, base + first, base + last)


def halve(keeps, backs, groups=1):
    outs = [like(keep.shape[0] // 2, keep.shape[1]) for keep in keeps]
    high, low = (
        call(lambda *refs, side=side: halve_kernel(groups, side, *refs), outs, (*keeps, *backs), "halve")
        for side in (1, 0)
    )
    return low, high


def halve_join_kernel(side, *refs):
    count = len(refs) // 5
    keeps, backs, outs = refs[: 2 * count], refs[2 * count : 4 * count], refs[4 * count :]
    for k in range(count):
        for which in range(2):
            keep, back = keeps[which * count + k], backs[which * count + k]
            rows = keep.shape[0] // 2
            for first in range(0, rows, CHUNK):
                last = min(first + CHUNK, rows)
                outs[k][which * rows + first : which * rows + last] = row_sum(
                    keep, back, side * rows + first, side * rows + last
                )


def halve_join(keeps, backs):
    outs = [like(keep.shape[0], keep.shape[1]) for keep in keeps[: len(keeps) // 2]]
    high, low = (
        call(lambda *refs, side=side: halve_join_kernel(side, *refs), outs, (*keeps, *backs), "halve_join")
        for side in (1, 0)
    )
    return low, high


def merge_rows_kernel(*refs):
    count = (len(refs) - 2) // 2
    low, high = refs[2 * count :]
    rows, width = low.shape[0], low.shape[1] // 2
    for which in range(2):
        lanes = slice(which * width, (which + 1) * width)
        place = 0
        for keep, back in zip(refs[:count], refs[count : 2 * count]):
            first, end = which * keep.shape[0] // 2, (which + 1) * keep.shape[0] // 2
            while first < end:
                out, base = (low, 0) if place < rows else (high, rows)
                step = min(end - first, base + rows - place)
                out[place - base : place - base + step, lanes] = row_sum(keep, back, first, first + step)
                first, place = first + step, place + step


def merge_lanes_kernel(*refs):
    count = (len(refs) - 2) // 2
    low, high = refs[2 * count :]
    rows, lane = low.shape[0], 0
    for keep, back in zip(refs[:count], refs[count : 2 * count]):
        lanes = slice(lane, lane + keep.shape[1])
        lane += keep.shape[1]
        low[:, lanes], high[:, lanes] = row_sum(keep, back, 0, rows), row_sum(keep, back, rows, 2 * rows)


def merge(kernel, keeps, backs, rows, width):
    return call(kernel, [like(rows, width)] * 2, (*keeps, *backs), "merge")


def row_steps(weights):
    unit = 0
    for weight in weights:
        rows = weight.shape[0]
        step = 256 if rows % 256 == 0 else 384
        for first in range(0, rows, step):
            yield weight, first, first + step, unit + first
        unit += rows


def up_kernel(x_ref, bias_ref, *refs):
    weights, (act_ref, slope_ref) = refs[:-2], refs[-2:]
    for weight, first, last, unit in row_steps(weights):
        units = slice(unit, unit + last - first)
        pre = nt(x_ref[...], weight[first:last]) + bias_ref[:, units]
        square = pre * pre
        inner = jnp.tanh(0.7978845608028654 * pre * (1.0 + 0.044715 * square))
        outer = 0.5 * (1.0 + inner)
        act_ref[:, units] = (pre * outer).astype(bf16)
        rise = (0.5 * 0.7978845608028654) * pre * (1.0 + (3 * 0.044715) * square)
        slope_ref[:, units] = (outer + rise * (1.0 - inner * inner)).astype(bf16)


def down_kernel(grad_mlp, slope, act, residual, cotangent, vectors, b_down, *refs):
    weights, (pre_ref, sum_ref, out, sums, total) = refs[:-5], refs[-5:]
    for weight, first, last, unit in row_steps(weights):
        units = slice(unit, unit + last - first)
        pre = (nt(grad_mlp[...], weight[first:last]) * slope[:, units].astype(f32)).astype(bf16)
        pre_ref[:, units] = pre
        sum_ref[:, units] = column_sum(pre.astype(f32))
    back_kernel(act, *weights, total)
    sums[...] = jnp.zeros(sums.shape, f32)
    for half in range(2):
        rows = split_rows(half)
        mlp = total[rows] + b_down[...]
        out[rows] = (residual[rows] + row(vectors, 5, half + 1) * mlp).astype(bf16)
        sums[half : half + 1] = column_sum(cotangent[rows].astype(f32) * mlp)
        sums[2:3] += column_sum(grad_mlp[rows].astype(f32))


def back_kernel(left_ref, *refs):
    weights, out_ref = refs[:-1], refs[-1]
    unit = 0
    for weight in weights:
        rows = weight.shape[0]
        part = nn(left_ref[:, unit : unit + rows], weight[...])
        out_ref[...] = part if unit == 0 else out_ref[...] + part
        unit += rows


def join_kernel(own, back, wide, narrow):
    rows = own.shape[0]
    more = wide.shape[0] - rows
    wide[:rows], wide[rows:] = own[...], back[:more]
    narrow[...] = back[more:]


def place_feed_kernel(done, grad_up, grad_down):
    for which, out in enumerate((grad_up, grad_down)):
        out[...] = jnp.concatenate([done[way, which] for way in range(done.shape[0])], 0).astype(f32).T


def gate_kernel(cotangent, vectors, out):
    for half in range(2):
        rows = split_rows(half)
        out[rows] = (row(vectors, 5, half + 1) * cotangent[rows].astype(f32)).astype(bf16)


def product_kernel(start, count, left_ref, right_ref, *refs):
    backs, outs = refs[:-count], refs[-count:]
    base = 0
    for out in outs:
        size = out.shape[0]
        step = 384 if backs or size % 256 else 256
        for first in range(0, size, step):
            column = base + first
            part = tn(left_ref[:, start + column : start + column + step], right_ref[...])
            if backs:
                rows = backs[0].shape[0]
                back = backs[column // rows]
                part = part + back[column % rows : column % rows + step].astype(f32)
            out[first : first + step] = part.astype(bf16)
        base += size


def products(left, right, start, counts, backs=()):
    outs = [like(size, right.shape[1]) for size in counts]
    kernel = lambda *refs: product_kernel(start, len(counts), *refs)
    return call(kernel, outs, (left, right, *backs), "products")


def unit_of(third, y, z, x):
    return ((x, 2 * y + z), (y, 2 * z + x), (z, 2 * x + y))[third]


def assemble_kernel(spot, *refs):
    sides, outs = (refs[:4], refs[4:8]), refs[8:]
    unit = outs[0].shape[0] // 4
    width = outs[0].shape[1] // 3

    def place(core, why):
        for kind, out in enumerate(outs):
            side, y = (kind & 1) ^ core, (kind >> 1) ^ why
            for third in range(3):
                lanes = slice(third * width, (third + 1) * width)
                for z in range(2):
                    for x in range(2):
                        array, index = unit_of(third, y, z, x)
                        rows = slice(index * unit, (index + 1) * unit)
                        source = sides[side][1 + third][rows] if array else sides[side][0][rows, lanes]
                        out[(2 * z + x) * unit : (2 * z + x + 1) * unit, lanes] = source

    for core in range(2):
        for why in range(2):
            pl.when((spot[0] == core) & (spot[1] == why))(lambda core=core, why=why: place(core, why))


def assemble(spot, arrays, width):
    return call(assemble_kernel, [like(width, width)] * 4, (spot, *arrays), "assemble", smem=1)


def kinds_kernel(side, spot, *refs):
    lefts, rights, refs, left, right = refs[:4], refs[4:6], refs[6:-2], refs[-2], refs[-1]
    back, outs = (None, refs) if side else (refs[0], refs[1:])
    width = left.shape[1]
    unit, third_width = width // 4, width // 3
    for y in range(2):
        kind = (spot[1] ^ y) * 2 + (spot[0] ^ side)
        for k in range(4):

            @pl.when(kind == k)
            def _():
                left[...] = lefts[k][...]
                right[...] = rights[k == 3][...]

        for third in range(3):
            lanes = slice(third * third_width, (third + 1) * third_width)
            part = tn(left[...], right[:, lanes])
            for z in range(2):
                for x in range(2):
                    array, index = unit_of(third, y, z, x)
                    rows = slice(index * unit, (index + 1) * unit)
                    both_rows = slice(array * width + index * unit, array * width + (index + 1) * unit)
                    piece = part[(2 * z + x) * unit : (2 * z + x + 1) * unit]
                    if side:
                        outs[0][both_rows, lanes] = piece.astype(bf16)
                    else:
                        piece = piece + back[both_rows, lanes].astype(f32)
                        outs[2 * third + array][rows] = piece.astype(bf16)


def kind_products(side, spot, lefts, rights, backs=()):
    rows, width = lefts[0].shape
    return call(
        lambda *refs: kinds_kernel(side, *refs),
        [like(2 * width, width)] if side else [like(width, width // 3)] * 6,
        (spot, *lefts, *rights, *backs),
        "kind_products",
        scratch=[pltpu.VMEM((rows, width), bf16)] * 2,
        smem=1,
    )


def rows_send(parts, axis, level, data_index):
    bit = (data_index >> level) & 1
    return pick(parts, axis, bit), swap(pick(parts, axis, 1 - bit), (1 << level, 0))


def lanes_join(keep, back, level, data_index):
    bit = (data_index >> level) & 1
    return jnp.where(bit == 0, jnp.concatenate([keep, back], -1), jnp.concatenate([back, keep], -1))


def lanes_split(block, level, data_index):
    bit = (data_index >> level) & 1
    width = block.shape[-1] // 2
    low, high = block[..., :width], block[..., width:]
    return jnp.where(bit == 0, low, high), jnp.where(bit == 0, high, low)


def lanes_send(block, level, data_index):
    keep, send = lanes_split(block, level, data_index)
    return keep, swap(send, (1 << level, 0))


def lanes_sum(block, level, data_index):
    keep, send = lanes_split(block, level, data_index)
    return added(keep, swap(send, (1 << level, 0)))


def rows_join(keep, back, level, data_index, lead):
    bit = (data_index >> level) & 1
    return jnp.where(bit == 0, jnp.stack([keep, back], lead), jnp.stack([back, keep], lead))


def halves(buf):
    size = buf.shape[0] // 2
    return buf[:size], buf[size:]


def added(keep, back):
    return (keep.astype(f32) + back.astype(f32)).astype(bf16)


def tree_sum(values):
    while values.shape[0] > 1:
        half = values.shape[0] // 2
        values = values[:half] + values[half:]
    return values[0]


def tie(*values):
    return lax.optimization_barrier(values) if len(values) > 1 else lax.optimization_barrier(values[0])


FEED = (((X, Y), (Y, Z1), (Z1, X)), ((Z1, Z1), (X, X), (Y, Y)))
THIRDS = tuple(tuple((bits, bits) for bits in order) for order in ((Z1, Y, X), (X, Z1, Y), (Y, X, Z1)))


def early_bits(model_bits):
    return [(0, 1 << k) for k in range(2, model_bits)]


def stage_swap(parts, plan, stage):
    return tuple(swap(part, *table[stage]) for part, table in zip(parts, plan))


def core_swap(parts):
    return tuple(swap(part, CORE) for part in parts)


def early_join(buf, bits):
    return jnp.concatenate([buf, swap(buf, bits)], 0)


def join_order(model_bits):
    return [*range(2, model_bits), 0, 1]


def join_masks(model_bits):
    joins = join_order(model_bits)
    return [sum(((place >> k) & 1) << bit for k, bit in enumerate(joins)) for place in range(1 << model_bits)]


def feed_places(rows, model_bits):
    early = early_bits(model_bits)
    unit_rows = rows << len(early)
    cut = unit_rows * 2 // 3
    step = math.gcd(rows, cut)
    tables = []
    for core in range(2):
        places = []
        spans = range(0, cut, step), range(cut, unit_rows, step)
        for side, last, (table, span), *bits in itertools.product(
            range(2), range(2), list(zip(FEED, spans)), range(2), range(2)
        ):
            d, m = side, 0
            for bit, stage in zip((last, *bits), reversed(table)):
                d, m = d ^ bit * stage[core ^ side][0], m ^ bit * stage[core ^ side][1]
            for row in span:
                block, m_row = row // rows, m
                for level, (_, m_bits) in enumerate(early):
                    m_row = m_row ^ ((block >> level) & 1) * m_bits
                places.append((join_masks(model_bits).index(m_row), d, row % rows // step))
        tables.append(np.array(places, np.int32))
    return step, tables


def one_hot_rows(index, count):
    return (index[:, None] == jnp.arange(count, dtype=jnp.int32)[None]).astype(f32)


def on_device(
    tokens,
    conditioning,
    lengths,
    w_ada,
    b_ada,
    w_qkv,
    b_qv,
    w_out,
    b_out,
    w_up,
    b_up,
    w_down,
    b_down,
    cotangent,
):
    data_ways, model_ways = lax.axis_size("dp"), lax.axis_size("mp")
    data_index, model_index = lax.axis_index("dp"), lax.axis_index("mp")
    data_bits, model_bits = bits_of(data_ways), bits_of(model_ways)
    early = early_bits(model_bits)
    local_rows, width = tokens.shape
    lanes = width // data_ways
    head_cols = w_qkv.shape[2]
    hidden = w_up.shape[1]
    images = lengths.shape[0]
    binary = (2,) * data_bits
    feed_count = hidden // 4
    all_hidden = hidden * model_ways
    spot = jnp.stack([data_index & 1, (data_index >> 1) & 1]).astype(jnp.int32)
    forth = [(k, k + 1) for k in range(model_ways - 1)]
    back_to = [(k + 1, k) for k in range(model_ways - 1)]

    mixed = jnp.concatenate([jnp.swapaxes(w_qkv, 1, 2), w_out[None]], 0).reshape(2, 2, 1, head_cols, lanes)
    keep, back = rows_send(mixed, 1, 0, data_index)
    feed = jnp.stack([jnp.swapaxes(w_up, 0, 1), w_down], 0).reshape(2, 2, 2, feed_count, lanes)
    feed_keep, feed_back = rows_send(feed, 2, 0, data_index)
    others = [swap(conditioning, (d, 0)) for d in range(1, data_ways)]
    back, feed_back, others = tie(back, feed_back, others)
    cond = jnp.stack([conditioning, *others], 0)
    mixed = lanes_join(keep, back, 0, data_index)
    joins = join_order(model_bits)
    small_rows, small_lanes = -(-(images + 1) // 8) * 8, -(-6 * head_cols // LANE) * LANE

    def modulate(cond):
        part = lax.dynamic_slice_in_dim(cond, data_index * lanes, lanes, 2).astype(f32)
        cond_act = jax.nn.silu(part).astype(bf16)
        mod = nn(cond_act.reshape(data_ways * images, lanes), w_ada.reshape(lanes, 6 * head_cols))
        mod = mod.reshape(data_ways, images, 6 * head_cols)
        backs = yield [swap(mod[d], (d, 0)) for d in range(1, data_ways)]
        mod = sum(backs, mod[0]) + b_ada.astype(f32).reshape(1, 6 * head_cols)
        biases = jnp.concatenate([b_qv.reshape(-1), b_up], 0).astype(f32)
        buf = jnp.pad(mod, ((0, small_rows - images), (0, small_lanes - 6 * head_cols)))
        bias = jnp.pad(biases[None], ((small_rows - 1, 0), (0, small_lanes - 6 * head_cols)))
        buf = (buf + bias)[None]
        for bit in joins:
            back = yield swap(buf, (0, 1 << bit))
            buf = jnp.concatenate([buf, back], 0)
        yield (cond_act, buf)

    steps = 1 + model_bits

    for k, bits in enumerate(early):
        back = swap(mixed, bits)
        if k == 0:
            feed = lanes_join(feed_keep, feed_back, 0, data_index)
            feed_keep, feed_back = rows_send(feed, 1, 1, data_index)
            chain = modulate(cond)
            small = next(chain)
            back, feed_back, small = tie(back, feed_back, small)
            small = chain.send(small)
            steps -= 1
        mixed = jnp.concatenate([mixed, back], 1)
    keep, back = rows_send(mixed, 0, 1, data_index)
    before, after = lax.ppermute(tokens[HALF:], "mp", forth), lax.ppermute(tokens[:HALF], "mp", back_to)
    back, small, lengths, before, after = tie(back, small, lengths, before, after)
    small = chain.send(small)
    steps -= 1
    mixed = lanes_join(keep, back, 1, data_index)
    for level in range(2, data_bits):
        mixed = lanes_join(mixed, swap(mixed, (1 << level, 0)), level, data_index)
    mixed = mixed.reshape(-1, width)
    third = width // 3
    mixed = tuple(mixed[:, k * third : (k + 1) * third] for k in range(3))
    feed = lanes_join(feed_keep, feed_back, 1, data_index)
    for level in range(2, data_bits):
        feed = lanes_join(feed, swap(feed, (1 << level, 0)), level, data_index)
    up, down = feed[0], feed[1]
    for bits in early[:-1]:
        up, down = early_join(up, bits), early_join(down, bits)
    up_back = swap(up, early[-1])
    backs, small, up_back, down = tie(stage_swap(mixed, THIRDS, 0), small, up_back, down)
    for _ in range(steps - 1):
        small = chain.send(small)
    mixed = grow(mixed, backs)

    starts = jnp.cumsum(lengths) - lengths
    half_rows = (model_index * 2 + jnp.arange(-1, 3, dtype=jnp.int32)) * HALF
    inside = (half_rows[:, None] >= starts[None]) & (half_rows[:, None] < (starts + lengths)[None])
    seated = jnp.any(inside, axis=1)
    is_first = jnp.any(inside & (half_rows[:, None] == starts[None]), axis=1)
    paired = jnp.any(inside & (lengths[None] == 2 * HALF), axis=1)
    own_index = jnp.arange(4, dtype=jnp.int32)
    partner = jnp.where(is_first, own_index + 1, own_index - 1)
    facts = jnp.stack([partner, paired.astype(jnp.int32), seated.astype(jnp.int32)], 1)[1:3]
    facts = facts.reshape(6).astype(jnp.int32)
    table = inside.astype(f32)
    number = jnp.sum(jnp.where(inside, jnp.arange(images, dtype=jnp.int32)[None], 0), axis=1)
    number = jnp.where(seated, number, -1)

    backs, table, facts, number, small, up, down = tie(
        stage_swap(mixed, THIRDS, 1), table, facts, number, small, up, down
    )
    mixed, mixed_both = grow_both(mixed, backs, 1)
    backs = stage_swap(mixed, THIRDS, 2)
    cond_act, buf = chain.send(small)

    shifts = jnp.array(join_masks(model_bits), jnp.int32) ^ model_index
    flip = (shifts[None] == jnp.arange(model_ways, dtype=jnp.int32)[:, None]).astype(f32)
    (vectors,) = call(
        lambda *refs: vectors_kernel(head_cols, *refs),
        [like(24, width, f32)],
        (number, shifts, buf),
        "modulation_vectors",
        scratch=[pltpu.VMEM((24, width), f32)],
        smem=2,
    )
    bias_rel = buf[:, -1, : 6 * head_cols]
    bias_q, bias_v = (bias_rel[:, k * head_cols : (k + 1) * head_cols].reshape(1, -1) for k in range(2))
    step, places = feed_places(feed_count, model_bits)
    place = jnp.where((data_index & 1) == 0, places[0], places[1])
    granules = all_hidden // step
    source = (place[:, 0] * 4 + (place[:, 1] ^ (data_index & 3))) * (feed_count // step) + place[:, 2]
    source = one_hot_rows(source, granules)
    bias_up = jnp.dot(source, bias_rel[:, 2 * head_cols :].reshape(granules, step), precision=highest)
    bias_up = bias_up.reshape(1, all_hidden)
    (grad_mlp,) = call(gate_kernel, [like(local_rows, width)], (cotangent, vectors), "grad_mlp")
    (span_input,) = call(
        span_kernel, [like(2 * local_rows, width)], (before, tokens, after, vectors), "attention_input"
    )
    b_out, b_down = b_out.astype(f32).reshape(1, width), b_down.astype(f32).reshape(1, width)
    own = slice(HALF, HALF + local_rows)
    near = swap(mixed_both, CORE)
    backs, near, span_input, bias_up, bias_q, bias_v, grad_mlp, b_out, b_down, vectors, source = tie(
        backs, near, span_input, bias_up, bias_q, bias_v, grad_mlp, b_out, b_down, vectors, source
    )
    cut = up.shape[0] * 4 // 3
    outs = [like(cut, width), like(cut // 2, width)]
    up = call(join_kernel, outs, (up, up_back), "join")
    up_backs = stage_swap(up, FEED, 0)
    far = core_swap(backs)
    up_backs, far, down = tie(up_backs, far, down)
    attn_input = span_input[own]

    up = grow(up, up_backs)
    up_backs = stage_swap(up, FEED, 1)
    down_back = swap(down, early[-1])
    wq, wk, wv, wo = assemble(spot, (mixed_both, *backs, near, *far), width)
    query, key, value = call(
        qkv_kernel,
        [like(2 * local_rows, width)] * 3,
        (span_input, wq, wk, wv, bias_q, bias_v),
        "query_key_value",
    )
    up_backs, down_back, query, key, value = tie(up_backs, down_back, query, key, value)
    up, up_both = grow_both(up, up_backs, 0)
    up_backs = stage_swap(up, FEED, 2)
    down = call(join_kernel, outs, (down, down_back), "join")
    down_backs = stage_swap(down, FEED, 0)
    up_near = swap(up_both, CORE)
    attended, branch, residual, mlp_input = call(
        attend_forward,
        [like(local_rows, width), like(local_rows, width, f32), like(local_rows, width, f32), like(local_rows, width)],
        (facts, query, key, value, wo, b_out, tokens, vectors),
        "attention_forward",
        scratch=[pltpu.VMEM((2 * HALF, width), bf16)] * 2,
        smem=1,
    )

    up_backs, up_near, down_backs, mlp_input = tie(up_backs, up_near, down_backs, mlp_input)
    up_far = core_swap(up_backs)
    down = grow(down, down_backs)
    down_backs = stage_swap(down, FEED, 1)
    up_far, down_backs, mlp_input = tie(up_far, down_backs, mlp_input)
    ups = up_both, *up_backs, up_near, *up_far
    act, slope = call(up_kernel, [like(local_rows, all_hidden)] * 2, (mlp_input, bias_up, *ups), "up")
    down, down_both = grow_both(down, down_backs, 0)
    down_backs = stage_swap(down, FEED, 2)
    down_near = swap(down_both, CORE)
    other = all_hidden // 2
    sizes = (up[0].shape[0], up[1].shape[0]) * 2
    sum_down = core_swap(products(act, grad_mlp, other, (other // 2,) * 2))
    down_backs, down_near, act = tie(down_backs, down_near, act)
    down_far = core_swap(down_backs)
    down_far, sum_down = tie(down_far, sum_down)
    downs = down_both, *down_backs, down_near, *down_far
    sum_down = products(act, grad_mlp, 0, sizes, sum_down)
    down_keeps, down_sends = sum_down[:2], sum_down[2:]
    sums_backs = stage_swap(down_sends, FEED, 2)
    grad_pre, grad_bias, output, output_sums = call(
        down_kernel,
        [like(local_rows, all_hidden), like(1, all_hidden, f32), like(local_rows, width), like(8, width, f32)],
        (grad_mlp, slope, act, residual, cotangent, vectors, b_down, *downs),
        "down",
        scratch=[pltpu.VMEM((local_rows, width), f32)],
    )
    (grad_mlp_input,) = call(back_kernel, [like(local_rows, width, f32)], (grad_pre, *ups), "grad_mlp_input")
    grad_residual, grad_branch, grad_attended, middle_sums = call(
        middle_kernel,
        [like(local_rows, width, f32), like(local_rows, width), like(local_rows, width), like(8, width, f32)],
        (grad_mlp_input, residual, branch, cotangent, vectors, wo),
        "grad_attended",
    )
    sum_up = products(grad_pre, mlp_input, other, (other,))
    down_backs, sum_up, grad_attended, grad_branch, grad_pre = tie(
        sums_backs, sum_up, grad_attended, grad_branch, grad_pre
    )
    sum_up = core_swap(sum_up)
    from_after = lax.ppermute(grad_branch[:HALF], "mp", back_to)
    from_before = lax.ppermute(grad_branch[HALF:], "mp", forth)

    full, half_full = pltpu.VMEM((2 * HALF, width), f32), pltpu.VMEM((2 * HALF, width), bf16)

    def attention_back(half, *operands):
        return call(
            lambda *refs: attend_backward(half, *refs),
            [like(local_rows, width), like(local_rows, width, f32), like(local_rows, width, f32)],
            (facts, query, key, value, grad_attended, *operands),
            "attention_backward",
            scratch=[half_full, half_full, full, full],
            smem=1,
        )

    first_half = attention_back(0)
    grad_query, own_key, own_value = attention_back(1, *first_half)
    sum_up, from_after, from_before, grad_query = tie(sum_up, from_after, from_before, grad_query)
    sum_up = products(grad_pre, mlp_input, 0, sizes, sum_up)
    up_keeps, up_sends = sum_up[:2], sum_up[2:]
    up_backs = stage_swap(up_sends, FEED, 2)
    from_after, from_before = lax.optimization_barrier(((from_after, from_before), up_sends))[0]
    grad_key, grad_value = call(
        attend_outside,
        [like(local_rows, width)] * 2,
        (facts, query, key, value, from_before, from_after, wo, own_key, own_value),
        "attention_outside",
        scratch=[half_full, half_full, pltpu.VMEM((HALF, width), bf16), full, full],
        smem=1,
    )
    lefts, rights = (grad_query, grad_key, grad_value, attended), (attn_input, grad_branch)
    sum_mixed = kind_products(1, spot, lefts, rights)
    up_backs, sum_mixed = tie(up_backs, sum_mixed)
    sum_mixed = core_swap(sum_mixed)
    feed_keeps, feed_sends = halve_join((*up_keeps, *down_keeps), (*up_backs, *down_backs))
    feed_backs = stage_swap(feed_sends, FEED, 1)
    grad_tokens, last_sums = call(
        last_kernel,
        [like(local_rows, width, f32), like(8, width, f32)],
        (grad_query, grad_key, grad_value, wq, wk, wv, tokens, vectors, grad_residual),
        "grad_tokens",
    )
    sum_mixed = kind_products(0, spot, lefts, rights, sum_mixed)
    mixed_keeps, mixed_sends = sum_mixed[0::2], sum_mixed[1::2]
    mixed_sends, last_sums = tie(mixed_sends, last_sums)
    feed_backs = lax.optimization_barrier((feed_backs, mixed_sends))[0]
    mixed_backs = stage_swap(mixed_sends, THIRDS, 2)
    feed_keeps, feed_sends = halve(feed_keeps, feed_backs, 2)
    feed_backs = stage_swap(feed_sends, FEED, 0)

    grad_bias = lax.optimization_barrier((grad_bias, feed_sends))[0]
    flat_up = lax.dot_general(
        source, grad_bias.reshape(granules, step), (((0,), (0,)), ((), ())), precision=highest
    ).reshape(model_ways, hidden)

    packed, plain = call(
        lambda *refs: pack_kernel(head_cols, *refs),
        [jax.ShapeDtypeStruct((model_ways, small_rows, small_lanes), f32), jax.ShapeDtypeStruct((1, 8, small_lanes), f32)],
        (number, shifts, last_sums, middle_sums, output_sums, flat_up),
        "pack_sums",
        scratch=[pltpu.VMEM((16, width), f32)],
        smem=2,
    )
    plain = jnp.pad(plain, ((0, 0), (0, small_rows - 8), (0, 0)))

    def gather_sums():
        buf, rest = packed.reshape((2,) * model_bits + (small_rows, small_lanes)), plain
        for bit in (0, 1, *range(2, model_bits)):
            axis = model_bits - 1 - joins.index(bit)
            keep, send = (lax.slice_in_dim(buf, k, k + 1, axis=axis) for k in (0, 1))
            send = jnp.concatenate([send.reshape(-1, small_rows, small_lanes), rest], 0).astype(bf16)
            back = yield swap(send, (0, 1 << bit))
            back = back.astype(f32)
            buf = keep + back[:-1].reshape(keep.shape)
            rest = send[-1:].astype(f32) + back[-1:]
        own = jnp.concatenate([buf.reshape(small_rows, small_lanes), rest[0, :8]], 0).astype(bf16)
        others = yield [swap(own, (d, 0)) for d in range(1, data_ways)]
        yield jnp.stack([own, *others], 0)

    mixed_backs, packed, plain = tie(mixed_backs, packed, plain)
    chain = gather_sums()
    steps = model_bits + 1
    small = next(chain)
    mixed_keeps, mixed_sends = halve(mixed_keeps, mixed_backs)
    mixed_backs = stage_swap(mixed_sends, THIRDS, 1)
    merged_rows = feed_count << len(early) - 1
    feed_keep, feed_send = merge(merge_rows_kernel, feed_keeps, feed_backs, merged_rows, 2 * width)
    feed_back = swap(feed_send, early[-1])
    mixed_backs, small = tie(mixed_backs, small)
    small = chain.send(small)
    steps -= 1
    mixed_keeps, mixed_sends = halve(mixed_keeps, mixed_backs)
    mixed_backs = stage_swap(mixed_sends, THIRDS, 0)
    feed_done = added(feed_keep, feed_back)
    for bits in reversed(early[:-1]):
        keep, send = halves(feed_done)
        feed_done = added(keep, swap(send, bits))
    feed_done = jnp.stack([feed_done[:, :width], feed_done[:, width:]], 0)
    for level in reversed(range(2, data_bits)):
        feed_done = lanes_sum(feed_done, level, data_index)
    mixed_backs, feed_done, small = tie(mixed_backs, feed_done, small)
    small = chain.send(small)
    steps -= 1
    merged_rows = head_cols << len(early) - 1
    mixed_keep, mixed_send = merge(merge_lanes_kernel, mixed_keeps, mixed_backs, merged_rows, width)
    mixed_back = swap(mixed_send, early[-1])
    feed_keep, feed_back = lanes_send(feed_done, 1, data_index)
    mixed_back, feed_back, small = tie(mixed_back, feed_back, small)
    small = chain.send(small)
    steps -= 1
    mixed_done = added(mixed_keep, mixed_back)
    for bits in reversed(early[:-1]):
        keep, send = halves(mixed_done)
        mixed_done = added(keep, swap(send, bits))
    for level in reversed(range(2, data_bits)):
        mixed_done = lanes_sum(mixed_done, level, data_index)
    keep, back = lanes_send(mixed_done, 1, data_index)
    feed_done = rows_join(feed_keep, feed_back, 1, data_index, 0)
    feed_keep, feed_back = lanes_send(feed_done, 0, data_index)
    back, feed_back, small = tie(back, feed_back, small)
    small = chain.send(small)
    steps -= 1
    mixed_done = rows_join(keep, back, 1, data_index, 0)
    keep, back = lanes_send(mixed_done, 0, data_index)
    feed_done = rows_join(feed_keep, feed_back, 0, data_index, 1).reshape(4, 2, feed_count, lanes)
    for _ in range(steps):
        small = chain.send(small)
    mixed_done = rows_join(keep, back, 0, data_index, 1).reshape(4, head_cols, lanes)
    grad_modulation = small[:, :images, : 6 * head_cols]
    rest = tree_sum(small[:, small_rows - 1 :].astype(f32))
    grad_w_ada = tn(
        cond_act.reshape(data_ways * images, lanes),
        grad_modulation.reshape(data_ways * images, 6 * head_cols),
    )
    grad_w_ada = grad_w_ada.reshape(lanes, 6, head_cols)
    grad_b_ada = tree_sum(jnp.sum(grad_modulation, axis=1, dtype=f32)).reshape(6, head_cols)
    per = -(-width // small_lanes)
    grad_b_out, grad_b_down = (rest[1 + k * per : 1 + (k + 1) * per].reshape(-1)[:width] for k in range(2))
    own_bias = rest[0, : 6 * head_cols]
    grad_b_qv, grad_b_up = own_bias[: 2 * head_cols].reshape(2, head_cols), own_bias[2 * head_cols :]

    grad_w_up, grad_w_down = call(
        place_feed_kernel, [like(lanes, hidden, f32)] * 2, (feed_done,), "place_feed_forward"
    )
    grad_w_down = jnp.swapaxes(grad_w_down, 0, 1)
    mixed_done = mixed_done.astype(f32)
    grad_w_qkv, grad_w_out = jnp.swapaxes(mixed_done[:3], 1, 2), mixed_done[3]
    return (
        output,
        grad_tokens,
        grad_w_ada,
        grad_b_ada,
        grad_w_qkv,
        grad_b_qv,
        grad_w_out,
        grad_b_out,
        grad_w_up,
        grad_b_up,
        grad_w_down,
        grad_b_down,
    )


def solution(mesh):
    in_specs = (
        P(("dp", "mp"), None),
        P("dp", None),
        P("dp"),
        P("dp", None, "mp"),
        P(None, "mp"),
        P(None, "dp", "mp"),
        P(None, "mp"),
        P("mp", "dp"),
        P(),
        P("dp", "mp"),
        P("mp"),
        P("mp", "dp"),
        P(),
        P(("dp", "mp"), None),
    )
    out_specs = (
        P(("dp", "mp"), None),
        P(("dp", "mp"), None),
        P("dp", None, "mp"),
        P(None, "mp"),
        P(None, "dp", "mp"),
        P(None, "mp"),
        P("mp", "dp"),
        P(),
        P("dp", "mp"),
        P("mp"),
        P("mp", "dp"),
        P(),
    )
    return jax.shard_map(
        on_device, mesh=mesh, in_specs=in_specs, out_specs=out_specs, check_vma=False
    )
```

```python
import itertools
import math

import jax
import jax.numpy as jnp
import numpy as np
from jax import lax
from jax.experimental import pallas as pl
from jax.experimental.pallas import tpu as pltpu
from jax.sharding import PartitionSpec as P

HD = 72
HALF = 128
LANE = 128
EPS = 1e-06
HIDE = -1e30

f32, bf16 = jnp.float32, jnp.bfloat16
highest = lax.Precision.HIGHEST

CORE, Y, X, Z1 = (1, 0), (2, 0), (0, 1), (0, 2)


def swap(values, even, odd=None):
    odd = even if odd is None else odd
    data_ways, model_ways = lax.axis_size("dp"), lax.axis_size("mp")
    pairs = []
    for d in range(data_ways):
        d_bits, m_bits = odd if d % 2 else even
        for m in range(model_ways):
            pairs.append((d * model_ways + m, (d ^ d_bits) * model_ways + (m ^ m_bits)))
    return lax.ppermute(values, ("dp", "mp"), pairs)


def bits_of(count):
    return count.bit_length() - 1


def pick(values, axis, index):
    low, high = (lax.index_in_dim(values, k, axis, keepdims=False) for k in (0, 1))
    return jnp.where(index == 0, low, high)


def nn(a, b):
    return jnp.dot(a, b, preferred_element_type=f32)


def nt(a, b):
    return lax.dot_general(a, b, (((1,), (1,)), ((), ())), preferred_element_type=f32)


def tn(a, b):
    return lax.dot_general(a, b, (((0,), (0,)), ((), ())), preferred_element_type=f32)


def head_windows(width):
    for head in range(width // HD):
        first, last = head * HD, head * HD + HD
        low = first // LANE * LANE
        high = -(-last // LANE) * LANE
        yield first, last, low, high


def lane_mask(first, last, low, high):
    lane = lax.broadcasted_iota(jnp.int32, (HALF, high - low), 1) + low
    return (lane >= first) & (lane < last)


def same_segment(paired, seated):
    row = lax.broadcasted_iota(jnp.int32, (HALF, 2 * HALF), 0)
    col = lax.broadcasted_iota(jnp.int32, (HALF, 2 * HALF), 1)
    own = (col < HALF) & ((row == col) | (seated > 0))
    return own | ((col >= HALF) & (paired > 0))


def same_segment_keys(paired, seated):
    key = lax.broadcasted_iota(jnp.int32, (2 * HALF, HALF), 0)
    col = lax.broadcasted_iota(jnp.int32, (2 * HALF, HALF), 1)
    own = (key < HALF) & ((key == col) | (seated > 0))
    return own | ((key >= HALF) & (paired > 0))


def split_rows(rows):
    return pl.ds(rows * HALF, HALF)


def row(vectors, kind, half):
    return vectors[4 * kind + half : 4 * kind + half + 1]


def normalize(values):
    centred = values - jnp.mean(values, axis=-1, keepdims=True)
    spread = jnp.mean(centred * centred, axis=-1, keepdims=True)
    root = lax.rsqrt(spread + EPS)
    return centred * root, root


def normalize_back(norm, root, upstream):
    return (
        upstream
        - jnp.mean(upstream, axis=-1, keepdims=True)
        - norm * jnp.mean(upstream * norm, axis=-1, keepdims=True)
    ) * root


def column_sum(values):
    return jnp.sum(values, axis=0, keepdims=True)


def vectors_kernel(columns, images, shifts, buf, out, part):
    part[...] = jnp.zeros(part.shape, f32)
    for block in range(buf.shape[0]):
        for half in range(4):
            number = lax.broadcasted_iota(jnp.int32, buf.shape[1:], 0)
            vector = column_sum(jnp.where(number == images[half], buf[block], 0.0))
            for kind in range(6):
                part[4 * kind + half : 4 * kind + half + 1, :columns] = vector[:, kind * columns : (kind + 1) * columns]
        moved = pltpu.roll(part[...], shifts[block] * columns, 1)
        out[...] = moved if block == 0 else out[...] + moved


def pack_kernel(columns, images, shifts, last, middle, output, bias_up, out, plain, rows):
    count, _, lanes = out.shape
    bias_row = out.shape[1] - 1
    width = rows.shape[1]
    rows[...] = jnp.zeros(rows.shape, f32)
    rows[0:4], rows[4:10], rows[10:12] = last[0:4], middle[0:6], output[0:2]
    out[...] = jnp.zeros(out.shape, f32)
    plain[...] = jnp.zeros(plain.shape, f32)
    for block in range(count):
        moved = pltpu.roll(rows[...], jnp.where(shifts[block] > 0, width - shifts[block] * columns, 0), 1)
        number = lax.broadcasted_iota(jnp.int32, (out.shape[1], columns), 0)
        for kind in range(6):
            place = slice(kind * columns, (kind + 1) * columns)
            low, high = (moved[2 * kind + half : 2 * kind + half + 1, :columns] for half in range(2))
            out[block, :, place] = jnp.where(number == images[1], low, 0.0) + jnp.where(number == images[2], high, 0.0)
        mine = slice(block * columns, (block + 1) * columns)
        out[block, bias_row : bias_row + 1, :columns] = last[4:5, mine]
        out[block, bias_row : bias_row + 1, columns : 2 * columns] = last[5:6, mine]
        out[block, bias_row : bias_row + 1, 2 * columns : 6 * columns] = bias_up[block : block + 1]
    per = -(-width // lanes)
    for k, source in enumerate((middle[6:7], output[2:3])):
        for piece in range(per):
            size = min(lanes, width - piece * lanes)
            plain[0, k * per + piece : k * per + piece + 1, :size] = source[:, piece * lanes : piece * lanes + size]


def span_kernel(before, tokens, after, vectors, out):
    for half in range(4):
        source = (before, tokens, tokens, after)[half]
        norm, _ = normalize(source[split_rows(half == 2)].astype(f32))
        out[split_rows(half)] = (norm * (1.0 + row(vectors, 1, half)) + row(vectors, 0, half)).astype(bf16)


def qkv_kernel(span, wq, wk, wv, bias_q, bias_v, query, key, value):
    query[...] = (nt(span[...], wq[...]) + bias_q[...]).astype(bf16)
    key[...] = nt(span[...], wk[...]).astype(bf16)
    value[...] = (nt(span[...], wv[...]) + bias_v[...]).astype(bf16)


def attend_forward(
    facts, q_ref, k_ref, v_ref, wo, b_out, tokens, vectors, o_ref, branch_ref, residual_ref, input_ref, kk, vv
):
    factor = HD ** (-0.5)
    for half in range(2):
        rows = split_rows(half)
        own = split_rows(half + 1)
        other = pl.ds(pl.multiple_of(facts[3 * half] * HALF, HALF), HALF)
        kk[0:HALF], kk[HALF:] = k_ref[own], k_ref[other]
        vv[0:HALF], vv[HALF:] = v_ref[own], v_ref[other]
        same = same_segment(facts[3 * half + 1], facts[3 * half + 2])
        for first, last, low, high in head_windows(q_ref.shape[1]):
            window = slice(low, high)
            mask = lane_mask(first, last, low, high)
            query = jnp.where(mask, q_ref[own, window], 0)
            scores = jnp.where(same, nt(query, kk[:, window]) * factor, HIDE)
            exp_scores = jnp.exp(scores - jnp.max(scores, axis=1, keepdims=True))
            prob = exp_scores * (1.0 / jnp.sum(exp_scores, axis=1, keepdims=True))
            mixed = nn(prob.astype(bf16), vv[:, window]).astype(bf16)
            o_ref[rows, window] = jnp.where(mask, mixed, o_ref[rows, window]) if first > low else mixed
    for half in range(2):
        rows = split_rows(half)
        branch = nn(o_ref[rows], wo[...]) + b_out[...]
        branch_ref[rows] = branch
        residual = tokens[rows].astype(f32) + row(vectors, 2, half + 1) * branch
        residual_ref[rows] = residual
        norm, _ = normalize(residual)
        input_ref[rows] = (norm * (1.0 + row(vectors, 4, half + 1)) + row(vectors, 3, half + 1)).astype(bf16)


def score_gradients(query, grad, keys, values, same):
    scores = nt(keys, query) * HD ** (-0.5)
    if same is not None:
        scores = jnp.where(same, scores, HIDE)
    exp_scores = jnp.exp(scores - jnp.max(scores, axis=0, keepdims=True))
    prob = exp_scores * (1.0 / jnp.sum(exp_scores, axis=0, keepdims=True))
    grad_prob = nt(values, grad)
    inner = jnp.sum(grad_prob * prob, axis=0, keepdims=True)
    return prob.astype(bf16), (prob * (grad_prob - inner)).astype(bf16)


def attend_backward(half, facts, q_ref, k_ref, v_ref, g_ref, *refs):
    earlier, refs = (refs[:3], refs[3:]) if half else (None, refs)
    dq_ref, own_k, own_v, kk, vv, dkk, dvv = refs
    factor = HD ** (-0.5)
    rows = split_rows(half)
    own = split_rows(half + 1)
    other = pl.ds(pl.multiple_of(facts[3 * half] * HALF, HALF), HALF)
    kk[0:HALF], kk[HALF:] = k_ref[own], k_ref[other]
    vv[0:HALF], vv[HALF:] = v_ref[own], v_ref[other]
    dkk[...] = jnp.zeros(dkk.shape, f32)
    dvv[...] = jnp.zeros(dvv.shape, f32)
    if half:
        dq_ref[0:HALF] = earlier[0][0:HALF]
    same = same_segment_keys(facts[3 * half + 1], facts[3 * half + 2])
    for first, last, low, high in head_windows(q_ref.shape[1]):
        window = slice(low, high)
        mask = lane_mask(first, last, low, high)
        query = jnp.where(mask, q_ref[own, window], 0)
        grad = jnp.where(mask, g_ref[rows, window], 0)
        prob, grad_scores = score_gradients(query, grad, kk[:, window], vv[:, window], same)
        dq = (tn(grad_scores, kk[:, window]) * factor).astype(bf16)
        dq_ref[rows, window] = jnp.where(mask, dq, dq_ref[rows, window]) if first > low else dq
        dkk[:, window] += nn(grad_scores, query) * factor
        dvv[:, window] += nn(prob, grad)
    inside = jnp.where(facts[3 * half] == 2 - half, 1.0, 0.0)
    for place, (total, mine) in enumerate(((dkk, own_k), (dvv, own_v))):
        mine_own, mine_other = total[0:HALF], total[HALF:] * inside
        if half:
            mine_own = mine_own + earlier[1 + place][split_rows(half)]
            mine_other = mine_other + earlier[1 + place][split_rows(1 - half)]
        mine[split_rows(half)], mine[split_rows(1 - half)] = mine_own, mine_other


def attend_outside(
    facts, q_ref, k_ref, v_ref, before, after, wo, own_k, own_v, key_ref, value_ref, kk, vv, grads, dk, dv
):
    factor = HD ** (-0.5)
    dk[...], dv[...] = own_k[...], own_v[...]
    for half, (outside, branch) in enumerate(((0, before), (3, after))):

        @pl.when((facts[3 * half] == outside) & (facts[3 * half + 1] > 0))
        def _():
            mine, theirs = split_rows(half), split_rows(outside)
            kk[0:HALF], kk[HALF:] = k_ref[theirs], k_ref[split_rows(half + 1)]
            vv[0:HALF], vv[HALF:] = v_ref[theirs], v_ref[split_rows(half + 1)]
            grads[...] = nt(branch[...], wo[...]).astype(bf16)
            for first, last, low, high in head_windows(q_ref.shape[1]):
                window = slice(low, high)
                mask = lane_mask(first, last, low, high)
                query = jnp.where(mask, q_ref[theirs, window], 0)
                grad = jnp.where(mask, grads[:, window], 0)
                prob, grad_scores = score_gradients(query, grad, kk[:, window], vv[:, window], None)
                dk[mine, window] += nn(grad_scores[HALF:], query) * factor
                dv[mine, window] += nn(prob[HALF:], grad)

    key_ref[...], value_ref[...] = dk[...].astype(bf16), dv[...].astype(bf16)


def middle_kernel(
    grad_input, residual, branch, cotangent, vectors, wo, grad_residual, grad_branch, grad_attended, sums
):
    sums[...] = jnp.zeros(sums.shape, f32)
    for half in range(2):
        rows = split_rows(half)
        norm, root = normalize(residual[rows])
        grad = grad_input[rows]
        total = cotangent[rows].astype(f32) + normalize_back(norm, root, grad * (1.0 + row(vectors, 4, half + 1)))
        grad_residual[rows] = total
        low = (row(vectors, 2, half + 1) * total).astype(bf16)
        grad_branch[rows] = low
        grad_attended[rows] = nt(low, wo[...]).astype(bf16)
        sums[half : half + 1] = column_sum(total * branch[rows])
        sums[2 + half : 3 + half] = column_sum(grad)
        sums[4 + half : 5 + half] = column_sum(grad * norm)
        sums[6:7] += column_sum(low.astype(f32))


def last_kernel(
    grad_query, grad_key, grad_value, wq, wk, wv, tokens, vectors, grad_residual, grad_tokens, sums
):
    sums[...] = jnp.zeros(sums.shape, f32)
    for half in range(2):
        rows = split_rows(half)
        norm, root = normalize(tokens[rows].astype(f32))
        grad = nn(grad_query[rows], wq[...]) + nn(grad_key[rows], wk[...]) + nn(grad_value[rows], wv[...])
        back = normalize_back(norm, root, grad * (1.0 + row(vectors, 1, half + 1)))
        grad_tokens[rows] = grad_residual[rows] + back
        sums[half : half + 1] = column_sum(grad)
        sums[2 + half : 3 + half] = column_sum(grad * norm)
        sums[4:5] += column_sum(grad_query[rows].astype(f32))
        sums[5:6] += column_sum(grad_value[rows].astype(f32))


VMEM = pl.BlockSpec(memory_space=pltpu.VMEM)
SMEM = pl.BlockSpec(memory_space=pltpu.SMEM)


CHUNK = 96
HINT = pl.CostEstimate(flops=1, bytes_accessed=1, transcendentals=0)


def call(kernel, outs, operands, name, scratch=(), smem=0):
    room = sum(math.prod(v.shape) * v.dtype.itemsize for v in (*scratch, *outs) if hasattr(v, "shape")) + 4 * 2**20
    return pl.pallas_call(
        kernel,
        out_shape=tuple(outs),
        in_specs=[SMEM] * smem + [VMEM] * (len(operands) - smem),
        out_specs=tuple(VMEM for _ in outs),
        scratch_shapes=list(scratch),
        compiler_params=pltpu.CompilerParams(vmem_limit_bytes=room),
        cost_estimate=HINT,
        name=name,
    )(*operands)


def like(rows, width, dtype=bf16):
    return jax.ShapeDtypeStruct((rows, width), dtype)


def grow_kernel(refs, axis=None):
    count = (len(refs) - (axis is not None)) // 3
    both, place = refs[-1], 0
    for own, back, out in zip(refs[:count], refs[count : 2 * count], refs[2 * count : 3 * count]):
        rows, lanes = own.shape
        out[:rows], out[rows:] = own[...], back[...]
        if axis == 0:
            both[place : place + rows], both[place + rows : place + 2 * rows] = own[...], back[...]
            place += 2 * rows
        if axis == 1:
            both[:rows, place : place + lanes], both[rows:, place : place + lanes] = own[...], back[...]
            place += lanes


def grow(parts, backs):
    outs = [like(2 * part.shape[0], part.shape[1]) for part in parts]
    return call(lambda *refs: grow_kernel(refs), outs, (*parts, *backs), "grow")


def grow_both(parts, backs, axis):
    outs = [like(2 * part.shape[0], part.shape[1]) for part in parts]
    if axis == 0:
        both = like(sum(out.shape[0] for out in outs), outs[0].shape[1])
    else:
        both = like(outs[0].shape[0], sum(out.shape[1] for out in outs))
    outs = call(lambda *refs: grow_kernel(refs, axis), [*outs, both], (*parts, *backs), "grow_both")
    return outs[:-1], outs[-1]


def row_sum(keep, back, first, last):
    return keep[first:last] + back[first:last]


def halve_kernel(groups, side, *refs):
    count = len(refs) // 3
    for keep, back, out in zip(refs[:count], refs[count : 2 * count], refs[2 * count :]):
        rows = keep.shape[0] // (2 * groups)
        for group in range(groups):
            base = (2 * group + side) * rows
            for first in range(0, rows, CHUNK):
                last = min(first + CHUNK, rows)
                out[group * rows + first : group * rows + last] = row_sum(keep, back, base + first, base + last)


def halve(keeps, backs, groups=1):
    outs = [like(keep.shape[0] // 2, keep.shape[1]) for keep in keeps]
    high, low = (
        call(lambda *refs, side=side: halve_kernel(groups, side, *refs), outs, (*keeps, *backs), "halve")
        for side in (1, 0)
    )
    return low, high


def halve_join_kernel(side, *refs):
    count = len(refs) // 5
    keeps, backs, outs = refs[: 2 * count], refs[2 * count : 4 * count], refs[4 * count :]
    for k in range(count):
        for which in range(2):
            keep, back = keeps[which * count + k], backs[which * count + k]
            rows = keep.shape[0] // 2
            for first in range(0, rows, CHUNK):
                last = min(first + CHUNK, rows)
                outs[k][which * rows + first : which * rows + last] = row_sum(
                    keep, back, side * rows + first, side * rows + last
                )


def halve_join(keeps, backs):
    outs = [like(keep.shape[0], keep.shape[1]) for keep in keeps[: len(keeps) // 2]]
    high, low = (
        call(lambda *refs, side=side: halve_join_kernel(side, *refs), outs, (*keeps, *backs), "halve_join")
        for side in (1, 0)
    )
    return low, high


def merge_rows_kernel(*refs):
    count = (len(refs) - 2) // 2
    low, high = refs[2 * count :]
    rows, width = low.shape[0], low.shape[1] // 2
    for which in range(2):
        lanes = slice(which * width, (which + 1) * width)
        place = 0
        for keep, back in zip(refs[:count], refs[count : 2 * count]):
            first, end = which * keep.shape[0] // 2, (which + 1) * keep.shape[0] // 2
            while first < end:
                out, base = (low, 0) if place < rows else (high, rows)
                step = min(end - first, base + rows - place)
                out[place - base : place - base + step, lanes] = row_sum(keep, back, first, first + step)
                first, place = first + step, place + step


def merge_lanes_kernel(*refs):
    count = (len(refs) - 2) // 2
    low, high = refs[2 * count :]
    rows, lane = low.shape[0], 0
    for keep, back in zip(refs[:count], refs[count : 2 * count]):
        lanes = slice(lane, lane + keep.shape[1])
        lane += keep.shape[1]
        low[:, lanes], high[:, lanes] = row_sum(keep, back, 0, rows), row_sum(keep, back, rows, 2 * rows)


def merge(kernel, keeps, backs, rows, width):
    return call(kernel, [like(rows, width)] * 2, (*keeps, *backs), "merge")


def row_steps(weights):
    unit = 0
    for weight in weights:
        rows = weight.shape[0]
        step = 256 if rows % 256 == 0 else 384
        for first in range(0, rows, step):
            yield weight, first, first + step, unit + first
        unit += rows


def up_kernel(x_ref, bias_ref, *refs):
    weights, (act_ref, slope_ref) = refs[:-2], refs[-2:]
    for weight, first, last, unit in row_steps(weights):
        units = slice(unit, unit + last - first)
        pre = nt(x_ref[...], weight[first:last]) + bias_ref[:, units]
        square = pre * pre
        inner = jnp.tanh(0.7978845608028654 * pre * (1.0 + 0.044715 * square))
        outer = 0.5 * (1.0 + inner)
        act_ref[:, units] = (pre * outer).astype(bf16)
        rise = (0.5 * 0.7978845608028654) * pre * (1.0 + (3 * 0.044715) * square)
        slope_ref[:, units] = (outer + rise * (1.0 - inner * inner)).astype(bf16)


def down_kernel(grad_mlp, slope, act, residual, cotangent, vectors, b_down, *refs):
    weights, (pre_ref, sum_ref, out, sums, total) = refs[:-5], refs[-5:]
    for weight, first, last, unit in row_steps(weights):
        units = slice(unit, unit + last - first)
        pre = (nt(grad_mlp[...], weight[first:last]) * slope[:, units].astype(f32)).astype(bf16)
        pre_ref[:, units] = pre
        sum_ref[:, units] = column_sum(pre.astype(f32))
    back_kernel(act, *weights, total)
    sums[...] = jnp.zeros(sums.shape, f32)
    for half in range(2):
        rows = split_rows(half)
        mlp = total[rows] + b_down[...]
        out[rows] = (residual[rows] + row(vectors, 5, half + 1) * mlp).astype(bf16)
        sums[half : half + 1] = column_sum(cotangent[rows].astype(f32) * mlp)
        sums[2:3] += column_sum(grad_mlp[rows].astype(f32))


def back_kernel(left_ref, *refs):
    weights, out_ref = refs[:-1], refs[-1]
    unit = 0
    for weight in weights:
        rows = weight.shape[0]
        part = nn(left_ref[:, unit : unit + rows], weight[...])
        out_ref[...] = part if unit == 0 else out_ref[...] + part
        unit += rows


def join_kernel(own, back, wide, narrow):
    rows = own.shape[0]
    more = wide.shape[0] - rows
    wide[:rows], wide[rows:] = own[...], back[:more]
    narrow[...] = back[more:]


def place_feed_kernel(done, grad_up, grad_down):
    for which, out in enumerate((grad_up, grad_down)):
        out[...] = jnp.concatenate([done[way, which] for way in range(done.shape[0])], 0).astype(f32).T


def gate_kernel(cotangent, vectors, out):
    for half in range(2):
        rows = split_rows(half)
        out[rows] = (row(vectors, 5, half + 1) * cotangent[rows].astype(f32)).astype(bf16)


def product_kernel(start, count, left_ref, right_ref, *refs):
    backs, outs = refs[:-count], refs[-count:]
    base = 0
    for out in outs:
        size = out.shape[0]
        step = 384 if backs or size % 256 else 256
        for first in range(0, size, step):
            column = base + first
            part = tn(left_ref[:, start + column : start + column + step], right_ref[...])
            if backs:
                rows = backs[0].shape[0]
                back = backs[column // rows]
                part = part + back[column % rows : column % rows + step].astype(f32)
            out[first : first + step] = part.astype(bf16)
        base += size


def products(left, right, start, counts, backs=()):
    outs = [like(size, right.shape[1]) for size in counts]
    kernel = lambda *refs: product_kernel(start, len(counts), *refs)
    return call(kernel, outs, (left, right, *backs), "products")


def unit_of(third, y, z, x):
    return ((x, 2 * y + z), (y, 2 * z + x), (z, 2 * x + y))[third]


def assemble_kernel(spot, *refs):
    sides, outs = (refs[:4], refs[4:8]), refs[8:]
    unit = outs[0].shape[0] // 4
    width = outs[0].shape[1] // 3

    def place(core, why):
        for kind, out in enumerate(outs):
            side, y = (kind & 1) ^ core, (kind >> 1) ^ why
            for third in range(3):
                lanes = slice(third * width, (third + 1) * width)
                for z in range(2):
                    for x in range(2):
                        array, index = unit_of(third, y, z, x)
                        rows = slice(index * unit, (index + 1) * unit)
                        source = sides[side][1 + third][rows] if array else sides[side][0][rows, lanes]
                        out[(2 * z + x) * unit : (2 * z + x + 1) * unit, lanes] = source

    for core in range(2):
        for why in range(2):
            pl.when((spot[0] == core) & (spot[1] == why))(lambda core=core, why=why: place(core, why))


def assemble(spot, arrays, width):
    return call(assemble_kernel, [like(width, width)] * 4, (spot, *arrays), "assemble", smem=1)


def kinds_kernel(side, spot, *refs):
    lefts, rights, refs, left, right = refs[:4], refs[4:6], refs[6:-2], refs[-2], refs[-1]
    back, outs = (None, refs) if side else (refs[0], refs[1:])
    width = left.shape[1]
    unit, third_width = width // 4, width // 3
    for y in range(2):
        kind = (spot[1] ^ y) * 2 + (spot[0] ^ side)
        for k in range(4):

            @pl.when(kind == k)
            def _():
                left[...] = lefts[k][...]
                right[...] = rights[k == 3][...]

        for third in range(3):
            lanes = slice(third * third_width, (third + 1) * third_width)
            part = tn(left[...], right[:, lanes])
            for z in range(2):
                for x in range(2):
                    array, index = unit_of(third, y, z, x)
                    rows = slice(index * unit, (index + 1) * unit)
                    both_rows = slice(array * width + index * unit, array * width + (index + 1) * unit)
                    piece = part[(2 * z + x) * unit : (2 * z + x + 1) * unit]
                    if side:
                        outs[0][both_rows, lanes] = piece.astype(bf16)
                    else:
                        piece = piece + back[both_rows, lanes].astype(f32)
                        outs[2 * third + array][rows] = piece.astype(bf16)


def kind_products(side, spot, lefts, rights, backs=()):
    rows, width = lefts[0].shape
    return call(
        lambda *refs: kinds_kernel(side, *refs),
        [like(2 * width, width)] if side else [like(width, width // 3)] * 6,
        (spot, *lefts, *rights, *backs),
        "kind_products",
        scratch=[pltpu.VMEM((rows, width), bf16)] * 2,
        smem=1,
    )


def rows_send(parts, axis, level, data_index):
    bit = (data_index >> level) & 1
    return pick(parts, axis, bit), swap(pick(parts, axis, 1 - bit), (1 << level, 0))


def lanes_join(keep, back, level, data_index):
    bit = (data_index >> level) & 1
    return jnp.where(bit == 0, jnp.concatenate([keep, back], -1), jnp.concatenate([back, keep], -1))


def lanes_split(block, level, data_index):
    bit = (data_index >> level) & 1
    width = block.shape[-1] // 2
    low, high = block[..., :width], block[..., width:]
    return jnp.where(bit == 0, low, high), jnp.where(bit == 0, high, low)


def lanes_send(block, level, data_index):
    keep, send = lanes_split(block, level, data_index)
    return keep, swap(send, (1 << level, 0))


def lanes_sum(block, level, data_index):
    keep, send = lanes_split(block, level, data_index)
    return added(keep, swap(send, (1 << level, 0)))


def rows_join(keep, back, level, data_index, lead):
    bit = (data_index >> level) & 1
    return jnp.where(bit == 0, jnp.stack([keep, back], lead), jnp.stack([back, keep], lead))


def halves(buf):
    size = buf.shape[0] // 2
    return buf[:size], buf[size:]


def added(keep, back):
    return (keep.astype(f32) + back.astype(f32)).astype(bf16)


def tree_sum(values):
    while values.shape[0] > 1:
        half = values.shape[0] // 2
        values = values[:half] + values[half:]
    return values[0]


def tie(*values):
    return lax.optimization_barrier(values) if len(values) > 1 else lax.optimization_barrier(values[0])


FEED = (((X, Y), (Y, Z1), (Z1, X)), ((Z1, Z1), (X, X), (Y, Y)))
THIRDS = tuple(tuple((bits, bits) for bits in order) for order in ((Z1, Y, X), (X, Z1, Y), (Y, X, Z1)))


def early_bits(model_bits):
    return [(0, 1 << k) for k in range(2, model_bits)]


def stage_swap(parts, plan, stage):
    return tuple(swap(part, *table[stage]) for part, table in zip(parts, plan))


def core_swap(parts):
    return tuple(swap(part, CORE) for part in parts)


def early_join(buf, bits):
    return jnp.concatenate([buf, swap(buf, bits)], 0)


def join_order(model_bits):
    return [*range(2, model_bits), 0, 1]


def join_masks(model_bits):
    joins = join_order(model_bits)
    return [sum(((place >> k) & 1) << bit for k, bit in enumerate(joins)) for place in range(1 << model_bits)]


def feed_places(rows, model_bits):
    early = early_bits(model_bits)
    unit_rows = rows << len(early)
    cut = unit_rows * 2 // 3
    step = math.gcd(rows, cut)
    tables = []
    for core in range(2):
        places = []
        spans = range(0, cut, step), range(cut, unit_rows, step)
        for side, last, (table, span), *bits in itertools.product(
            range(2), range(2), list(zip(FEED, spans)), range(2), range(2)
        ):
            d, m = side, 0
            for bit, stage in zip((last, *bits), reversed(table)):
                d, m = d ^ bit * stage[core ^ side][0], m ^ bit * stage[core ^ side][1]
            for row in span:
                block, m_row = row // rows, m
                for level, (_, m_bits) in enumerate(early):
                    m_row = m_row ^ ((block >> level) & 1) * m_bits
                places.append((join_masks(model_bits).index(m_row), d, row % rows // step))
        tables.append(np.array(places, np.int32))
    return step, tables


def one_hot_rows(index, count):
    return (index[:, None] == jnp.arange(count, dtype=jnp.int32)[None]).astype(f32)


def on_device(
    tokens,
    conditioning,
    lengths,
    w_ada,
    b_ada,
    w_qkv,
    b_qv,
    w_out,
    b_out,
    w_up,
    b_up,
    w_down,
    b_down,
    cotangent,
):
    data_ways, model_ways = lax.axis_size("dp"), lax.axis_size("mp")
    data_index, model_index = lax.axis_index("dp"), lax.axis_index("mp")
    data_bits, model_bits = bits_of(data_ways), bits_of(model_ways)
    early = early_bits(model_bits)
    local_rows, width = tokens.shape
    lanes = width // data_ways
    head_cols = w_qkv.shape[2]
    hidden = w_up.shape[1]
    images = lengths.shape[0]
    binary = (2,) * data_bits
    feed_count = hidden // 4
    all_hidden = hidden * model_ways
    spot = jnp.stack([data_index & 1, (data_index >> 1) & 1]).astype(jnp.int32)
    forth = [(k, k + 1) for k in range(model_ways - 1)]
    back_to = [(k + 1, k) for k in range(model_ways - 1)]

    mixed = jnp.concatenate([jnp.swapaxes(w_qkv, 1, 2), w_out[None]], 0).reshape(2, 2, 1, head_cols, lanes)
    keep, back = rows_send(mixed, 1, 0, data_index)
    feed = jnp.stack([jnp.swapaxes(w_up, 0, 1), w_down], 0).reshape(2, 2, 2, feed_count, lanes)
    feed_keep, feed_back = rows_send(feed, 2, 0, data_index)
    others = [swap(conditioning, (d, 0)) for d in range(1, data_ways)]
    back, feed_back, others = tie(back, feed_back, others)
    cond = jnp.stack([conditioning, *others], 0)
    mixed = lanes_join(keep, back, 0, data_index)
    joins = join_order(model_bits)
    small_rows, small_lanes = -(-(images + 1) // 8) * 8, -(-6 * head_cols // LANE) * LANE

    def modulate(cond):
        part = lax.dynamic_slice_in_dim(cond, data_index * lanes, lanes, 2).astype(f32)
        cond_act = jax.nn.silu(part).astype(bf16)
        mod = nn(cond_act.reshape(data_ways * images, lanes), w_ada.reshape(lanes, 6 * head_cols))
        mod = mod.reshape(data_ways, images, 6 * head_cols)
        backs = yield [swap(mod[d], (d, 0)) for d in range(1, data_ways)]
        mod = sum(backs, mod[0]) + b_ada.astype(f32).reshape(1, 6 * head_cols)
        biases = jnp.concatenate([b_qv.reshape(-1), b_up], 0).astype(f32)
        buf = jnp.pad(mod, ((0, small_rows - images), (0, small_lanes - 6 * head_cols)))
        bias = jnp.pad(biases[None], ((small_rows - 1, 0), (0, small_lanes - 6 * head_cols)))
        buf = (buf + bias)[None]
        for bit in joins:
            back = yield swap(buf, (0, 1 << bit))
            buf = jnp.concatenate([buf, back], 0)
        yield (cond_act, buf)

    steps = 1 + model_bits

    for k, bits in enumerate(early):
        back = swap(mixed, bits)
        if k == 0:
            feed = lanes_join(feed_keep, feed_back, 0, data_index)
            feed_keep, feed_back = rows_send(feed, 1, 1, data_index)
            chain = modulate(cond)
            small = next(chain)
            back, feed_back, small = tie(back, feed_back, small)
            small = chain.send(small)
            steps -= 1
        mixed = jnp.concatenate([mixed, back], 1)
    keep, back = rows_send(mixed, 0, 1, data_index)
    before, after = lax.ppermute(tokens[HALF:], "mp", forth), lax.ppermute(tokens[:HALF], "mp", back_to)
    back, small, lengths, before, after = tie(back, small, lengths, before, after)
    small = chain.send(small)
    steps -= 1
    mixed = lanes_join(keep, back, 1, data_index)
    for level in range(2, data_bits):
        mixed = lanes_join(mixed, swap(mixed, (1 << level, 0)), level, data_index)
    mixed = mixed.reshape(-1, width)
    third = width // 3
    mixed = tuple(mixed[:, k * third : (k + 1) * third] for k in range(3))
    feed = lanes_join(feed_keep, feed_back, 1, data_index)
    for level in range(2, data_bits):
        feed = lanes_join(feed, swap(feed, (1 << level, 0)), level, data_index)
    up, down = feed[0], feed[1]
    for bits in early[:-1]:
        up, down = early_join(up, bits), early_join(down, bits)
    up_back = swap(up, early[-1])
    backs, small, up_back, down = tie(stage_swap(mixed, THIRDS, 0), small, up_back, down)
    for _ in range(steps - 1):
        small = chain.send(small)
    mixed = grow(mixed, backs)

    starts = jnp.cumsum(lengths) - lengths
    half_rows = (model_index * 2 + jnp.arange(-1, 3, dtype=jnp.int32)) * HALF
    inside = (half_rows[:, None] >= starts[None]) & (half_rows[:, None] < (starts + lengths)[None])
    seated = jnp.any(inside, axis=1)
    is_first = jnp.any(inside & (half_rows[:, None] == starts[None]), axis=1)
    paired = jnp.any(inside & (lengths[None] == 2 * HALF), axis=1)
    own_index = jnp.arange(4, dtype=jnp.int32)
    partner = jnp.where(is_first, own_index + 1, own_index - 1)
    facts = jnp.stack([partner, paired.astype(jnp.int32), seated.astype(jnp.int32)], 1)[1:3]
    facts = facts.reshape(6).astype(jnp.int32)
    table = inside.astype(f32)
    number = jnp.sum(jnp.where(inside, jnp.arange(images, dtype=jnp.int32)[None], 0), axis=1)
    number = jnp.where(seated, number, -1)

    backs, table, facts, number, small, up, down = tie(
        stage_swap(mixed, THIRDS, 1), table, facts, number, small, up, down
    )
    mixed, mixed_both = grow_both(mixed, backs, 1)
    backs = stage_swap(mixed, THIRDS, 2)
    cond_act, buf = chain.send(small)

    shifts = jnp.array(join_masks(model_bits), jnp.int32) ^ model_index
    flip = (shifts[None] == jnp.arange(model_ways, dtype=jnp.int32)[:, None]).astype(f32)
    (vectors,) = call(
        lambda *refs: vectors_kernel(head_cols, *refs),
        [like(24, width, f32)],
        (number, shifts, buf),
        "modulation_vectors",
        scratch=[pltpu.VMEM((24, width), f32)],
        smem=2,
    )
    bias_rel = buf[:, -1, : 6 * head_cols]
    bias_q, bias_v = (bias_rel[:, k * head_cols : (k + 1) * head_cols].reshape(1, -1) for k in range(2))
    step, places = feed_places(feed_count, model_bits)
    place = jnp.where((data_index & 1) == 0, places[0], places[1])
    granules = all_hidden // step
    source = (place[:, 0] * 4 + (place[:, 1] ^ (data_index & 3))) * (feed_count // step) + place[:, 2]
    source = one_hot_rows(source, granules)
    bias_up = jnp.dot(source, bias_rel[:, 2 * head_cols :].reshape(granules, step), precision=highest)
    bias_up = bias_up.reshape(1, all_hidden)
    (grad_mlp,) = call(gate_kernel, [like(local_rows, width)], (cotangent, vectors), "grad_mlp")
    (span_input,) = call(
        span_kernel, [like(2 * local_rows, width)], (before, tokens, after, vectors), "attention_input"
    )
    b_out, b_down = b_out.astype(f32).reshape(1, width), b_down.astype(f32).reshape(1, width)
    own = slice(HALF, HALF + local_rows)
    near = swap(mixed_both, CORE)
    backs, near, span_input, bias_up, bias_q, bias_v, grad_mlp, b_out, b_down, vectors, source = tie(
        backs, near, span_input, bias_up, bias_q, bias_v, grad_mlp, b_out, b_down, vectors, source
    )
    cut = up.shape[0] * 4 // 3
    outs = [like(cut, width), like(cut // 2, width)]
    up = call(join_kernel, outs, (up, up_back), "join")
    up_backs = stage_swap(up, FEED, 0)
    far = core_swap(backs)
    up_backs, far, down = tie(up_backs, far, down)
    attn_input = span_input[own]

    up = grow(up, up_backs)
    up_backs = stage_swap(up, FEED, 1)
    down_back = swap(down, early[-1])
    wq, wk, wv, wo = assemble(spot, (mixed_both, *backs, near, *far), width)
    query, key, value = call(
        qkv_kernel,
        [like(2 * local_rows, width)] * 3,
        (span_input, wq, wk, wv, bias_q, bias_v),
        "query_key_value",
    )
    up_backs, down_back, query, key, value = tie(up_backs, down_back, query, key, value)
    up, up_both = grow_both(up, up_backs, 0)
    up_backs = stage_swap(up, FEED, 2)
    down = call(join_kernel, outs, (down, down_back), "join")
    down_backs = stage_swap(down, FEED, 0)
    up_near = swap(up_both, CORE)
    attended, branch, residual, mlp_input = call(
        attend_forward,
        [like(local_rows, width), like(local_rows, width, f32), like(local_rows, width, f32), like(local_rows, width)],
        (facts, query, key, value, wo, b_out, tokens, vectors),
        "attention_forward",
        scratch=[pltpu.VMEM((2 * HALF, width), bf16)] * 2,
        smem=1,
    )

    up_backs, up_near, down_backs, mlp_input = tie(up_backs, up_near, down_backs, mlp_input)
    up_far = core_swap(up_backs)
    down = grow(down, down_backs)
    down_backs = stage_swap(down, FEED, 1)
    up_far, down_backs, mlp_input = tie(up_far, down_backs, mlp_input)
    ups = up_both, *up_backs, up_near, *up_far
    act, slope = call(up_kernel, [like(local_rows, all_hidden)] * 2, (mlp_input, bias_up, *ups), "up")
    down, down_both = grow_both(down, down_backs, 0)
    down_backs = stage_swap(down, FEED, 2)
    down_near = swap(down_both, CORE)
    other = all_hidden // 2
    sizes = (up[0].shape[0], up[1].shape[0]) * 2
    sum_down = core_swap(products(act, grad_mlp, other, (other // 2,) * 2))
    down_backs, down_near, act = tie(down_backs, down_near, act)
    down_far = core_swap(down_backs)
    down_far, sum_down = tie(down_far, sum_down)
    downs = down_both, *down_backs, down_near, *down_far
    sum_down = products(act, grad_mlp, 0, sizes, sum_down)
    down_keeps, down_sends = sum_down[:2], sum_down[2:]
    sums_backs = stage_swap(down_sends, FEED, 2)
    grad_pre, grad_bias, output, output_sums = call(
        down_kernel,
        [like(local_rows, all_hidden), like(1, all_hidden, f32), like(local_rows, width), like(8, width, f32)],
        (grad_mlp, slope, act, residual, cotangent, vectors, b_down, *downs),
        "down",
        scratch=[pltpu.VMEM((local_rows, width), f32)],
    )
    (grad_mlp_input,) = call(back_kernel, [like(local_rows, width, f32)], (grad_pre, *ups), "grad_mlp_input")
    grad_residual, grad_branch, grad_attended, middle_sums = call(
        middle_kernel,
        [like(local_rows, width, f32), like(local_rows, width), like(local_rows, width), like(8, width, f32)],
        (grad_mlp_input, residual, branch, cotangent, vectors, wo),
        "grad_attended",
    )
    sum_up = products(grad_pre, mlp_input, other, (other,))
    down_backs, sum_up, grad_attended, grad_branch, grad_pre = tie(
        sums_backs, sum_up, grad_attended, grad_branch, grad_pre
    )
    sum_up = core_swap(sum_up)
    from_after = lax.ppermute(grad_branch[:HALF], "mp", back_to)
    from_before = lax.ppermute(grad_branch[HALF:], "mp", forth)

    full, half_full = pltpu.VMEM((2 * HALF, width), f32), pltpu.VMEM((2 * HALF, width), bf16)

    def attention_back(half, *operands):
        return call(
            lambda *refs: attend_backward(half, *refs),
            [like(local_rows, width), like(local_rows, width, f32), like(local_rows, width, f32)],
            (facts, query, key, value, grad_attended, *operands),
            "attention_backward",
            scratch=[half_full, half_full, full, full],
            smem=1,
        )

    first_half = attention_back(0)
    grad_query, own_key, own_value = attention_back(1, *first_half)
    sum_up, from_after, from_before, grad_query = tie(sum_up, from_after, from_before, grad_query)
    sum_up = products(grad_pre, mlp_input, 0, sizes, sum_up)
    up_keeps, up_sends = sum_up[:2], sum_up[2:]
    up_backs = stage_swap(up_sends, FEED, 2)
    from_after, from_before = lax.optimization_barrier(((from_after, from_before), up_sends))[0]
    grad_key, grad_value = call(
        attend_outside,
        [like(local_rows, width)] * 2,
        (facts, query, key, value, from_before, from_after, wo, own_key, own_value),
        "attention_outside",
        scratch=[half_full, half_full, pltpu.VMEM((HALF, width), bf16), full, full],
        smem=1,
    )
    lefts, rights = (grad_query, grad_key, grad_value, attended), (attn_input, grad_branch)
    sum_mixed = kind_products(1, spot, lefts, rights)
    up_backs, sum_mixed = tie(up_backs, sum_mixed)
    sum_mixed = core_swap(sum_mixed)
    feed_keeps, feed_sends = halve_join((*up_keeps, *down_keeps), (*up_backs, *down_backs))
    feed_backs = stage_swap(feed_sends, FEED, 1)
    grad_tokens, last_sums = call(
        last_kernel,
        [like(local_rows, width, f32), like(8, width, f32)],
        (grad_query, grad_key, grad_value, wq, wk, wv, tokens, vectors, grad_residual),
        "grad_tokens",
    )
    sum_mixed = kind_products(0, spot, lefts, rights, sum_mixed)
    mixed_keeps, mixed_sends = sum_mixed[0::2], sum_mixed[1::2]
    mixed_sends, last_sums = tie(mixed_sends, last_sums)
    feed_backs = lax.optimization_barrier((feed_backs, mixed_sends))[0]
    mixed_backs = stage_swap(mixed_sends, THIRDS, 2)
    feed_keeps, feed_sends = halve(feed_keeps, feed_backs, 2)
    feed_backs = stage_swap(feed_sends, FEED, 0)

    grad_bias = lax.optimization_barrier((grad_bias, feed_sends))[0]
    flat_up = lax.dot_general(
        source, grad_bias.reshape(granules, step), (((0,), (0,)), ((), ())), precision=highest
    ).reshape(model_ways, hidden)

    packed, plain = call(
        lambda *refs: pack_kernel(head_cols, *refs),
        [jax.ShapeDtypeStruct((model_ways, small_rows, small_lanes), f32), jax.ShapeDtypeStruct((1, 8, small_lanes), f32)],
        (number, shifts, last_sums, middle_sums, output_sums, flat_up),
        "pack_sums",
        scratch=[pltpu.VMEM((16, width), f32)],
        smem=2,
    )
    plain = jnp.pad(plain, ((0, 0), (0, small_rows - 8), (0, 0)))

    def gather_sums():
        buf, rest = packed.reshape((2,) * model_bits + (small_rows, small_lanes)), plain
        for bit in (0, 1, *range(2, model_bits)):
            axis = model_bits - 1 - joins.index(bit)
            keep, send = (lax.slice_in_dim(buf, k, k + 1, axis=axis) for k in (0, 1))
            send = jnp.concatenate([send.reshape(-1, small_rows, small_lanes), rest], 0).astype(bf16)
            back = yield swap(send, (0, 1 << bit))
            back = back.astype(f32)
            buf = keep + back[:-1].reshape(keep.shape)
            rest = send[-1:].astype(f32) + back[-1:]
        own = jnp.concatenate([buf.reshape(small_rows, small_lanes), rest[0, :8]], 0).astype(bf16)
        others = yield [swap(own, (d, 0)) for d in range(1, data_ways)]
        yield jnp.stack([own, *others], 0)

    mixed_backs, packed, plain = tie(mixed_backs, packed, plain)
    chain = gather_sums()
    steps = model_bits + 1
    small = next(chain)
    mixed_keeps, mixed_sends = halve(mixed_keeps, mixed_backs)
    mixed_backs = stage_swap(mixed_sends, THIRDS, 1)
    merged_rows = feed_count << len(early) - 1
    feed_keep, feed_send = merge(merge_rows_kernel, feed_keeps, feed_backs, merged_rows, 2 * width)
    feed_back = swap(feed_send, early[-1])
    mixed_backs, small = tie(mixed_backs, small)
    small = chain.send(small)
    steps -= 1
    mixed_keeps, mixed_sends = halve(mixed_keeps, mixed_backs)
    mixed_backs = stage_swap(mixed_sends, THIRDS, 0)
    feed_done = added(feed_keep, feed_back)
    for bits in reversed(early[:-1]):
        keep, send = halves(feed_done)
        feed_done = added(keep, swap(send, bits))
    feed_done = jnp.stack([feed_done[:, :width], feed_done[:, width:]], 0)
    for level in reversed(range(2, data_bits)):
        feed_done = lanes_sum(feed_done, level, data_index)
    mixed_backs, feed_done, small = tie(mixed_backs, feed_done, small)
    small = chain.send(small)
    steps -= 1
    merged_rows = head_cols << len(early) - 1
    mixed_keep, mixed_send = merge(merge_lanes_kernel, mixed_keeps, mixed_backs, merged_rows, width)
    mixed_back = swap(mixed_send, early[-1])
    feed_keep, feed_back = lanes_send(feed_done, 1, data_index)
    mixed_back, feed_back, small = tie(mixed_back, feed_back, small)
    small = chain.send(small)
    steps -= 1
    mixed_done = added(mixed_keep, mixed_back)
    for bits in reversed(early[:-1]):
        keep, send = halves(mixed_done)
        mixed_done = added(keep, swap(send, bits))
    for level in reversed(range(2, data_bits)):
        mixed_done = lanes_sum(mixed_done, level, data_index)
    keep, back = lanes_send(mixed_done, 1, data_index)
    feed_done = rows_join(feed_keep, feed_back, 1, data_index, 0)
    feed_keep, feed_back = lanes_send(feed_done, 0, data_index)
    back, feed_back, small = tie(back, feed_back, small)
    small = chain.send(small)
    steps -= 1
    mixed_done = rows_join(keep, back, 1, data_index, 0)
    keep, back = lanes_send(mixed_done, 0, data_index)
    feed_done = rows_join(feed_keep, feed_back, 0, data_index, 1).reshape(4, 2, feed_count, lanes)
    for _ in range(steps):
        small = chain.send(small)
    mixed_done = rows_join(keep, back, 0, data_index, 1).reshape(4, head_cols, lanes)
    grad_modulation = small[:, :images, : 6 * head_cols]
    rest = tree_sum(small[:, small_rows - 1 :].astype(f32))
    grad_w_ada = tn(
        cond_act.reshape(data_ways * images, lanes),
        grad_modulation.reshape(data_ways * images, 6 * head_cols),
    )
    grad_w_ada = grad_w_ada.reshape(lanes, 6, head_cols)
    grad_b_ada = tree_sum(jnp.sum(grad_modulation, axis=1, dtype=f32)).reshape(6, head_cols)
    per = -(-width // small_lanes)
    grad_b_out, grad_b_down = (rest[1 + k * per : 1 + (k + 1) * per].reshape(-1)[:width] for k in range(2))
    own_bias = rest[0, : 6 * head_cols]
    grad_b_qv, grad_b_up = own_bias[: 2 * head_cols].reshape(2, head_cols), own_bias[2 * head_cols :]

    grad_w_up, grad_w_down = call(
        place_feed_kernel, [like(lanes, hidden, f32)] * 2, (feed_done,), "place_feed_forward"
    )
    grad_w_down = jnp.swapaxes(grad_w_down, 0, 1)
    mixed_done = mixed_done.astype(f32)
    grad_w_qkv, grad_w_out = jnp.swapaxes(mixed_done[:3], 1, 2), mixed_done[3]
    return (
        output,
        grad_tokens,
        grad_w_ada,
        grad_b_ada,
        grad_w_qkv,
        grad_b_qv,
        grad_w_out,
        grad_b_out,
        grad_w_up,
        grad_b_up,
        grad_w_down,
        grad_b_down,
    )


def solution(mesh):
    in_specs = (
        P(("dp", "mp"), None),
        P("dp", None),
        P("dp"),
        P("dp", None, "mp"),
        P(None, "mp"),
        P(None, "dp", "mp"),
        P(None, "mp"),
        P("mp", "dp"),
        P(),
        P("dp", "mp"),
        P("mp"),
        P("mp", "dp"),
        P(),
        P(("dp", "mp"), None),
    )
    out_specs = (
        P(("dp", "mp"), None),
        P(("dp", "mp"), None),
        P("dp", None, "mp"),
        P(None, "mp"),
        P(None, "dp", "mp"),
        P(None, "mp"),
        P("mp", "dp"),
        P(),
        P("dp", "mp"),
        P("mp"),
        P("mp", "dp"),
        P(),
    )
    return jax.shard_map(
        on_device, mesh=mesh, in_specs=in_specs, out_specs=out_specs, check_vma=False
    )
```
